128 devices in a mesh: rep: 32 (over x, z_hi, y), shard: 4 (over z_lo, core).
Axes of the slice: x: 4, y: 4, z: 4 (z_hi: 2, z_lo: 2; z = z_hi * 2 + z_lo), core: 2. Of those that a mesh axis runs over, the one named last changes fastest.
Arguments:
- inputs: bfloat16 [16384, 1024], P(('rep', 'shard')), may hold values from -10 to 10
- lengths: int32 [32], P('rep'), may hold values from 385 to 512, as said below
- gains: bfloat16 [2, 1024], P(None, 'shard'), may hold values from 0.5 to 1.5
- shifts: bfloat16 [2, 1024], P(None, 'shard'), may hold values from -4 to 4
- triple: bfloat16 [2, 1024, 3072], P(None, 'shard'), may hold values from -0.1875 to 0.1875
- triple_bias: bfloat16 [2, 3072], P(None, 'shard'), may hold values from -4 to 4
- merger: bfloat16 [2, 1024, 1024], P(None, 'shard'), may hold values from -1.5 to 1.5
- merger_bias: bfloat16 [2, 1024], P(None, 'shard'), may hold values from -4 to 4
- expander: bfloat16 [2, 1024, 4096], P(None, 'shard'), may hold values from -0.1875 to 0.1875
- expander_bias: bfloat16 [2, 4096], P(None, 'shard'), may hold values from -4 to 4
- shrinker: bfloat16 [2, 4096, 1024], P(None, 'shard'), may hold values from -0.09375 to 0.09375
- shrinker_bias: bfloat16 [2, 1024], P(None, 'shard'), may hold values from -4 to 4
- cotangent: bfloat16 [16384, 1024], P(('rep', 'shard')), may hold values from -6 to 6
Outputs:
- hidden_out: bfloat16 [16384, 1024], P(('rep', 'shard'))
- input_grad: float32 [16384, 1024], P(('rep', 'shard'))
- gains_gradient: float32 [2, 1024], P(None, 'shard')
- shifts_gradient: float32 [2, 1024], P(None, 'shard')
- triple_gradient: float32 [2, 1024, 3072], P(None, 'shard')
- triple_bias_gradient: float32 [2, 3072], P(None, 'shard')
- merger_gradient: float32 [2, 1024, 1024], P(None, 'shard')
- merger_bias_gradient: float32 [2, 1024], P(None, 'shard')
- expander_gradient: float32 [2, 1024, 4096], P(None, 'shard')
- expander_bias_gradient: float32 [2, 4096], P(None, 'shard')
- shrinker_gradient: float32 [2, 4096, 1024], P(None, 'shard')
- shrinker_bias_gradient: float32 [2, 1024], P(None, 'shard')
- rms_stats: float32 [32, 6], P('rep')
The draws below stay inside these ranges and needn't reach their ends.
Inputs may be any that keep to these rules, and one draw needn't show every extreme that they name: `lengths`: one sequence of every draw has all 512 slots valid.
All inputs are finite; a program needn't handle non-finite values.
Results may differ from the reference program's by a relative error of at most 0.025.
Values may be sent and summed in bfloat16 or wider, within the bound.
No kernel may reach another device: no remote copies, remote signals or barrier semaphores. Data moves between devices by JAX's collectives and lax.ppermute only.
A program may use at most 256 MiB of HBM per device.

```python
import math
import jax
import jax.numpy as jnp
from jax import lax

D = 1024
H = 16
HD = 64
ROT = 32
FF = 4096
LAYERS = 2
TOK_DEV = 128
SEQ = 512
TOKENS = 16384
N_REP = 32


def draw_lengths(key, part):
    key = jax.random.fold_in(key, 11)
    first, second = jax.random.split(key)
    drawn = jax.random.randint(first, (N_REP,), SEQ - TOK_DEV + 1, SEQ + 1)
    chosen = jax.random.randint(second, (), 0, N_REP)
    return jnp.where(jnp.arange(N_REP) == chosen, SEQ, drawn).astype(jnp.int32)


def draw_inputs(key, part):
    key = jax.random.fold_in(key, 23)
    first = jax.random.fold_in(key, 0)
    place = (jnp.arange(TOKENS) % SEQ).astype(jnp.float32) / SEQ
    ramp = 0.5 + 1.5 * place
    base = jnp.clip(jax.random.normal(first, (TOKENS, D), jnp.float32), -5.0, 5.0)
    return (base * ramp[:, None]).astype(jnp.bfloat16)


def block_levels(rng, shape, cuts, smallest, largest):
    factor_of, own = 1.0, jax.random.fold_in(rng, 6)
    for axis_at, parts in cuts:
        heights = jnp.exp(jax.random.uniform(jax.random.fold_in(own, axis_at), (parts,), jnp.float32, smallest / len(cuts), largest / len(cuts)))
        factor_of = factor_of * jnp.repeat(heights, shape[axis_at] // parts).reshape([-1 if axis == axis_at else 1 for axis in range(len(shape))])
    return factor_of


def bell_draw(key, shape, scale, most, cuts=(), kind=jnp.bfloat16):
    entries = jax.random.normal(key, shape, jnp.float32) * scale
    if len(cuts) > 0:
        entries = block_levels(key, shape, cuts, -0.22, 0.18) * entries
    return jnp.clip(entries, min=-most, max=most).astype(kind)


def setup_inputs(seed: int = 0) -> dict:
    streams_of = jax.random.split(jax.random.key(seed), 14)
    return {
        "inputs": draw_inputs(jax.random.fold_in(streams_of[13], 71), 0),
        "lengths": draw_lengths(jax.random.fold_in(streams_of[13], 71), 0),
        "gains": jnp.clip(1.0 + 0.1 * jax.random.normal(streams_of[2], (LAYERS, D), jnp.float32), 0.5, 1.5).astype(jnp.bfloat16),
        "shifts": bell_draw(streams_of[3], (LAYERS, D), 0.3, 4.0, ((1, 4),)),
        "triple": bell_draw(streams_of[4], (LAYERS, D, 3 * D), D ** -0.5, 0.1875, ((1, 4),)),
        "triple_bias": bell_draw(streams_of[5], (LAYERS, 3 * D), 0.5, 4.0, ((1, 4),)),
        "merger": bell_draw(streams_of[6], (LAYERS, D, D), (D // 64) ** -0.5, 1.5, ((1, 4),)),
        "merger_bias": bell_draw(streams_of[7], (LAYERS, D), 0.3, 4.0, ((1, 4),)),
        "expander": bell_draw(streams_of[8], (LAYERS, D, FF), D ** -0.5, 0.1875, ((1, 4),)),
        "expander_bias": bell_draw(streams_of[9], (LAYERS, FF), 0.5, 4.0, ((1, 4),)),
        "shrinker": bell_draw(streams_of[10], (LAYERS, FF, D), FF ** -0.5, 0.09375, ((1, 4),)),
        "shrinker_bias": bell_draw(streams_of[11], (LAYERS, D), 0.3, 4.0, ((1, 4),)),
        "cotangent": bell_draw(streams_of[12], (TOKENS, D), 1.0, 6.0, ((0, 128),)),
    }


@jax.custom_vjp
def low(v):
    return lax.optimization_barrier(v.astype(jnp.bfloat16)).astype(jnp.float32)

@jax.custom_vjp
def low_back(v):
    return v

def low_keep(v):
    return (low(v), None)

def low_pass(kept, grad):
    return (grad,)

def back_keep(v):
    return (v, None)

def back_low(kept, grad):
    return (low(grad),)
low.defvjp(low_keep, low_pass)
low_back.defvjp(back_keep, back_low)
EPS_NORM = 1e-05

def matmul(left, right):
    return jnp.dot(left, right, precision=lax.Precision.HIGHEST, preferred_element_type=jnp.float32)

def layer_norm(state, gain, shift):
    mean = lax.optimization_barrier(jnp.mean(state, axis=-1, keepdims=True))
    centred = state - mean
    spread = lax.optimization_barrier(jnp.mean(centred * centred, axis=-1, keepdims=True))
    return centred * lax.rsqrt(spread + EPS_NORM) * gain + shift

def angles(positions):
    index = jnp.arange(ROT // 2, dtype=jnp.float32)
    freq = jnp.exp(index * (-2.0 * math.log(10000.0) / ROT))
    phase = positions[:, None] * freq[None, :]
    return (jnp.cos(phase)[:, None, :], jnp.sin(phase)[:, None, :])

def rotate(values, cosine, sine):
    half = ROT // 2
    first = values[..., :half]
    second = values[..., half:ROT]
    return jnp.concatenate([first * cosine - second * sine, second * cosine + first * sine, values[..., ROT:]], axis=-1)

def one_layer(state, weights, allowed, cosine, sine):
    gain, shift, triple, triple_bias, merger, merger_bias, expander, expander_bias, shrinker, shrinker_bias = weights
    count = state.shape[0]
    normed = low(layer_norm(state, gain, shift))
    triple_out = low_back(matmul(normed, triple) + triple_bias)
    query = triple_out[:, :D].reshape(count, H, HD)
    keys = triple_out[:, D:2 * D].reshape(count, H, HD)
    values = low(triple_out[:, 2 * D:]).reshape(count, H, HD)
    query = low(rotate(query, cosine, sine) * HD ** (-0.5))
    keys = low(rotate(keys, cosine, sine))
    scores = low_back(jnp.einsum('qhd,khd->hqk', query, keys, precision=lax.Precision.HIGHEST))
    scores = jnp.where(allowed[None], scores, -1000000000.0)
    probs = low(jax.nn.softmax(scores, axis=-1))
    mixed = jnp.einsum('hqk,khd->qhd', probs, values, precision=lax.Precision.HIGHEST)
    mixed = low(low_back(mixed)).reshape(count, D)
    attended = low_back(matmul(mixed, merger) + merger_bias)
    before = low_back(matmul(normed, expander) + expander_bias)
    activated = low(jax.nn.gelu(before, approximate=True))
    branch = low_back(matmul(activated, shrinker) + shrinker_bias)
    return (state + attended + branch, attended, branch)

def forward(first_state, params, valid, allowed, cosine, sine):
    state = first_state
    squares = []
    for layer in range(LAYERS):
        weights = tuple((p[layer] for p in params))
        following, attended, branch = one_layer(state, weights, allowed, cosine, sine)
        for item in (state, attended, branch):
            squares.append(jnp.sum(lax.optimization_barrier(jnp.sum(item * item, axis=1)) * valid))
        state = following
    return (state * valid[:, None], jnp.stack(squares))

def reference(inputs, lengths, gains, shifts, triple, triple_bias, merger, merger_bias, expander, expander_bias, shrinker, shrinker_bias, cotangent):
    params = tuple((p.astype(jnp.float32) for p in (gains, shifts, triple, triple_bias, merger, merger_bias, expander, expander_bias, shrinker, shrinker_bias)))
    rows = inputs.astype(jnp.float32).reshape(N_REP, SEQ, D)
    slopes = cotangent.astype(jnp.float32).reshape(N_REP, SEQ, D)
    positions = jnp.arange(SEQ, dtype=jnp.int32)
    cosine, sine = angles(positions.astype(jnp.float32))

    def step(total, item):
        seq_rows, seq_slope, length = item
        valid = (positions < length).astype(jnp.float32)
        allowed = (positions[None, :] <= positions[:, None]) & (positions[None, :] < length)

        def local_forward(first_state, weights):
            return forward(first_state, weights, valid, allowed, cosine, sine)
        result, pull, squares = jax.vjp(local_forward, rows_dummy_fix(seq_rows), params, has_aux=True)
        input_slope, param_slopes = pull(seq_slope)
        total = jax.tree.map(lambda a, b: a + b, total, param_slopes)
        stats = jnp.sqrt(squares / (length.astype(jnp.float32) * D) + 1e-06)
        return (total, (result, input_slope, stats))
    zeros = tuple((jnp.zeros_like(p) for p in params))
    total, (results, input_slopes, stats) = lax.scan(step, zeros, (rows, slopes, lengths))
    hidden_out = results.reshape(TOKENS, D).astype(jnp.bfloat16)
    input_grad = input_slopes.reshape(TOKENS, D)
    return (hidden_out, input_grad, total[0], total[1], total[2], total[3], total[4], total[5], total[6], total[7], total[8], total[9], stats)

def rows_dummy_fix(values):
    return values
```

```python
import functools
import math

import jax
import jax.numpy as jnp
from jax import lax
from jax.experimental import pallas as pl
from jax.experimental.pallas import tpu as pltpu
from jax.sharding import PartitionSpec as P

HD = 64
ROT = 32
LAYERS = 2
EPS_NORM = 1e-05
AXES = ("rep", "shard")
BF = jnp.bfloat16
F32 = jnp.float32
MINE = 4
W = 1024
WIDE = 1792
CHUNK = 1536

VM = pl.BlockSpec(memory_space=pltpu.VMEM)
ANY = pl.BlockSpec(memory_space=pl.ANY)
SM = pl.BlockSpec(memory_space=pltpu.SMEM)


def place_of(index):
    rep, shard = divmod(index, 4)
    x, rest = divmod(rep, 8)
    z_hi, y = divmod(rest, 4)
    z_lo, core = divmod(shard, 2)
    return x, y, z_hi * 2 + z_lo, core


def index_of(x, y, z, core):
    return ((x * 2 + z // 2) * 4 + y) * 4 + (z % 2) * 2 + core


def move(value, dx=0, dy=0, flip_z=0, flip_core=0):
    pairs = []
    for index in range(128):
        x, y, z, core = place_of(index)
        target = index_of((x + dx) % 4, (y + dy) % 4, z ^ flip_z, core ^ flip_core)
        pairs.append((index, target))
    return lax.ppermute(value, AXES, pairs)


def step(value, axis, by):
    return move(value, dx=by) if axis == 0 else move(value, dy=by)


def after(value, *others):
    return lax.optimization_barrier((value,) + others)[0]


def pick(value, index, axis=0):
    return lax.dynamic_index_in_dim(value, index, axis, keepdims=False)


def shape(*dims, dtype=BF):
    return jax.ShapeDtypeStruct(dims, dtype)


def call(body, args, specs, outs, out_specs=None, scratch=(), flops=0, aliases=None):
    moved = sum(math.prod(o.shape) * o.dtype.itemsize for o in outs)
    moved += sum(math.prod(a.shape) * a.dtype.itemsize for a, s in zip(args, specs) if s is VM)
    return pl.pallas_call(
        body,
        out_shape=outs,
        in_specs=specs,
        out_specs=out_specs or [VM] * len(outs),
        scratch_shapes=scratch,
        input_output_aliases=aliases or {},
        compiler_params=pltpu.CompilerParams(vmem_limit_bytes=56 * 2**20),
        cost_estimate=pl.CostEstimate(flops=flops, bytes_accessed=moved, transcendentals=0),
    )(*args)


def dot(left, right):
    return jnp.dot(left, right, preferred_element_type=F32)


def dot_t(left, right):
    return lax.dot_general(left, right, (((1,), (1,)), ((), ())), preferred_element_type=F32)


def t_dot(left, right):
    return lax.dot_general(left, right, (((0,), (0,)), ((), ())), preferred_element_type=F32)


def copies(pairs, sems):
    started = []
    for at, (source, target) in enumerate(pairs):
        copy = pltpu.make_async_copy(source, target, sems.at[at])
        copy.start()
        started.append(copy)
    return started


def finish(started):
    for copy in started:
        copy.wait()


def lanes(start, size):
    return pl.ds(pl.multiple_of(start, 128), size)


def rows_at(start, size):
    return pl.ds(pl.multiple_of(start, 16), size)


def cut_triple(place, triple, out1, out2a, out2b, out3a, out3b, slab, sems):
    shard = place[2]
    finish(copies([(triple.at[0], slab)], sems))
    for k, refs in ((2, (out2a, out2b)), (3, (out3a, out3b)), (1, (out1,))):
        block = shard ^ k
        size = 256 // len(refs)
        for at, ref in enumerate(refs):
            for p in range(3):
                ref[:, pl.ds(p * 256, 256)] = slab[
                    pl.ds(at * size, size), lanes(p * W + block * 256, 256)
                ]


def cut_rest(
    place, triple, expander, e1, e2a, e2b, e3a, e3b, w1, w2, w3, slab, first, second, sems
):
    shard = place[2]
    pairs = [(expander.at[0], first), (expander.at[1], second), (triple.at[1], slab)]
    started = copies(pairs, sems)
    started[0].wait()
    for k, refs in ((2, (e2a, e2b)), (3, (e3a, e3b)), (1, (e1,))):
        size = 256 // len(refs)
        for at, ref in enumerate(refs):
            ref[...] = first[pl.ds(at * size, size), lanes((shard ^ k) * W, W)]
    finish(started[1:])
    for k, ref in ((2, w2), (3, w3), (1, w1)):
        block = shard ^ k
        ref[:, pl.ds(0, W)] = second[:, lanes(block * W, W)]
        for p in range(3):
            ref[:, pl.ds(W + p * 256, 256)] = slab[:, lanes(p * W + block * 256, 256)]


def own_triple(shard, layer, triple, wide):
    return [
        (
            triple.at[layer, :, lanes(p * W + shard * 256, 256)],
            wide.at[rows_at(shard * 256, 256), pl.ds(W + p * 256, 256)],
        )
        for p in range(3)
    ]


def own_expander(shard, layer, expander, wide):
    return [
        (expander.at[layer, :, lanes(shard * W, W)], wide.at[rows_at(shard * 256, 256), pl.ds(0, W)])
    ]


def first_triple(shard, pieces, wide):
    pairs = []
    one, two_a, two_b, three_a, three_b = pieces
    for k, refs in ((1, (one,)), (2, (two_a, two_b)), (3, (three_a, three_b))):
        size = 256 // len(refs)
        for at, ref in enumerate(refs):
            target = wide.at[rows_at((shard ^ k) * 256 + at * size, size), pl.ds(W, 768)]
            pairs.append((ref, target))
    return pairs


def first_expander(shard, pieces, wide):
    pairs = []
    one, two_a, two_b, three_a, three_b = pieces
    for k, refs in ((1, (one,)), (2, (two_a, two_b)), (3, (three_a, three_b))):
        size = 256 // len(refs)
        for at, ref in enumerate(refs):
            pairs.append((ref, wide.at[rows_at((shard ^ k) * 256 + at * size, size), pl.ds(0, W)]))
    return pairs


def second_wide(shard, pieces, wide):
    return [
        (ref, wide.at[rows_at((shard ^ k) * 256, 256), :]) for k, ref in zip((1, 2, 3), pieces)
    ]


def spots(shard):
    row = lax.broadcasted_iota(jnp.int32, (512, 1), 0)
    col = lax.broadcasted_iota(jnp.int32, (1, 512), 1)

    def at(i):
        return (((i >> 7) ^ shard) << 7) | (i & 127)

    return at(row), at(col)


def rotate(values, turn, back=False):
    ahead = pltpu.roll(values, 256 - 16, 1) * turn[1]
    behind = pltpu.roll(values, 16, 1) * turn[2]
    if back:
        return values * turn[0] - ahead - behind
    return values * turn[0] + ahead + behind


def normalize(state):
    mean = jnp.mean(state, axis=-1, keepdims=True)
    centred = state - mean
    spread = jnp.mean(centred * centred, axis=-1, keepdims=True)
    factor = lax.rsqrt(spread + EPS_NORM)
    return centred * factor, factor


ROOT = math.sqrt(2.0 / math.pi)


def gelu_both(v):
    square = v * v
    t = jnp.tanh(ROOT * v * (1.0 + 0.044715 * square))
    half = 0.5 * (1.0 + t)
    slope = half + 0.5 * v * (1.0 - t * t) * (ROOT + (3.0 * 0.044715 * ROOT) * square)
    return v * half, slope


def heads_out(normed, wide, bias, turn, qkv):
    scale = HD ** (-0.5)
    for p in range(3):
        part = dot(normed[...], wide[:, pl.ds(W + p * 256, 256)]) + bias[:, pl.ds(p * 256, 256)]
        if p < 2:
            part = rotate(part, turn)
        if p == 0:
            part = part * scale
        qkv[:, pl.ds(p * 256, 256)] = part.astype(BF)


def probabilities(qkv, h, allowed):
    q = qkv[:, pl.ds(h * HD, HD)]
    k = qkv[:, pl.ds(256 + h * HD, HD)]
    scores = jnp.where(allowed, dot_t(q, k), -1000000000.0)
    powered = jnp.exp(scores - jnp.max(scores, axis=-1, keepdims=True))
    return powered * (1.0 / jnp.sum(powered, axis=-1, keepdims=True))


def attend(qkv, allowed, mixed):
    for h in range(MINE):
        low = probabilities(qkv, h, allowed).astype(BF)
        mixed[:, pl.ds(h * HD, HD)] = dot(low, qkv[:, pl.ds(512 + h * HD, HD)]).astype(BF)


def attend_back(qkv, allowed, mixed, slope_mixed, slopes, forward):
    for h in range(MINE):
        probs = probabilities(qkv, h, allowed)
        low = probs.astype(BF)
        q = qkv[:, pl.ds(h * HD, HD)]
        k = qkv[:, pl.ds(256 + h * HD, HD)]
        v = qkv[:, pl.ds(512 + h * HD, HD)]
        if forward:
            mixed[:, pl.ds(h * HD, HD)] = dot(low, v).astype(BF)
        out = slope_mixed[:, pl.ds(h * HD, HD)]
        slope_probs = dot_t(out, v)
        centre = jnp.sum(probs * slope_probs, axis=-1, keepdims=True)
        slope_scores = (probs * (slope_probs - centre)).astype(BF)
        slopes[:, pl.ds(h * HD, HD)] = dot(slope_scores, k)
        slopes[:, pl.ds(256 + h * HD, HD)] = t_dot(slope_scores, q)
        slopes[:, pl.ds(512 + h * HD, HD)] = t_dot(low, out)


def hand_out(left, right, send, keep):
    for n in range(4):
        cols = pl.ds(n * 256, 256)
        part = dot(left[...], right[:, cols])
        spread_out(part, cols, send, keep)


def spread_out(part, cols, send, keep):
    keep[pl.ds(0, 128), cols] = part[0:128]
    send[pl.ds(0, 128), cols] = part[128:256].astype(BF)
    keep[pl.ds(128, 128), cols] = part[256:384]
    send[pl.ds(128, 128), cols] = part[384:512].astype(BF)


def first_attention(
    place, x0, x1, x2, x3, vec, turn, triple, merger, t1, t2a, t2b, t3a, t3b,
    normed, qkv, mixed, send, keep, wide, merge, sems,
):
    shard, length = place[2], place[3]
    pairs = own_triple(shard, 0, triple, wide) + [(merger.at[0], merge)]
    started = copies(pairs + first_triple(shard, (t1, t2a, t2b, t3a, t3b), wide), sems)
    gain, shift = vec[pl.ds(0, 1), :], vec[pl.ds(2, 1), :]
    for k, ref in enumerate((x0, x1, x2, x3)):
        hat, _ = normalize(ref[...].astype(F32))
        normed[pl.ds(k * 128, 128), :] = (hat * gain + shift).astype(BF)
    finish(started)
    row, col = spots(shard)
    allowed = (col <= row) & (col < length)
    heads_out(normed, wide, vec[pl.ds(8, 1), pl.ds(0, 768)], turn, qkv)
    attend(qkv, allowed, mixed)
    hand_out(mixed, merge, send, keep)


def first_forward(
    place, normed, vec, expander, shrinker, e1, e2a, e2b, e3a, e3b,
    before, send, keep, wide, shrink, act, sems,
):
    shard = place[2]
    pairs = own_expander(shard, 0, expander, wide) + first_expander(shard, (e1, e2a, e2b, e3a, e3b), wide)
    started = copies(pairs + [(shrinker.at[0], shrink)], sems)
    finish(started)
    for n in range(4):
        cols = pl.ds(n * 256, 256)
        part = dot(normed[...], wide[:, cols]) + vec[pl.ds(10, 1), cols]
        before[:, cols] = part
        act[:, cols] = gelu_both(part)[0].astype(BF)
    hand_out(act, shrink, send, keep)


def slopes_out(ss, bias, wide, send, keep):
    bias[...] = jnp.broadcast_to(jnp.sum(ss[...].astype(F32), axis=0, keepdims=True), bias.shape)
    for n in range(4):
        part = dot_t(ss[...], wide[pl.ds(n * 256, 256), :])
        spread_out(part, pl.ds(n * 256, 256), send, keep)


def triple_slopes(slopes, turn, ss):
    scale = HD ** (-0.5)
    ss[:, pl.ds(W, 256)] = (rotate(slopes[:, pl.ds(0, 256)], turn, True) * scale).astype(BF)
    ss[:, pl.ds(W + 256, 256)] = rotate(slopes[:, pl.ds(256, 256)], turn, True).astype(BF)
    ss[:, pl.ds(W + 512, 256)] = slopes[:, pl.ds(512, 256)].astype(BF)


def last_layer(
    place, n0, n1, n2, n3, u0, u1, u2, u3, vec, turn, triple, merger, expander, shrinker, w1, w2, w3,
    normed, up, act, ss, mixed, asend, akeep, fsend, fkeep, send, keep, bias,
    wide, merge, shrink, qkv, slopes, out, before, sems,
):
    shard, length = place[2], place[3]
    pairs = own_triple(shard, 1, triple, wide) + own_expander(shard, 1, expander, wide)
    pairs += second_wide(shard, (w1, w2, w3), wide) + [(merger.at[1], merge), (shrinker.at[1], shrink)]
    started = copies(pairs, sems)
    row, col = spots(shard)
    for k, (n, u) in enumerate(((n0, u0), (n1, u1), (n2, u2), (n3, u3))):
        rows = pl.ds(k * 128, 128)
        normed[rows, :] = n[...]
        up[rows, :] = jnp.where(row[k * 128 : k * 128 + 128] < length, u[...].astype(F32), 0.0).astype(BF)
    finish(started)
    for n in range(4):
        cols = pl.ds(n * 256, 256)
        part = dot(normed[...], wide[:, cols]) + vec[pl.ds(11, 1), cols]
        value, slope = gelu_both(part)
        act[:, cols] = value.astype(BF)
        ss[:, cols] = (dot_t(up[...], shrink[cols, :]) * slope).astype(BF)
    hand_out(act, shrink, fsend, fkeep)
    allowed = (col <= row) & (col < length)
    heads_out(normed, wide, vec[pl.ds(9, 1), pl.ds(0, 768)], turn, qkv)
    out[...] = dot_t(up[...], merge[...]).astype(BF)
    attend_back(qkv, allowed, mixed, out, slopes, True)
    hand_out(mixed, merge, asend, akeep)
    triple_slopes(slopes, turn, ss)
    slopes_out(ss, bias, wide, send, keep)


def first_back(
    place, u0, u1, u2, u3, before, qkv, turn, triple, merger, expander, shrinker,
    t1, t2a, t2b, t3a, t3b, e1, e2a, e2b, e3a, e3b,
    up, act, ss, send, keep, bias, wide, merge, shrink, slopes, out, sems,
):
    shard, length = place[2], place[3]
    pairs = own_triple(shard, 0, triple, wide) + own_expander(shard, 0, expander, wide)
    pairs += first_triple(shard, (t1, t2a, t2b, t3a, t3b), wide)
    pairs += first_expander(shard, (e1, e2a, e2b, e3a, e3b), wide)
    started = copies(pairs + [(merger.at[0], merge), (shrinker.at[0], shrink)], sems)
    for k, u in enumerate((u0, u1, u2, u3)):
        up[pl.ds(k * 128, 128), :] = u[...]
    finish(started)
    for n in range(4):
        cols = pl.ds(n * 256, 256)
        value, slope = gelu_both(before[:, cols])
        act[:, cols] = value.astype(BF)
        ss[:, cols] = (dot_t(up[...], shrink[cols, :]) * slope).astype(BF)
    row, col = spots(shard)
    allowed = (col <= row) & (col < length)
    out[...] = dot_t(up[...], merge[...]).astype(BF)
    attend_back(qkv, allowed, None, out, slopes, False)
    triple_slopes(slopes, turn, ss)
    slopes_out(ss, bias, wide, send, keep)


def cut(at, d):
    return pl.ds(pl.multiple_of(((at + d) & 3) * 64, 64), 64)


def terms_a(place, act, up, normed, ss, a0, a1, a2, a3, term):
    x = place[0]
    for o in range(4):
        cols = pl.ds(o * 256, 256)
        term[:, pl.ds(0, W)] = t_dot(act[:, cols], up[...])
        term[:, pl.ds(W, 512)] = t_dot(normed[:, cols], ss[:, pl.ds(W, 512)])
        for d, ref in enumerate((a0, a1, a2, a3)):
            ref[pl.ds(o * 64, 64), :] = term[cut(x, d), :].astype(BF)


def terms_b(place, normed, ss, mixed, up, b0, b1, b2, b3, term, last):
    y = place[1]
    last[...] = t_dot(mixed[...], up[...])
    for o in range(4):
        cols = pl.ds(o * 256, 256)
        term[:, pl.ds(0, W)] = t_dot(normed[:, cols], ss[:, pl.ds(0, W)])
        term[:, pl.ds(W, 256)] = t_dot(normed[:, cols], ss[:, pl.ds(1536, 256)])
        for d, ref in enumerate((b0, b1, b2, b3)):
            ref[pl.ds(o * 64, 64), pl.ds(0, 1280)] = term[cut(y, d), :].astype(BF)
            ref[pl.ds(o * 64, 64), pl.ds(1280, 256)] = last[cut(y, d), cols].astype(BF)


def weight_terms(place, act, normed, up, ss, mixed):
    a = call(
        terms_a, [place, act, up, normed, ss], [SM] + [VM] * 4, [shape(256, CHUNK)] * 4,
        scratch=[pltpu.VMEM((256, CHUNK), F32)], flops=2 * 10**9,
    )
    b = call(
        terms_b, [place, normed, ss, mixed, up], [SM] + [VM] * 4, [shape(256, CHUNK)] * 4,
        scratch=[pltpu.VMEM((256, 1280), F32), pltpu.VMEM((256, W), F32)], flops=2 * 10**9,
    )
    return list(a), list(b)


def join(place, state, ak, ag, az, fk, fg, fz, vec, new, out, squares, *, layer):
    shard, length = place[2], place[3]
    spot = shard * 128 + lax.broadcasted_iota(jnp.int32, (128, 1), 0)
    valid = (spot < length).astype(F32)
    attended = ak[pl.ds(0, 128), :] + ag[pl.ds(0, 128), :].astype(F32) + az[...].astype(F32)
    attended = attended + vec[pl.ds(4 + layer, 1), :]
    branch = fk[pl.ds(0, 128), :] + fg[pl.ds(0, 128), :].astype(F32) + fz[...].astype(F32)
    branch = branch + vec[pl.ds(6 + layer, 1), :]
    old = state[...].astype(F32)
    for at, item in enumerate((old, attended, branch)):
        total = jnp.sum(jnp.sum(item * item, axis=1, keepdims=True) * valid)
        squares[pl.ds(at, 1), :] = jnp.full((1, 128), total, F32)
    state_new = old + attended + branch
    new[...] = state_new
    if layer == 0:
        hat, _ = normalize(state_new)
        out[...] = (hat * vec[pl.ds(1, 1), :] + vec[pl.ds(3, 1), :]).astype(BF)
    else:
        out[...] = (state_new * valid).astype(BF)


def norm_back(place, state, slope, up, sk, sg, sz, vec, new, low, rows, *, layer):
    shard, length = place[2], place[3]
    spot = shard * 128 + lax.broadcasted_iota(jnp.int32, (128, 1), 0)
    given = slope[...].astype(F32)
    upstream = up[...].astype(F32)
    if layer == LAYERS - 1:
        given = jnp.where(spot < length, given, 0.0)
        upstream = given
    sn = sk[pl.ds(0, 128), :] + sg[pl.ds(0, 128), :].astype(F32) + sz[...].astype(F32)
    hat, factor = normalize(state[...].astype(F32))
    rows[...] = jnp.zeros_like(rows)
    rows[pl.ds(0, 1), :] = jnp.sum(sn * hat, axis=0, keepdims=True)
    rows[pl.ds(1, 1), :] = jnp.sum(sn, axis=0, keepdims=True)
    rows[pl.ds(2, 1), :] = jnp.sum(upstream, axis=0, keepdims=True)
    d = sn * vec[pl.ds(layer, 1), :]
    mean = jnp.mean(d, axis=-1, keepdims=True)
    along = jnp.mean(d * hat, axis=-1, keepdims=True)
    result = given + factor * (d - mean - hat * along)
    new[...] = result
    low[...] = result.astype(BF)


def vectors_out(place, rows0, bias0, rows1, bias1, out, full):
    shard = place[2]
    full[...] = jnp.zeros_like(full)
    for at, (rows, bias) in enumerate(((rows0, bias0), (rows1, bias1))):
        base = at * 7
        full[pl.ds(base, 3), :] = rows[pl.ds(0, 3), :]
        for p in range(3):
            full[pl.ds(base + 3 + p, 1), lanes(shard * 256, 256)] = bias[
                pl.ds(0, 1), pl.ds(W + p * 256, 256)
            ]
        full[pl.ds(base + 6, 1), :] = bias[pl.ds(0, 1), pl.ds(0, W)]
    out[pl.ds(0, 16), :] = full[:, pl.ds(0, 512)]
    out[pl.ds(16, 16), :] = full[:, pl.ds(512, 512)]


def second_cut(place, own, r1, r2, r3, c0, c1, c2, c3, *, axis):
    at = place[axis]
    for o in range(4):
        for e, ref in enumerate((c0, c1, c2, c3)):
            rows = rows_at(o * 64 + ((at + e) & 3) * 16, 16)
            total = own[rows, :].astype(F32)
            for other in (r1, r2, r3):
                total = total + other[rows, :].astype(F32)
            ref[pl.ds(o * 16, 16), :] = total.astype(BF)


def z_send(place, a0, a1, a2, a3, b0, b1, b2, b3, vector, side, across, cross, plain, wide):
    shard = place[2]
    z_lo = shard >> 1
    a = a0[...].astype(F32) + a1[...].astype(F32) + a2[...].astype(F32) + a3[...].astype(F32)
    b = b0[...].astype(F32) + b1[...].astype(F32) + b2[...].astype(F32) + b3[...].astype(F32)
    wide[:, pl.ds(0, W)] = b[:, 0:W]
    wide[:, pl.ds(W, 512)] = a[:, W:CHUNK]
    wide[:, pl.ds(1536, 256)] = b[:, W:1280]
    plain[:, pl.ds(0, W)] = a[:, 0:W]
    plain[:, pl.ds(W, 256)] = b[:, 1280:CHUNK]
    cross[...] = wide[rows_at(z_lo * 32, 32), :]
    side[:, pl.ds(0, WIDE)] = wide[rows_at((1 - z_lo) * 32, 32), :].astype(BF)
    side[:, pl.ds(WIDE, 512)] = vector[...].astype(BF)
    across[:, pl.ds(0, WIDE)] = cross[...].astype(BF)
    across[:, pl.ds(WIDE, 1280)] = plain[pl.ds(0, 32), :].astype(BF)
    across[:, pl.ds(WIDE + 1280, 1280)] = plain[pl.ds(32, 32), :].astype(BF)
    across[:, pl.ds(WIDE + 2560, 512)] = vector[...].astype(BF)


def local_rows():
    row = lax.broadcasted_iota(jnp.int32, (32, 1), 0) & 15
    return (row == 6) | (row == 13)


def z_sum(place, cross, plain, vector, za, zb, z2, near, kept, whole, vec, both):
    core = place[2] & 1
    both[pl.ds(0, 32), :] = cross[...] + z2[:, pl.ds(0, WIDE)].astype(F32)
    both[pl.ds(32, 32), :] = za[:, pl.ds(0, WIDE)].astype(F32) + zb[:, pl.ds(0, WIDE)].astype(F32)
    for at in range(2):
        own = both[rows_at(at * 32 + core * 16, 16), :]
        other = both[rows_at(at * 32 + (1 - core) * 16, 16), :]
        kept[pl.ds(at * 16, 16), :] = own
        near[pl.ds(at * 16, 16), pl.ds(0, WIDE)] = other.astype(BF)
    for at in range(2):
        rows = pl.ds(at * 32, 32)
        got = z2[:, pl.ds(WIDE + at * 1280, 1280)].astype(F32)
        whole[rows, :] = (plain[rows, :] + got).astype(BF)
    sides = za[:, pl.ds(WIDE, 512)].astype(F32) + zb[:, pl.ds(WIDE, 512)].astype(F32)
    total = vector[...] + z2[:, pl.ds(WIDE + 2560, 512)].astype(F32)
    total = total + jnp.where(local_rows(), 0.0, sides)
    vec[...] = total
    near[:, pl.ds(WIDE, 512)] = total.astype(BF)


def payload(place, kept, near, whole, vec, a, b):
    shard = place[2]
    for k in range(4):
        rows = rows_at((shard ^ k) * 16, 16)
        ref, at = (near, k >> 1) if k & 1 else (kept, k >> 1)
        source = ref[pl.ds(at * 16, 16), pl.ds(0, WIDE)].astype(BF)
        b[rows, pl.ds(0, W)] = source[:, 0:W]
        a[rows, pl.ds(W, 512)] = source[:, W:1536]
        b[rows, pl.ds(W, 256)] = source[:, 1536:WIDE]
    a[pl.ds(0, 64), pl.ds(0, W)] = whole[:, pl.ds(0, W)]
    b[pl.ds(0, 64), pl.ds(1280, 256)] = whole[:, pl.ds(W, 256)]
    if a.shape[0] == 64:
        return
    total = vec[...] + jnp.where(local_rows(), 0.0, near[:, pl.ds(WIDE, 512)].astype(F32))
    low = total.astype(BF)
    a[pl.ds(64, 16), :] = jnp.zeros((16, CHUNK), BF)
    a[pl.ds(64, 16), pl.ds(0, 512)] = low[0:16]
    a[pl.ds(64, 16), pl.ds(512, 512)] = low[16:32]


def assemble(place, *refs, layer):
    a_refs, b_refs = refs[0:4], refs[4:8]
    refs = refs[8 + (4 if layer == 0 else 0) :]
    t_out, m_out, e_out, s_out, v_out, t, m, e, s, sems = refs
    x, y = place[0], place[1]
    started = []
    vector = jnp.zeros((16, W), F32)
    for d in range(4):
        for h in range(4):
            base = pl.multiple_of(((x + d) & 3) * 64 + ((y + h) & 3) * 16, 16)
            for o in range(4):
                value = a_refs[d][pl.ds(h * 64 + o * 16, 16), :].astype(F32)
                s[rows_at(o * 256 + base, 16), :] = value[:, 0:W]
                rows = pl.ds(base, 16)
                t[rows, pl.ds(o * 256, 256)] = value[:, W:1280]
                t[rows, pl.ds(W + o * 256, 256)] = value[:, 1280:CHUNK]
        if layer == 0:
            vector = vector + a_refs[d][pl.ds(256, 16), pl.ds(0, W)].astype(F32)
    started += copies([(s, s_out.at[layer])], sems)
    for d in range(4):
        for h in range(4):
            rows = pl.ds(pl.multiple_of(((y + d) & 3) * 64 + ((x + h) & 3) * 16, 16), 16)
            for o in range(4):
                value = b_refs[d][pl.ds(h * 64 + o * 16, 16), :].astype(F32)
                e[rows, pl.ds(o * W, W)] = value[:, 0:W]
                t[rows, pl.ds(2 * W + o * 256, 256)] = value[:, W:1280]
                m[rows, pl.ds(o * 256, 256)] = value[:, 1280:CHUNK]
    pairs = [(t, t_out.at[layer]), (m, m_out.at[layer]), (e, e_out.at[layer])]
    started += copies(pairs, sems.at[pl.ds(1, 3)])
    v_out[...] = vector
    finish(started)


def bundle(own, r1, r2, r3, out):
    for h, ref in enumerate((own, r1, r2, r3)):
        out[pl.ds(h * 64, 64), :] = ref[pl.ds(0, 64), :]
    if out.shape[0] > 256:
        rows = pl.ds(64, 16)
        total = own[rows, :].astype(F32) + r1[rows, :].astype(F32)
        total = total + r2[rows, :].astype(F32) + r3[rows, :].astype(F32)
        out[pl.ds(256, 16), :] = total.astype(BF)


def sum_over_reps(place, start, a, b, vector, layer, earlier):
    def exchange(chunks, axis):
        return [chunks[0]] + [step(chunks[d], axis, d) for d in (1, 2, 3)]

    a = exchange(a, 0)
    b = exchange(b, 1)
    chunk = [shape(64, CHUNK)] * 4
    a = call(functools.partial(second_cut, axis=1), [start] + a, [SM] + [VM] * 4, chunk)
    b = call(functools.partial(second_cut, axis=0), [start] + b, [SM] + [VM] * 4, chunk)
    a = exchange(a, 1)
    b = exchange(b, 0)
    side, across, cross, plain = call(
        z_send, [place] + a + b + [vector], [SM] + [VM] * 9,
        [shape(32, 2304), shape(32, 4864), shape(32, WIDE, dtype=F32), shape(64, 1280, dtype=F32)],
        scratch=[pltpu.VMEM((64, WIDE), F32)],
    )
    z2 = move(across, flip_z=2)
    za = move(side, flip_z=1)
    zb = move(side, flip_z=3)
    near, kept, whole, vec = call(
        z_sum, [place, cross, plain, vector, za, zb, z2], [SM] + [VM] * 6,
        [shape(32, 2304), shape(32, WIDE, dtype=F32), shape(64, 1280), shape(32, 512, dtype=F32)],
        scratch=[pltpu.VMEM((64, WIDE), F32)],
    )
    near = move(near, flip_core=1)
    a, b = call(
        payload, [place, kept, near, whole, vec], [SM] + [VM] * 4,
        [shape(64 if layer else 80, CHUNK), shape(64, CHUNK)],
    )

    def collect(own, axis):
        return [own] + [step(own, axis, -d) for d in (1, 2, 3)]

    (a,) = call(bundle, collect(a, 1), [VM] * 4, [shape(256 if layer else 272, CHUNK)])
    (b,) = call(bundle, collect(b, 0), [VM] * 4, [shape(256, CHUNK)])
    a = collect(a, 0)
    b = collect(b, 1)
    outs = [
        shape(LAYERS, 256, 3072, dtype=F32),
        shape(LAYERS, 256, 1024, dtype=F32),
        shape(LAYERS, 256, 4096, dtype=F32),
        shape(LAYERS, 1024, 1024, dtype=F32),
        shape(16, W, dtype=F32),
    ]
    args, specs = [place] + a + b, [SM] + [VM] * 8
    aliases = {}
    if layer == 0:
        args, specs = args + list(earlier), specs + [ANY] * 4
        aliases = {9 + i: i for i in range(4)}
    return call(
        functools.partial(assemble, layer=layer), args, specs, outs, out_specs=[ANY] * 4 + [VM],
        scratch=[
            pltpu.VMEM((256, 3072), F32),
            pltpu.VMEM((256, 1024), F32),
            pltpu.VMEM((256, 4096), F32),
            pltpu.VMEM((1024, 1024), F32),
            pltpu.SemaphoreType.DMA((4,)),
        ],
        aliases=aliases,
    )


def gather_tokens(own):
    far = move(own, flip_z=1)
    near = move(own, flip_core=1)
    return [own, near, far, move(far, flip_core=1)]


def body(
    inputs,
    lengths,
    gains,
    shifts,
    triple,
    triple_bias,
    merger,
    merger_bias,
    expander,
    expander_bias,
    shrinker,
    shrinker_bias,
    cotangent,
):
    rep = lax.axis_index("rep")
    shard = lax.axis_index("shard")
    length = lengths[0]
    place = jnp.stack([rep // 8, rep % 4, shard, length]).astype(jnp.int32)

    pieces = call(
        cut_triple, [place, triple], [SM, ANY], [shape(256, 768)] + [shape(128, 768)] * 4,
        scratch=[pltpu.VMEM((256, 3072), BF), pltpu.SemaphoreType.DMA((1,))],
    )
    x_blocks = gather_tokens(inputs)
    small = jnp.concatenate(
        [v.reshape(-1, 256) for v in (gains, shifts, merger_bias, shrinker_bias, triple_bias)]
    )
    small = [small] + [move(small, flip_z=k >> 1, flip_core=k & 1) for k in (1, 2, 3)]

    def halves(cut):
        return [
            move(cut[0], flip_core=1),
            move(cut[1], flip_z=1),
            move(cut[2], flip_z=3),
            move(cut[3], flip_z=1, flip_core=1),
            move(cut[4], flip_z=3, flip_core=1),
        ]

    t_pieces = halves(pieces)
    cut = call(
        cut_rest, [after(place, pieces[0]), triple, expander], [SM, ANY, ANY],
        [shape(256, W)] + [shape(128, W)] * 4 + [shape(256, WIDE)] * 3,
        scratch=[
            pltpu.VMEM((256, 3072), BF), pltpu.VMEM((256, 4096), BF), pltpu.VMEM((256, 4096), BF),
            pltpu.SemaphoreType.DMA((3,)),
        ],
    )
    e_pieces = halves(after(tuple(cut[:5]), t_pieces[2], t_pieces[4]))
    rest = after(tuple(cut[5:]), e_pieces[2], e_pieces[4])
    w_pieces = [
        move(rest[0], flip_core=1),
        move(rest[1], flip_z=3),
        move(rest[2], flip_z=3, flip_core=1),
    ]
    up_blocks = gather_tokens(after(cotangent, e_pieces[1], e_pieces[3]))

    lined = jnp.stack([pick(jnp.stack(small), shard ^ j) for j in range(4)]).astype(F32)
    triple_rows = lined[:, 8:14].reshape(4, LAYERS, 3, 256).transpose(1, 0, 2, 3)
    triple_rows = pick(triple_rows.reshape(LAYERS, 3, 4, 256), shard, 2).reshape(LAYERS, 768)
    vec = jnp.concatenate(
        [
            lined[:, :8].transpose(1, 0, 2).reshape(8, W),
            jnp.pad(triple_rows, ((0, 0), (0, 256))),
            expander_bias.astype(F32),
        ]
    )
    spot = jnp.arange(512, dtype=jnp.int32)
    spot = (((spot >> 7) ^ shard) << 7) | (spot & 127)
    index = jnp.arange(ROT // 2, dtype=F32)
    freq = jnp.exp(index * (-2.0 * math.log(10000.0) / ROT))
    lane = jnp.arange(256, dtype=jnp.int32) % HD
    phase = spot.astype(F32)[:, None] * jnp.tile(freq, 16)[None, :]
    cosine, sine = jnp.cos(phase), jnp.sin(phase)
    turn = jnp.stack(
        [
            jnp.where(lane < ROT, cosine, 1.0),
            jnp.where(lane < ROT // 2, -sine, 0.0),
            jnp.where((lane >= ROT // 2) & (lane < ROT), sine, 0.0),
        ]
    )

    full = shape(512, W)
    send, keep = shape(256, W), shape(256, W, dtype=F32)
    wide = pltpu.VMEM((W, WIDE), BF)
    merge, shrink = pltpu.VMEM((256, W), BF), pltpu.VMEM((W, W), BF)

    normed0, qkv0, mixed0, a_send, a_keep = call(
        first_attention,
        [place] + x_blocks + [vec, turn, triple, merger] + t_pieces,
        [SM] + [VM] * 6 + [ANY] * 7,
        [full, shape(512, 768), shape(512, 256), send, keep],
        scratch=[wide, merge, pltpu.SemaphoreType.DMA((9,))],
        flops=2 * 10**9,
    )
    a_got = move(a_send, flip_core=1)
    before0, f_send, f_keep = call(
        first_forward,
        [place, normed0, vec, expander, shrinker] + e_pieces,
        [SM, VM, VM] + [ANY] * 7,
        [shape(512, W, dtype=F32), send, keep],
        scratch=[wide, shrink, pltpu.VMEM((512, W), BF), pltpu.SemaphoreType.DMA((7,))],
        flops=2 * 10**9,
    )
    f_got = move(f_send, flip_core=1)

    def other(kept, got):
        return move((kept[128:] + got[128:].astype(F32)).astype(BF), flip_z=1)

    sums = [a_keep, a_got, other(a_keep, a_got), f_keep, f_got, other(f_keep, f_got)]
    block = [shape(128, W, dtype=F32), shape(128, W), shape(8, 128, dtype=F32)]
    state1, normed1, squares0 = call(
        functools.partial(join, layer=0), [place, inputs] + sums + [vec], [SM] + [VM] * 8, block
    )
    n_blocks = gather_tokens(normed1)

    (normed1, up1, act1, ss1, mixed1, a_send, a_keep, f_send, f_keep, send1, keep1, bias1) = call(
        last_layer,
        [place] + n_blocks + up_blocks + [vec, turn, triple, merger, expander, shrinker] + w_pieces,
        [SM] + [VM] * 10 + [ANY] * 7,
        [full, full, full, shape(512, WIDE), shape(512, 256)]
        + [send, keep] * 3
        + [shape(8, WIDE, dtype=F32)],
        scratch=[
            wide, merge, shrink, pltpu.VMEM((512, 768), BF), pltpu.VMEM((512, 768), F32),
            pltpu.VMEM((512, 256), BF), pltpu.VMEM((512, W), F32), pltpu.SemaphoreType.DMA((9,)),
        ],
        flops=8 * 10**9,
    )
    got1 = move(send1, flip_core=1)
    far1 = other(keep1, got1)
    a1, b1 = weight_terms(place, act1, normed1, up1, ss1, mixed1)
    slope1, low1, rows1 = call(
        functools.partial(norm_back, layer=1),
        [place, state1, cotangent, cotangent, keep1, got1, far1, vec],
        [SM] + [VM] * 7,
        [shape(128, W, dtype=F32), shape(128, W), shape(8, W, dtype=F32)],
    )
    u_blocks = gather_tokens(low1)
    a_got = move(a_send, flip_core=1)
    f_got = move(f_send, flip_core=1)
    sums = [a_keep, a_got, other(a_keep, a_got), f_keep, f_got, other(f_keep, f_got)]
    _, hidden_out, squares1 = call(
        functools.partial(join, layer=1), [place, state1] + sums + [vec], [SM] + [VM] * 8, block
    )

    up0, act0, ss0, send0, keep0, bias0 = call(
        first_back,
        [place] + u_blocks + [before0, qkv0, turn, triple, merger, expander, shrinker]
        + t_pieces + e_pieces,
        [SM] + [VM] * 7 + [ANY] * 14,
        [full, full, shape(512, WIDE), send, keep, shape(8, WIDE, dtype=F32)],
        scratch=[
            wide, merge, shrink, pltpu.VMEM((512, 768), F32), pltpu.VMEM((512, 256), BF),
            pltpu.SemaphoreType.DMA((16,)),
        ],
        flops=5 * 10**9,
    )
    *sums1, _ = sum_over_reps(place, after(place, up0), a1, b1, jnp.zeros((32, 512), F32), 1, None)
    a0, b0 = weight_terms(place, act0, normed0, up0, ss0, mixed0)
    got0 = move(send0, flip_core=1)
    far0 = other(keep0, got0)
    input_grad, _, rows0 = call(
        functools.partial(norm_back, layer=0),
        [place, inputs, slope1, low1, keep0, got0, far0, vec],
        [SM] + [VM] * 7,
        [shape(128, W, dtype=F32), shape(128, W), shape(8, W, dtype=F32)],
    )
    (vector,) = call(
        vectors_out, [place, rows0, bias0, rows1, bias1], [SM] + [VM] * 4,
        [shape(32, 512, dtype=F32)], scratch=[pltpu.VMEM((16, W), F32)],
    )
    *sums0, summed = sum_over_reps(place, place, a0, b0, vector, 0, sums1)

    totals = jnp.concatenate([squares0[:3, :1], squares1[:3, :1]]).reshape(1, 6)
    totals = totals + move(totals, flip_core=1)
    totals = totals + move(totals, flip_z=1)
    rms_stats = jnp.sqrt(totals / (length.astype(F32) * W) + 1e-06)

    def vector_of(row, count):
        both = jnp.stack([summed[row : row + count], summed[row + 7 : row + 7 + count]])
        return pick(both.reshape(LAYERS, 4, -1), shard, 1)

    bias_part = vector_of(2, 1)
    return (
        hidden_out,
        input_grad,
        vector_of(0, 1),
        vector_of(1, 1),
        sums0[0],
        vector_of(3, 3),
        sums0[1],
        bias_part,
        sums0[2],
        jnp.stack([summed[6], summed[13]]),
        sums0[3],
        bias_part,
        rms_stats,
    )


def solution(mesh):
    return jax.shard_map(
        body,
        mesh=mesh,
        in_specs=(
            P(("rep", "shard"), None),
            P("rep"),
            P(None, "shard"),
            P(None, "shard"),
            P(None, "shard", None),
            P(None, "shard"),
            P(None, "shard", None),
            P(None, "shard"),
            P(None, "shard", None),
            P(None, "shard"),
            P(None, "shard", None),
            P(None, "shard"),
            P(("rep", "shard"), None),
        ),
        out_specs=(
            P(("rep", "shard"), None),
            P(("rep", "shard"), None),
            P(None, "shard"),
            P(None, "shard"),
            P(None, "shard", None),
            P(None, "shard"),
            P(None, "shard", None),
            P(None, "shard"),
            P(None, "shard", None),
            P(None, "shard"),
            P(None, "shard", None),
            P(None, "shard"),
            P("rep", None),
        ),
        check_vma=False,
    )
```

```python
import functools
import math

import jax
import jax.numpy as jnp
from jax import lax
from jax.experimental import pallas as pl
from jax.experimental.pallas import tpu as pltpu
from jax.sharding import PartitionSpec as P

HD = 64
ROT = 32
LAYERS = 2
EPS_NORM = 1e-05
AXES = ("rep", "shard")
BF = jnp.bfloat16
F32 = jnp.float32
MINE = 4
W = 1024
WIDE = 1792
PART = 768
PAIR = 1536
ORDERS = ((0, 2, 1, 3), (2, 0, 1, 3), (1, 3, 2, 0), (3, 1, 2, 0))

VM = pl.BlockSpec(memory_space=pltpu.VMEM)
ANY = pl.BlockSpec(memory_space=pl.ANY)
SM = pl.BlockSpec(memory_space=pltpu.SMEM)


def place_of(index):
    rep, shard = divmod(index, 4)
    x, rest = divmod(rep, 8)
    z_hi, y = divmod(rest, 4)
    z_lo, core = divmod(shard, 2)
    return x, y, z_hi * 2 + z_lo, core


def index_of(x, y, z, core):
    return ((x * 2 + z // 2) * 4 + y) * 4 + (z % 2) * 2 + core


def move(value, flip_x=0, flip_y=0, flip_z=0, flip_core=0):
    pairs = []
    for index in range(128):
        x, y, z, core = place_of(index)
        pairs.append((index, index_of(x ^ flip_x, y ^ flip_y, z ^ flip_z, core ^ flip_core)))
    return lax.ppermute(value, AXES, pairs)


def hop(value, link):
    by = 3 if link & 1 else 1
    return move(value, flip_y=by) if link > 1 else move(value, flip_x=by)


def link_bit(place, link):
    return place[4 + link]


def after(value, *others):
    return lax.optimization_barrier((value,) + others)[0]


def pick(value, index, axis=0):
    return lax.dynamic_index_in_dim(value, index, axis, keepdims=False)


def shape(*dims, dtype=BF):
    return jax.ShapeDtypeStruct(dims, dtype)


def call(body, args, specs, outs, out_specs=None, scratch=(), flops=0, aliases=None):
    return pl.pallas_call(
        body,
        out_shape=outs,
        in_specs=specs,
        out_specs=out_specs or [VM] * len(outs),
        scratch_shapes=scratch,
        input_output_aliases=aliases or {},
        compiler_params=pltpu.CompilerParams(vmem_limit_bytes=56 * 2**20),
        cost_estimate=pl.CostEstimate(flops=flops, bytes_accessed=10**6, transcendentals=0),
    )(*args)


def dot(left, right):
    return jnp.dot(left, right, preferred_element_type=F32)


def dot_t(left, right):
    return lax.dot_general(left, right, (((1,), (1,)), ((), ())), preferred_element_type=F32)


def t_dot(left, right):
    return lax.dot_general(left, right, (((0,), (0,)), ((), ())), preferred_element_type=F32)


def copies(pairs, sems):
    started = []
    for at, (source, target) in enumerate(pairs):
        copy = pltpu.make_async_copy(source, target, sems.at[at])
        copy.start()
        started.append(copy)
    return started


def finish(started):
    for copy in started:
        copy.wait()


def lanes(start, size):
    return pl.ds(pl.multiple_of(start, 128), size)


def rows_at(start, size):
    return pl.ds(pl.multiple_of(start, 16), size)


def cut_triple(
    place, gains, shifts, merger_bias, shrinker_bias, triple_bias, triple,
    small, out1, out2a, out2b, out3a, out3b, slab, sems,
):
    shard = place[2]
    started = copies([(triple.at[0], slab)], sems)
    narrow = [v[...].astype(F32) for v in (gains, shifts, merger_bias, shrinker_bias)]
    narrow = jnp.concatenate(narrow + [jnp.zeros((8, 256), F32)], axis=0)
    tall = jnp.concatenate(
        [jnp.zeros((8, 768), F32), triple_bias[...].astype(F32), jnp.zeros((6, 768), F32)], axis=0
    )
    both = jnp.concatenate([narrow, jnp.zeros((16, 512), F32)], axis=1) + tall
    small[...] = both.astype(BF)
    for ref in (out1, out2a, out3a):
        ref[pl.ds(ref.shape[0] - 16, 16), :] = both.astype(BF)
    finish(started)
    for k, refs in ((2, (out2a, out2b)), (3, (out3a, out3b)), (1, (out1,))):
        block = shard ^ k
        size = 256 // len(refs)
        for at, ref in enumerate(refs):
            for p in range(3):
                ref[pl.ds(0, size), pl.ds(p * 256, 256)] = slab[
                    pl.ds(at * size, size), lanes(p * W + block * 256, 256)
                ]


def cut_rest(
    place, triple, expander, e1, e2a, e2b, e3a, e3b, w1, w2, w3, slab, first, second, sems
):
    shard = place[2]
    pairs = [(expander.at[0], first), (expander.at[1], second), (triple.at[1], slab)]
    started = copies(pairs, sems)
    started[0].wait()
    for k, refs in ((2, (e2a, e2b)), (3, (e3a, e3b)), (1, (e1,))):
        size = 256 // len(refs)
        for at, ref in enumerate(refs):
            ref[...] = first[pl.ds(at * size, size), lanes((shard ^ k) * W, W)]
    finish(started[1:])
    for k, ref in ((2, w2), (3, w3), (1, w1)):
        block = shard ^ k
        ref[:, pl.ds(0, W)] = second[:, lanes(block * W, W)]
        for p in range(3):
            ref[:, pl.ds(W + p * 256, 256)] = slab[:, lanes(p * W + block * 256, 256)]


def own_triple(shard, layer, triple, wide):
    return [
        (
            triple.at[layer, :, lanes(p * W + shard * 256, 256)],
            wide.at[rows_at(shard * 256, 256), pl.ds(W + p * 256, 256)],
        )
        for p in range(3)
    ]


def own_expander(shard, layer, expander, wide):
    return [
        (expander.at[layer, :, lanes(shard * W, W)], wide.at[rows_at(shard * 256, 256), pl.ds(0, W)])
    ]


def first_triple(shard, pieces, wide):
    pairs = []
    one, two_a, two_b, three_a, three_b = pieces
    for k, refs in ((1, (one,)), (2, (two_a, two_b)), (3, (three_a, three_b))):
        size = 256 // len(refs)
        for at, ref in enumerate(refs):
            target = wide.at[rows_at((shard ^ k) * 256 + at * size, size), pl.ds(W, 768)]
            pairs.append((ref.at[pl.ds(0, size)], target))
    return pairs


def first_expander(shard, pieces, wide):
    pairs = []
    one, two_a, two_b, three_a, three_b = pieces
    for k, refs in ((1, (one,)), (2, (two_a, two_b)), (3, (three_a, three_b))):
        size = 256 // len(refs)
        for at, ref in enumerate(refs):
            pairs.append((ref, wide.at[rows_at((shard ^ k) * 256 + at * size, size), pl.ds(0, W)]))
    return pairs


def second_wide(shard, pieces, wide):
    return [
        (ref, wide.at[rows_at((shard ^ k) * 256, 256), :]) for k, ref in zip((1, 2, 3), pieces)
    ]


def spots(shard):
    row = lax.broadcasted_iota(jnp.int32, (512, 1), 0)
    col = lax.broadcasted_iota(jnp.int32, (1, 512), 1)

    def at(i):
        return (((i >> 7) ^ shard) << 7) | (i & 127)

    return at(row), at(col)


def rotate(values, turn, back=False):
    ahead = pltpu.roll(values, 256 - 16, 1) * turn[1]
    behind = pltpu.roll(values, 16, 1) * turn[2]
    if back:
        return values * turn[0] - ahead - behind
    return values * turn[0] + ahead + behind


def normalize(state):
    mean = jnp.mean(state, axis=-1, keepdims=True)
    centred = state - mean
    spread = jnp.mean(centred * centred, axis=-1, keepdims=True)
    factor = lax.rsqrt(spread + EPS_NORM)
    return centred * factor, factor


ROOT = math.sqrt(2.0 / math.pi)


def gelu_both(v):
    square = v * v
    t = jnp.tanh(ROOT * v * (1.0 + 0.044715 * square))
    half = 0.5 * (1.0 + t)
    slope = half + 0.5 * v * (1.0 - t * t) * (ROOT + (3.0 * 0.044715 * ROOT) * square)
    return v * half, slope


def heads_out(normed, wide, bias, turn, qkv):
    scale = HD ** (-0.5)
    for p in range(3):
        part = dot(normed[...], wide[:, pl.ds(W + p * 256, 256)]) + bias[:, pl.ds(p * 256, 256)]
        if p < 2:
            part = rotate(part, turn)
        if p == 0:
            part = part * scale
        qkv[:, pl.ds(p * 256, 256)] = part.astype(BF)


def probabilities(qkv, h, allowed):
    q = qkv[:, pl.ds(h * HD, HD)]
    k = qkv[:, pl.ds(256 + h * HD, HD)]
    scores = jnp.where(allowed, dot_t(q, k), -1000000000.0)
    powered = jnp.exp(scores - jnp.max(scores, axis=-1, keepdims=True))
    return powered * (1.0 / jnp.sum(powered, axis=-1, keepdims=True))


def attend(qkv, allowed, mixed):
    for h in range(MINE):
        low = probabilities(qkv, h, allowed).astype(BF)
        mixed[:, pl.ds(h * HD, HD)] = dot(low, qkv[:, pl.ds(512 + h * HD, HD)]).astype(BF)


def attend_back(qkv, allowed, mixed, slope_mixed, slopes, forward):
    for h in range(MINE):
        probs = probabilities(qkv, h, allowed)
        low = probs.astype(BF)
        q = qkv[:, pl.ds(h * HD, HD)]
        k = qkv[:, pl.ds(256 + h * HD, HD)]
        v = qkv[:, pl.ds(512 + h * HD, HD)]
        if forward:
            mixed[:, pl.ds(h * HD, HD)] = dot(low, v).astype(BF)
        out = slope_mixed[:, pl.ds(h * HD, HD)]
        slope_probs = dot_t(out, v)
        centre = jnp.sum(probs * slope_probs, axis=-1, keepdims=True)
        slope_scores = (probs * (slope_probs - centre)).astype(BF)
        slopes[:, pl.ds(h * HD, HD)] = dot(slope_scores, k)
        slopes[:, pl.ds(256 + h * HD, HD)] = t_dot(slope_scores, q)
        slopes[:, pl.ds(512 + h * HD, HD)] = t_dot(low, out)


def hand_out(left, right, send, keep):
    for n in range(4):
        cols = pl.ds(n * 256, 256)
        part = dot(left[...], right[:, cols])
        spread_out(part, cols, send, keep)


def spread_out(part, cols, send, keep):
    keep[pl.ds(0, 128), cols] = part[0:128]
    send[pl.ds(0, 128), cols] = part[128:256].astype(BF)
    keep[pl.ds(128, 128), cols] = part[256:384]
    send[pl.ds(128, 128), cols] = part[384:512].astype(BF)


def first_attention(
    place, x0, x1, x2, x3, small, bias, turn, triple, merger, t1, t2a, t2b, t3a, t3b,
    normed, qkv, mixed, send, keep, vec, wide, merge, smalls, sems,
):
    shard, length = place[2], place[3]
    pairs = [(small, smalls.at[shard])]
    pairs += [(t1.at[pl.ds(256, 16)], smalls.at[shard ^ 1])]
    pairs += [(t2a.at[pl.ds(128, 16)], smalls.at[shard ^ 2])]
    pairs += [(t3a.at[pl.ds(128, 16)], smalls.at[shard ^ 3])]
    pairs += own_triple(shard, 0, triple, wide) + [(merger.at[0], merge)]
    started = copies(pairs + first_triple(shard, (t1, t2a, t2b, t3a, t3b), wide), sems)
    for copy in started[:4]:
        copy.wait()
    vec[...] = jnp.zeros_like(vec)
    for j in range(4):
        vec[pl.ds(0, 8), pl.ds(j * 256, 256)] = smalls[j].astype(F32)[0:8, 0:256]
    for p in range(3):
        block = p * 4 + shard
        j = (block * 11) >> 5
        vec[pl.ds(8, 2), pl.ds(p * 256, 256)] = smalls[j, :, lanes((block - 3 * j) * 256, 256)].astype(
            F32
        )[8:10]
    vec[pl.ds(10, 2), :] = bias[...].astype(F32)
    gain, shift = vec[pl.ds(0, 1), :], vec[pl.ds(2, 1), :]
    for k, ref in enumerate((x0, x1, x2, x3)):
        hat, _ = normalize(ref[...].astype(F32))
        normed[pl.ds(k * 128, 128), :] = (hat * gain + shift).astype(BF)
    finish(started[4:])
    row, col = spots(shard)
    allowed = (col <= row) & (col < length)
    heads_out(normed, wide, vec[pl.ds(8, 1), pl.ds(0, 768)], turn, qkv)
    attend(qkv, allowed, mixed)
    hand_out(mixed, merge, send, keep)


def first_forward(
    place, normed, vec, expander, shrinker, e1, e2a, e2b, e3a, e3b,
    before, send, keep, wide, shrink, act, sems,
):
    shard = place[2]
    pairs = own_expander(shard, 0, expander, wide) + first_expander(shard, (e1, e2a, e2b, e3a, e3b), wide)
    started = copies(pairs + [(shrinker.at[0], shrink)], sems)
    finish(started)
    for n in range(4):
        cols = pl.ds(n * 256, 256)
        part = dot(normed[...], wide[:, cols]) + vec[pl.ds(10, 1), cols]
        before[:, cols] = part
        act[:, cols] = gelu_both(part)[0].astype(BF)
    hand_out(act, shrink, send, keep)


def slopes_out(ss, bias, wide, send, keep):
    bias[...] = jnp.broadcast_to(jnp.sum(ss[...].astype(F32), axis=0, keepdims=True), bias.shape)
    for n in range(4):
        part = dot_t(ss[...], wide[pl.ds(n * 256, 256), :])
        spread_out(part, pl.ds(n * 256, 256), send, keep)


def triple_slopes(slopes, turn, ss):
    scale = HD ** (-0.5)
    ss[:, pl.ds(W, 256)] = (rotate(slopes[:, pl.ds(0, 256)], turn, True) * scale).astype(BF)
    ss[:, pl.ds(W + 256, 256)] = rotate(slopes[:, pl.ds(256, 256)], turn, True).astype(BF)
    ss[:, pl.ds(W + 512, 256)] = slopes[:, pl.ds(512, 256)].astype(BF)


def last_layer(
    place, n0, n1, n2, n3, u0, u1, u2, u3, vec, turn, triple, merger, expander, shrinker, w1, w2, w3,
    normed, up, act, ss, mixed, bsend, bkeep, send, keep, bias,
    wide, merge, shrink, qkv, slopes, out, before, sems,
):
    shard, length = place[2], place[3]
    pairs = own_triple(shard, 1, triple, wide) + own_expander(shard, 1, expander, wide)
    pairs += second_wide(shard, (w1, w2, w3), wide) + [(merger.at[1], merge), (shrinker.at[1], shrink)]
    started = copies(pairs, sems)
    row, col = spots(shard)
    for k, (n, u) in enumerate(((n0, u0), (n1, u1), (n2, u2), (n3, u3))):
        rows = pl.ds(k * 128, 128)
        normed[rows, :] = n[...]
        up[rows, :] = jnp.where(row[k * 128 : k * 128 + 128] < length, u[...].astype(F32), 0.0).astype(BF)
    finish(started)
    for n in range(4):
        cols = pl.ds(n * 256, 256)
        part = dot(normed[...], wide[:, cols]) + vec[pl.ds(11, 1), cols]
        value, slope = gelu_both(part)
        act[:, cols] = value.astype(BF)
        ss[:, cols] = (dot_t(up[...], shrink[cols, :]) * slope).astype(BF)
    hand_out(act, shrink, bsend.at[pl.ds(256, 256)], bkeep.at[pl.ds(256, 256)])
    allowed = (col <= row) & (col < length)
    heads_out(normed, wide, vec[pl.ds(9, 1), pl.ds(0, 768)], turn, qkv)
    out[...] = dot_t(up[...], merge[...]).astype(BF)
    attend_back(qkv, allowed, mixed, out, slopes, True)
    hand_out(mixed, merge, bsend.at[pl.ds(0, 256)], bkeep.at[pl.ds(0, 256)])
    triple_slopes(slopes, turn, ss)
    slopes_out(ss, bias, wide, send, keep)


def first_back(
    place, u0, u1, u2, u3, before, qkv, turn, triple, merger, expander, shrinker,
    t1, t2a, t2b, t3a, t3b, e1, e2a, e2b, e3a, e3b,
    up, act, ss, send, keep, bias, wide, merge, shrink, slopes, out, sems,
):
    shard, length = place[2], place[3]
    pairs = own_triple(shard, 0, triple, wide) + own_expander(shard, 0, expander, wide)
    pairs += first_triple(shard, (t1, t2a, t2b, t3a, t3b), wide)
    pairs += first_expander(shard, (e1, e2a, e2b, e3a, e3b), wide)
    started = copies(pairs + [(merger.at[0], merge), (shrinker.at[0], shrink)], sems)
    for k, u in enumerate((u0, u1, u2, u3)):
        up[pl.ds(k * 128, 128), :] = u[...]
    finish(started)
    for n in range(4):
        cols = pl.ds(n * 256, 256)
        value, slope = gelu_both(before[:, cols])
        act[:, cols] = value.astype(BF)
        ss[:, cols] = (dot_t(up[...], shrink[cols, :]) * slope).astype(BF)
    row, col = spots(shard)
    allowed = (col <= row) & (col < length)
    out[...] = dot_t(up[...], merge[...]).astype(BF)
    attend_back(qkv, allowed, None, out, slopes, False)
    triple_slopes(slopes, turn, ss)
    slopes_out(ss, bias, wide, send, keep)


def halve(term, cols, o, bit, send, keep, at):
    for ref, half in ((keep, bit), (send, 1 - bit)):
        value = term[pl.ds(pl.multiple_of(half * 128, 128), 128), cols].astype(BF)
        for k in range(8):
            ref[pl.ds(k * 64 + o * 16, 16), at] = value[k * 16 : k * 16 + 16]


def terms_one(place, act, up, normed, ss, s0, k0, s2, k2, term):
    whole = pl.ds(0, PART)
    for o in range(4):
        cols = pl.ds(o * 256, 256)
        term[...] = t_dot(act[:, cols], up[:, pl.ds(0, PART)])
        halve(term, whole, o, link_bit(place, ORDERS[0][0]), s0, k0, whole)
        term[...] = t_dot(normed[:, cols], ss[:, pl.ds(0, PART)])
        halve(term, whole, o, link_bit(place, ORDERS[2][0]), s2, k2, whole)


def terms_two(place, act, up, normed, ss, mixed, s1, k1, s3, k3, term, last):
    one, three = link_bit(place, ORDERS[1][0]), link_bit(place, ORDERS[3][0])
    whole = pl.ds(0, PART)
    last[...] = t_dot(mixed[...], up[...])
    for o in range(4):
        cols = pl.ds(o * 256, 256)
        term[:, pl.ds(0, 256)] = t_dot(act[:, cols], up[:, pl.ds(PART, 256)])
        term[:, pl.ds(256, 256)] = last[:, cols]
        both = t_dot(normed[:, cols], ss[:, pl.ds(PART, W)])
        term[:, pl.ds(512, 256)] = both[:, 256:512]
        halve(term, whole, o, one, s1, k1, whole)
        term[:, pl.ds(0, 256)] = both[:, 0:256]
        term[:, pl.ds(256, 512)] = both[:, 512:W]
        halve(term, whole, o, three, s3, k3, whole)


def weight_one(place, act, up, normed, ss):
    return call(
        terms_one, [place, act, up, normed, ss], [SM] + [VM] * 4, [shape(512, PART)] * 4,
        scratch=[pltpu.VMEM((256, PART), F32)], flops=2 * 10**9,
    )


def weight_two(place, act, up, normed, ss, mixed):
    return call(
        terms_two, [place, act, up, normed, ss, mixed], [SM] + [VM] * 5, [shape(512, PART)] * 4,
        scratch=[pltpu.VMEM((256, PART), F32), pltpu.VMEM((256, W), F32)], flops=2 * 10**9,
    )


def join(place, state, *refs, layer):
    shard, length = place[2], place[3]
    spot = shard * 128 + lax.broadcasted_iota(jnp.int32, (128, 1), 0)
    valid = (spot < length).astype(F32)
    if layer == 0:
        ak, ag, az, fk, fg, fz, vec, new, out, squares = refs
        attended = ak[pl.ds(0, 128), :] + ag[pl.ds(0, 128), :].astype(F32) + az[...].astype(F32)
        branch = fk[pl.ds(0, 128), :] + fg[pl.ds(0, 128), :].astype(F32) + fz[...].astype(F32)
    else:
        kept, got, far, vec, out, squares = refs
        attended, branch = [
            kept[pl.ds(at * 256, 128), :]
            + got[pl.ds(at * 256, 128), :].astype(F32)
            + far[pl.ds(at * 128, 128), :].astype(F32)
            for at in (0, 1)
        ]
    attended = attended + vec[pl.ds(4 + layer, 1), :]
    branch = branch + vec[pl.ds(6 + layer, 1), :]
    old = state[...].astype(F32)
    for at, item in enumerate((old, attended, branch)):
        total = jnp.sum(jnp.sum(item * item, axis=1, keepdims=True) * valid)
        squares[pl.ds(at, 1), :] = jnp.full((1, 128), total, F32)
    state_new = old + attended + branch
    if layer == 0:
        new[...] = state_new
        hat, _ = normalize(state_new)
        out[...] = (hat * vec[pl.ds(1, 1), :] + vec[pl.ds(3, 1), :]).astype(BF)
    else:
        out[...] = (state_new * valid).astype(BF)


def norm_back(place, state, slope, up, sk, sg, sz, vec, new, low, rows, *, layer):
    shard, length = place[2], place[3]
    spot = shard * 128 + lax.broadcasted_iota(jnp.int32, (128, 1), 0)
    given = slope[...].astype(F32)
    upstream = up[...].astype(F32)
    if layer == LAYERS - 1:
        given = jnp.where(spot < length, given, 0.0)
        upstream = given
    sn = sk[pl.ds(0, 128), :] + sg[pl.ds(0, 128), :].astype(F32) + sz[...].astype(F32)
    hat, factor = normalize(state[...].astype(F32))
    rows[...] = jnp.zeros_like(rows)
    rows[pl.ds(0, 1), :] = jnp.sum(sn * hat, axis=0, keepdims=True)
    rows[pl.ds(1, 1), :] = jnp.sum(sn, axis=0, keepdims=True)
    rows[pl.ds(2, 1), :] = jnp.sum(upstream, axis=0, keepdims=True)
    d = sn * vec[pl.ds(layer, 1), :]
    mean = jnp.mean(d, axis=-1, keepdims=True)
    along = jnp.mean(d * hat, axis=-1, keepdims=True)
    result = given + factor * (d - mean - hat * along)
    new[...] = result
    low[...] = result.astype(BF)


def vectors_out(place, rows0, bias0, rows1, bias1, out, full):
    shard = place[2]
    full[...] = jnp.zeros_like(full)
    for at, (rows, bias) in enumerate(((rows0, bias0), (rows1, bias1))):
        base = at * 7
        full[pl.ds(base, 3), :] = rows[pl.ds(0, 3), :]
        for p in range(3):
            full[pl.ds(base + 3 + p, 1), lanes(shard * 256, 256)] = bias[
                pl.ds(0, 1), pl.ds(W + p * 256, 256)
            ]
        full[pl.ds(base + 6, 1), :] = bias[pl.ds(0, 1), pl.ds(0, W)]
    out[pl.ds(0, 16), :] = full[:, pl.ds(0, 512)]
    out[pl.ds(16, 16), :] = full[:, pl.ds(512, 512)]


def add_half(kept, got, bit, refs, at):
    size = kept.shape[0] // 2
    for ref, half in zip(refs, (1 - bit, bit)):
        rows = rows_at(half * size, size)
        total = kept[rows, :].astype(F32) + got[rows, :].astype(F32)
        ref[:, at] = total.astype(BF)


def fold_one(place, ka, ga, kb, gb, sa, ha, sb, hb, *, parts):
    for part, (k, g, s, h) in zip(parts, ((ka, ga, sa, ha), (kb, gb, sb, hb))):
        add_half(k, g, link_bit(place, ORDERS[part][1]), (s, h), slice(None))


def fold_two(place, k0, g0, k1, g1, k2, g2, k3, g3, sa, ha, sb, hb):
    for part, (k, g) in enumerate(((k0, g0), (k1, g1), (k2, g2), (k3, g3))):
        refs = (sb, hb) if part > 1 else (sa, ha)
        at = pl.ds((part & 1) * PART, PART)
        add_half(k, g, link_bit(place, ORDERS[part][2]), refs, at)


def fold_three(place, ka, ga, kb, gb, sa, ha, sb, hb):
    for part, (k, g, s, h) in zip((0, 2), ((ka, ga, sa, ha), (kb, gb, sb, hb))):
        add_half(k, g, link_bit(place, ORDERS[part][3]), (s, h), slice(None))


def first_folds(place, kept, got, parts):
    args = [kept[0], got[0], kept[1], got[1]]
    return call(
        functools.partial(fold_one, parts=parts), [place] + args, [SM] + [VM] * 4, [shape(256, PART)] * 4
    )


def z_send(place, *refs):
    ka, ga, kb, gb, *refs = refs
    shard = place[2]
    z_lo = shard >> 1
    if len(refs) == 6:
        vector, *refs = refs
    else:
        vector = None
    side, across, cross, plain, wide = refs
    a = ka[...].astype(F32) + ga[...].astype(F32)
    b = kb[...].astype(F32) + gb[...].astype(F32)
    wide[:, pl.ds(0, W)] = b[:, 0:W]
    wide[:, pl.ds(W, 256)] = a[:, 1280:PAIR]
    wide[:, pl.ds(1280, 512)] = b[:, W:PAIR]
    plain[...] = a[:, 0:1280]
    cross[...] = wide[rows_at(z_lo * 32, 32), :]
    side[:, pl.ds(0, WIDE)] = wide[rows_at((1 - z_lo) * 32, 32), :].astype(BF)
    across[:, pl.ds(0, WIDE)] = cross[...].astype(BF)
    across[:, pl.ds(WIDE, 1280)] = plain[pl.ds(0, 32), :].astype(BF)
    across[:, pl.ds(WIDE + 1280, 1280)] = plain[pl.ds(32, 32), :].astype(BF)
    if vector is not None:
        side[:, pl.ds(WIDE, 512)] = vector[...].astype(BF)
        across[:, pl.ds(WIDE + 2560, 512)] = vector[...].astype(BF)


def local_rows():
    row = lax.broadcasted_iota(jnp.int32, (32, 1), 0) & 15
    return (row == 6) | (row == 13)


def z_sum(place, *refs):
    cross, plain, za, zb, z2, *refs = refs
    vector = None
    if len(refs) == 6:
        vector, *refs = refs
        near, kept, whole, vec, both = refs
    else:
        near, kept, whole, both = refs
    core = place[2] & 1
    both[pl.ds(0, 32), :] = cross[...] + z2[:, pl.ds(0, WIDE)].astype(F32)
    both[pl.ds(32, 32), :] = za[:, pl.ds(0, WIDE)].astype(F32) + zb[:, pl.ds(0, WIDE)].astype(F32)
    for at in range(2):
        own = both[rows_at(at * 32 + core * 16, 16), :]
        other = both[rows_at(at * 32 + (1 - core) * 16, 16), :]
        kept[pl.ds(at * 16, 16), :] = own.astype(BF)
        near[pl.ds(at * 16, 16), pl.ds(0, WIDE)] = other.astype(BF)
    for at in range(2):
        rows = pl.ds(at * 32, 32)
        got = z2[:, pl.ds(WIDE + at * 1280, 1280)].astype(F32)
        whole[rows, :] = (plain[rows, :] + got).astype(BF)
    if vector is not None:
        sides = za[:, pl.ds(WIDE, 512)].astype(F32) + zb[:, pl.ds(WIDE, 512)].astype(F32)
        total = vector[...] + z2[:, pl.ds(WIDE + 2560, 512)].astype(F32)
        total = total + jnp.where(local_rows(), 0.0, sides)
        vec[...] = total
        near[:, pl.ds(WIDE, 512)] = total.astype(BF)


def payload_parts(place, kept, near, whole, a, b):
    shard = place[2]
    for k in range(4):
        rows = rows_at((shard ^ k) * 16, 16)
        ref, at = (near, k >> 1) if k & 1 else (kept, k >> 1)
        source = ref[pl.ds(at * 16, 16), pl.ds(0, WIDE)]
        b[rows, pl.ds(0, W)] = source[:, 0:W]
        a[rows, pl.ds(1280, 256)] = source[:, W:1280]
        b[rows, pl.ds(W, 512)] = source[:, 1280:WIDE]
    a[pl.ds(0, 64), pl.ds(0, 1280)] = whole[...]


def payload_both(place, kept, near, whole, out):
    payload_parts(place, kept, near, whole, out.at[pl.ds(0, 64)], out.at[pl.ds(64, 64)])


def payload(place, kept, near, whole, *refs):
    *vec, a, b = refs
    payload_parts(place, kept, near, whole, a, b)
    if not vec:
        return
    vec = vec[0]
    total = vec[...] + jnp.where(local_rows(), 0.0, near[:, pl.ds(WIDE, 512)].astype(F32))
    low = total.astype(BF)
    a[pl.ds(64, 16), :] = jnp.zeros((16, PAIR), BF)
    a[pl.ds(64, 16), pl.ds(0, 512)] = low[0:16]
    a[pl.ds(64, 16), pl.ds(512, 512)] = low[16:32]


def line_up(own, got, bit, size, outs, cols):
    for ref, at in zip(outs, cols):
        ref[rows_at(bit * size, size), :] = own[pl.ds(0, size), at]
        ref[rows_at((1 - bit) * size, size), :] = got[pl.ds(0, size), at]


def vector_rows(own, got, at, size):
    rows = pl.ds(at, size)
    return (own[rows, :].astype(F32) + got[rows, :].astype(F32)).astype(BF)


def gather_four(place, oa, ga, ob, gb, a, b):
    line_up(oa, ga, link_bit(place, ORDERS[0][3]), 64, [a], [slice(None)])
    line_up(ob, gb, link_bit(place, ORDERS[2][3]), 64, [b], [slice(None)])
    if a.shape[0] > 128:
        a[pl.ds(128, 16), :] = vector_rows(oa, ga, 64, 16)


def gather_three(place, oa, ga, ob, gb, p0, p1, p2, p3):
    cols = [pl.ds(0, PART), pl.ds(PART, PART)]
    line_up(oa, ga, link_bit(place, ORDERS[0][2]), 128, [p0, p1], cols)
    line_up(ob, gb, link_bit(place, ORDERS[2][2]), 128, [p2, p3], cols)
    if p0.shape[0] == 256:
        return
    low = vector_rows(oa, ga, 128, 16)
    p0[pl.ds(256, 32), :] = jnp.zeros((32, PART), BF)
    p0[pl.ds(256, 16), pl.ds(0, 512)] = low[:, 0:512]
    p0[pl.ds(272, 16), pl.ds(0, 512)] = low[:, 512:W]


def gather_two(place, o0, g0, o1, g1, o2, g2, o3, g3, p0, p1, p2, p3):
    outs = (p0, p1, p2, p3)
    for part, (o, g) in enumerate(((o0, g0), (o1, g1), (o2, g2), (o3, g3))):
        line_up(o, g, link_bit(place, ORDERS[part][1]), 256, [outs[part]], [slice(None)])
    if p0.shape[0] > 512:
        p0[pl.ds(512, 32), :] = vector_rows(o0, g0, 256, 32)


def put(part, value, o, base, t, m, e, s):
    rows = rows_at(base, 16)
    if part == 0:
        s[rows_at(o * 256 + base, 16), pl.ds(0, PART)] = value
    elif part == 1:
        s[rows_at(o * 256 + base, 16), pl.ds(PART, 256)] = value[:, 0:256]
        m[rows, pl.ds(o * 256, 256)] = value[:, 256:512]
        t[rows, pl.ds(o * 256, 256)] = value[:, 512:PART]
    elif part == 2:
        e[rows, pl.ds(o * W, PART)] = value
    else:
        e[rows, pl.ds(o * W + PART, 256)] = value[:, 0:256]
        t[rows, pl.ds(W + o * 256, 256)] = value[:, 256:512]
        t[rows, pl.ds(2 * W + o * 256, 256)] = value[:, 512:PART]


def assemble_last(every, t_out, m_out, e_out, s_out, t, m, e, s, sems):
    for x in range(4):
        for y in range(4):
            bits = ((x & 1) ^ (x >> 1), x >> 1, (y & 1) ^ (y >> 1), y >> 1)
            for part in range(4):
                unit = sum(bits[link] << (3 - at) for at, link in enumerate(ORDERS[part]))
                for o in range(4):
                    first = (x * 4 + y) * 128 + (part >> 1) * 64 + o * 16
                    value = every[pl.ds(first, 16), pl.ds((part & 1) * PART, PART)].astype(F32)
                    put(part, value, o, unit * 16, t, m, e, s)
    pairs = [(t, t_out.at[1]), (m, m_out.at[1]), (e, e_out.at[1]), (s, s_out.at[1])]
    finish(copies(pairs, sems))


def assemble(place, *refs, layer):
    halves = refs[0:8]
    if layer == 0:
        refs = refs[12:]
        (t_out, m_out, e_out, s_out, g_sum, s_sum, b_sum, t_sum, e_sum, t, m, e, s, vec, sems) = refs
    else:
        t_out, m_out, e_out, s_out, t, m, e, s, sems = refs[8:]
    shard = place[2]
    started = []
    for part in (2, 0, 1, 3):
        bit = link_bit(place, ORDERS[part][0])
        for ref, half in ((halves[2 * part], bit), (halves[2 * part + 1], 1 - bit)):
            for k in range(8):
                for o in range(4):
                    value = ref[pl.ds(k * 64 + o * 16, 16), :].astype(F32)
                    put(part, value, o, half * 128 + k * 16, t, m, e, s)
        if part == 1:
            started += copies([(m, m_out.at[layer]), (s, s_out.at[layer])], sems)
    started += copies([(t, t_out.at[layer]), (e, e_out.at[layer])], sems.at[pl.ds(2, 2)])
    if layer == 0:
        low = vector_rows(halves[0], halves[1], 512, 32).astype(F32)
        vec[:, pl.ds(0, 512)] = low[0:16, 0:512]
        vec[:, pl.ds(512, 512)] = low[16:32, 0:512]
        for at in range(LAYERS):
            own_sums(vec, at, shard, g_sum, s_sum, b_sum, t_sum, e_sum)
    finish(started)


def own_sums(vec, layer, shard, g_sum, s_sum, b_sum, t_sum, e_sum):
    base = layer * 7
    row = pl.ds(layer, 1)
    for at, ref in enumerate((g_sum, s_sum, b_sum)):
        ref[row, :] = vec[pl.ds(base + at, 1), lanes(shard * 256, 256)]
    for r in range(3):
        block = shard * 3 + r
        t_sum[row, pl.ds(r * 256, 256)] = vec[
            pl.ds(base + 3 + (block >> 2), 1), lanes((block & 3) * 256, 256)
        ]
    e_sum[row, :] = vec[pl.ds(base + 6, 1), :]


def hops(values, parts, phase):
    return [hop(value, ORDERS[part][phase]) for value, part in zip(values, parts)]


def fold_middle(place, one, two):
    kept = [one[0], two[0], one[1], two[1]]
    got = [one[2], two[2], one[3], two[3]]
    args = [v for pair in zip(kept, got) for v in pair]
    sa, ka, sb, kb = call(fold_two, [place] + args, [SM] + [VM] * 8, [shape(128, PAIR)] * 4)
    ga, gb = hops([sa, sb], (0, 2), 2)
    return [ka, ga, kb, gb]


def fold_last(place, units):
    sa, ka, sb, kb = call(fold_three, [place] + units, [SM] + [VM] * 4, [shape(64, PAIR)] * 4)
    ga, gb = hops([sa, sb], (0, 2), 3)
    return [ka, ga, kb, gb]


def send_z(place, units, vector):
    more = 512 * len(vector)
    side, across, cross, plain = call(
        z_send, [place] + units + vector, [SM] + [VM] * (4 + len(vector)),
        [
            shape(32, WIDE + more), shape(32, WIDE + 2560 + more),
            shape(32, WIDE, dtype=F32), shape(64, 1280, dtype=F32),
        ],
        scratch=[pltpu.VMEM((64, WIDE), F32)],
    )
    z2 = move(across, flip_z=2)
    za = move(side, flip_z=1)
    zb = move(side, flip_z=3)
    return [cross, plain, za, zb, z2] + vector


def sum_z(place, terms):
    vectors = len(terms) - 5
    near, kept, whole, *vec = call(
        z_sum, [place] + terms, [SM] + [VM] * len(terms),
        [shape(32, WIDE + 512 * vectors), shape(32, WIDE), shape(64, 1280)]
        + [shape(32, 512, dtype=F32)] * vectors,
        scratch=[pltpu.VMEM((64, WIDE), F32)],
    )
    return [kept, move(near, flip_core=1), whole] + vec


OUTS = [
    shape(LAYERS, 256, 3072, dtype=F32),
    shape(LAYERS, 256, 1024, dtype=F32),
    shape(LAYERS, 256, 4096, dtype=F32),
    shape(LAYERS, 1024, 1024, dtype=F32),
]


def line_unit(place, pieces):
    rows = 80 if len(pieces) == 4 else 64
    a, b = call(
        payload, [place] + pieces, [SM] + [VM] * len(pieces), [shape(rows, PAIR), shape(64, PAIR)]
    )
    ga, gb = hops([a, b], (0, 2), 3)
    return [a, ga, b, gb]


def line_four(place, args):
    rows = args[0].shape[0] + 64
    a, b = call(gather_four, [place] + args, [SM] + [VM] * 4, [shape(rows, PAIR), shape(128, PAIR)])
    ga, gb = hops([a, b], (0, 2), 2)
    return [a, ga, b, gb]


def line_three(place, args):
    rows = 288 if args[0].shape[0] > 128 else 256
    own = call(
        gather_three, [place] + args, [SM] + [VM] * 4, [shape(rows, PART)] + [shape(256, PART)] * 3
    )
    got = hops(own, range(4), 1)
    return [v for pair in zip(own, got) for v in pair]


def line_two(place, args):
    rows = args[0].shape[0] + 256
    own = call(
        gather_two, [place] + args, [SM] + [VM] * 8, [shape(rows, PART)] + [shape(512, PART)] * 3
    )
    got = hops(own, range(4), 0)
    return [v for pair in zip(own, got) for v in pair]


def collect_last(place, pieces):
    (both,) = call(payload_both, [place] + pieces, [SM] + [VM] * 3, [shape(128, PAIR)])
    planes = [[(x * 2 + z) * 4 + y for x in range(4) for y in range(4)] for z in range(2)]
    return lax.all_gather(both, "rep", axis_index_groups=planes, axis=0, tiled=True)


def put_last(every):
    return call(
        assemble_last, [every], [VM], OUTS, out_specs=[ANY] * 4,
        scratch=[pltpu.VMEM(out.shape[1:], F32) for out in OUTS] + [pltpu.SemaphoreType.DMA((4,))],
    )


def put_sums(place, halves, earlier):
    outs, specs = list(OUTS), [ANY] * 4
    scratch = [pltpu.VMEM(out.shape[1:], F32) for out in OUTS]
    if earlier:
        outs += [shape(LAYERS, n, dtype=F32) for n in (256, 256, 256, 768, 1024)]
        specs += [VM] * 5
        scratch += [pltpu.VMEM((16, W), F32)]
    return call(
        functools.partial(assemble, layer=0 if earlier else 1), [place] + halves + earlier,
        [SM] + [VM] * 8 + [ANY] * len(earlier), outs, out_specs=specs,
        scratch=scratch + [pltpu.SemaphoreType.DMA((4,))],
        aliases={9 + i: i for i in range(len(earlier))},
    )


def gather_tokens(own):
    far = move(own, flip_z=1)
    near = move(own, flip_core=1)
    return [own, near, far, move(far, flip_core=1)]


def body(
    inputs,
    lengths,
    gains,
    shifts,
    triple,
    triple_bias,
    merger,
    merger_bias,
    expander,
    expander_bias,
    shrinker,
    shrinker_bias,
    cotangent,
):
    rep = lax.axis_index("rep")
    shard = lax.axis_index("shard")
    length = lengths[0]
    x, y = rep // 8, rep % 4
    place = [x, y, shard, length, (x & 1) ^ (x >> 1), x >> 1, (y & 1) ^ (y >> 1), y >> 1]
    place = jnp.stack(place).astype(jnp.int32)

    small, *pieces = call(
        cut_triple,
        [place, gains, shifts, merger_bias, shrinker_bias, triple_bias, triple],
        [SM] + [VM] * 5 + [ANY],
        [shape(16, 768), shape(272, 768)] + [shape(144, 768), shape(128, 768)] * 2,
        scratch=[pltpu.VMEM((256, 3072), BF), pltpu.SemaphoreType.DMA((1,))],
    )

    x_blocks = gather_tokens(after(inputs, small))

    def halves(cut):
        return [
            move(cut[0], flip_core=1),
            move(cut[1], flip_z=1),
            move(cut[2], flip_z=3),
            move(cut[3], flip_z=1, flip_core=1),
            move(cut[4], flip_z=3, flip_core=1),
        ]

    t_pieces = halves(pieces)
    cut = call(
        cut_rest, [after(place, pieces[0], x_blocks[3]), triple, expander], [SM, ANY, ANY],
        [shape(256, W)] + [shape(128, W)] * 4 + [shape(256, WIDE)] * 3,
        scratch=[
            pltpu.VMEM((256, 3072), BF), pltpu.VMEM((256, 4096), BF), pltpu.VMEM((256, 4096), BF),
            pltpu.SemaphoreType.DMA((3,)),
        ],
    )
    e_pieces = halves(after(tuple(cut[:5]), t_pieces[2], t_pieces[4]))

    spot = after(jnp.arange(512, dtype=jnp.int32), x_blocks[1])
    spot = (((spot >> 7) ^ shard) << 7) | (spot & 127)
    index = jnp.arange(ROT // 2, dtype=F32)
    freq = jnp.exp(index * (-2.0 * math.log(10000.0) / ROT))
    lane = jnp.arange(256, dtype=jnp.int32) % HD
    phase = spot.astype(F32)[:, None] * jnp.tile(freq, 16)[None, :]
    cosine, sine = jnp.cos(phase), jnp.sin(phase)
    turn = jnp.stack(
        [
            jnp.where(lane < ROT, cosine, 1.0),
            jnp.where(lane < ROT // 2, -sine, 0.0),
            jnp.where((lane >= ROT // 2) & (lane < ROT), sine, 0.0),
        ]
    )

    full = shape(512, W)
    send, keep = shape(256, W), shape(256, W, dtype=F32)
    wide = pltpu.VMEM((W, WIDE), BF)
    merge, shrink = pltpu.VMEM((256, W), BF), pltpu.VMEM((W, W), BF)

    normed0, qkv0, mixed0, a_send, a_keep, vec = call(
        first_attention,
        [place] + x_blocks + [small, expander_bias, turn, triple, merger] + t_pieces,
        [SM] + [VM] * 4 + [ANY, VM, VM] + [ANY] * 7,
        [full, shape(512, 768), shape(512, 256), send, keep, shape(16, W, dtype=F32)],
        scratch=[wide, merge, pltpu.VMEM((4, 16, 768), BF), pltpu.SemaphoreType.DMA((13,))],
        flops=2 * 10**9,
    )
    a_got = move(a_send, flip_core=1)
    rest = after(tuple(cut[5:]), a_send)
    w_pieces = [
        move(rest[0], flip_core=1),
        move(rest[1], flip_z=3),
        move(rest[2], flip_z=3, flip_core=1),
    ]
    before0, f_send, f_keep = call(
        first_forward,
        [place, normed0, vec, expander, shrinker] + e_pieces,
        [SM, VM, VM] + [ANY] * 7,
        [shape(512, W, dtype=F32), send, keep],
        scratch=[wide, shrink, pltpu.VMEM((512, W), BF), pltpu.SemaphoreType.DMA((7,))],
        flops=2 * 10**9,
    )
    f_got = move(f_send, flip_core=1)
    up_blocks = gather_tokens(after(cotangent, f_send))

    def other(kept, got):
        return move((kept[128:] + got[128:].astype(F32)).astype(BF), flip_z=1)

    sums = [a_keep, a_got, other(a_keep, a_got), f_keep, f_got, other(f_keep, f_got)]
    block = [shape(128, W, dtype=F32), shape(128, W), shape(8, 128, dtype=F32)]
    state1, normed1, squares0 = call(
        functools.partial(join, layer=0), [place, inputs] + sums + [vec], [SM] + [VM] * 8, block
    )
    n_blocks = gather_tokens(normed1)

    normed1, up1, act1, ss1, mixed1, b_send, b_keep, send1, keep1, bias1 = call(
        last_layer,
        [place] + n_blocks + up_blocks + [vec, turn, triple, merger, expander, shrinker] + w_pieces,
        [SM] + [VM] * 10 + [ANY] * 7,
        [full, full, full, shape(512, WIDE), shape(512, 256), full, shape(512, W, dtype=F32)]
        + [send, keep, shape(8, WIDE, dtype=F32)],
        scratch=[
            wide, merge, shrink, pltpu.VMEM((512, 768), BF), pltpu.VMEM((512, 768), F32),
            pltpu.VMEM((512, 256), BF), pltpu.VMEM((512, W), F32), pltpu.SemaphoreType.DMA((9,)),
        ],
        flops=8 * 10**9,
    )
    got1 = move(send1, flip_core=1)
    s0, k0, s2, k2 = weight_one(place, act1, up1, normed1, ss1)
    low1 = (keep1[128:] + after(got1, s0)[128:].astype(F32)).astype(BF)
    far1 = move(low1, flip_z=1)
    s1, k1, s3, k3 = weight_two(after(place, low1), act1, up1, normed1, ss1, mixed1)
    g0, g2 = hops(after((s0, s2), low1), (0, 2), 0)
    slope1, low1, rows1 = call(
        functools.partial(norm_back, layer=1),
        [after(place, s1), state1, cotangent, cotangent, keep1, got1, far1, vec],
        [SM] + [VM] * 7,
        [shape(128, W, dtype=F32), shape(128, W), shape(8, W, dtype=F32)],
    )
    u_blocks = gather_tokens(low1)
    g1, g3 = hops(after((s1, s3), low1), (1, 3), 0)
    s0, k0, s2, k2 = first_folds(after(place, low1), (k0, k2), (g0, g2), (0, 2))
    one1 = [k0, k2] + hops([s0, s2], (0, 2), 1)

    up0, act0, ss0, send0, keep0, bias0 = call(
        first_back,
        [place] + u_blocks + [before0, qkv0, turn, triple, merger, expander, shrinker]
        + t_pieces + e_pieces,
        [SM] + [VM] * 7 + [ANY] * 14,
        [full, full, shape(512, WIDE), send, keep, shape(8, WIDE, dtype=F32)],
        scratch=[
            wide, merge, shrink, pltpu.VMEM((512, 768), F32), pltpu.VMEM((512, 256), BF),
            pltpu.SemaphoreType.DMA((16,)),
        ],
        flops=5 * 10**9,
    )
    got0 = move(send0, flip_core=1)
    s0, k0, s2, k2 = weight_one(place, act0, up0, normed0, ss0)
    f1, h1, f3, h3 = first_folds(after(place, s0), (k1, k3), (g1, g3), (1, 3))
    g0, g2 = hops((s0, s2), (0, 2), 0)
    s1, k1, s3, k3 = weight_two(after(place, f1), act0, up0, normed0, ss0, mixed0)
    two1 = [h1, h3] + hops([f1, f3], (1, 3), 1)
    g1, g3 = hops((s1, s3), (1, 3), 0)
    far0 = other(keep0, got0)
    s0, k0, s2, k2 = first_folds(place, (k0, k2), (g0, g2), (0, 2))
    one0 = [k0, k2] + hops([s0, s2], (0, 2), 1)
    units1 = fold_middle(after(place, s0), one1, two1)
    s1, k1, s3, k3 = first_folds(place, (k1, k3), (g1, g3), (1, 3))
    two0 = [k1, k3] + hops([s1, s3], (1, 3), 1)
    units1 = fold_last(after(place, s1), units1)
    units0 = fold_middle(place, one0, two0)
    terms1 = send_z(after(place, units0[0]), units1, [])
    units0 = fold_last(place, units0)
    pieces1 = sum_z(after(place, units0[0]), terms1)
    input_grad, _, rows0 = call(
        functools.partial(norm_back, layer=0),
        [place, inputs, slope1, low1, keep0, got0, far0, vec],
        [SM] + [VM] * 7,
        [shape(128, W, dtype=F32), shape(128, W), shape(8, W, dtype=F32)],
    )
    (vector,) = call(
        vectors_out, [place, rows0, bias0, rows1, bias1], [SM] + [VM] * 4,
        [shape(32, 512, dtype=F32)], scratch=[pltpu.VMEM((16, W), F32)],
    )
    every1 = collect_last(after(place, units0[0]), pieces1)
    terms0 = send_z(place, units0, [vector])
    pieces0 = sum_z(place, terms0)
    line0 = line_unit(place, pieces0)
    line0 = line_four(place, line0)
    line0 = line_three(place, line0)
    line0 = line_two(place, line0)
    sums1 = put_last(after(every1, line0[0]))
    *sums0, g_sum, s_sum, b_sum, t_sum, e_sum = put_sums(place, line0, list(sums1))
    b_got = move(after(b_send, units0[0]), flip_core=1)
    b_low = (
        b_keep.reshape(2, 256, W)[:, 128:] + b_got.reshape(2, 256, W)[:, 128:].astype(F32)
    ).astype(BF)
    b_far = move(b_low.reshape(256, W), flip_z=1)
    hidden_out, squares1 = call(
        functools.partial(join, layer=1),
        [place, state1, b_keep, b_got, b_far, vec],
        [SM] + [VM] * 5,
        [shape(128, W), shape(8, 128, dtype=F32)],
    )

    totals = jnp.concatenate([squares0[:3, :1], squares1[:3, :1]]).reshape(1, 6)
    totals = totals + move(totals, flip_core=1)
    totals = totals + move(totals, flip_z=1)
    rms_stats = jnp.sqrt(totals / (length.astype(F32) * W) + 1e-06)

    return (
        hidden_out,
        input_grad,
        g_sum,
        s_sum,
        sums0[0],
        t_sum,
        sums0[1],
        b_sum,
        sums0[2],
        e_sum,
        sums0[3],
        b_sum,
        rms_stats,
    )


def solution(mesh):
    return jax.shard_map(
        body,
        mesh=mesh,
        in_specs=(
            P(("rep", "shard"), None),
            P("rep"),
            P(None, "shard"),
            P(None, "shard"),
            P(None, "shard", None),
            P(None, "shard"),
            P(None, "shard", None),
            P(None, "shard"),
            P(None, "shard", None),
            P(None, "shard"),
            P(None, "shard", None),
            P(None, "shard"),
            P(("rep", "shard"), None),
        ),
        out_specs=(
            P(("rep", "shard"), None),
            P(("rep", "shard"), None),
            P(None, "shard"),
            P(None, "shard"),
            P(None, "shard", None),
            P(None, "shard"),
            P(None, "shard", None),
            P(None, "shard"),
            P(None, "shard", None),
            P(None, "shard"),
            P(None, "shard", None),
            P(None, "shard"),
            P("rep", None),
        ),
        check_vma=False,
    )
```

```python
import functools
import math

import jax
import jax.numpy as jnp
from jax import lax
from jax.experimental import pallas as pl
from jax.experimental.pallas import tpu as pltpu
from jax.sharding import PartitionSpec as P

HD = 64
ROT = 32
LAYERS = 2
EPS_NORM = 1e-05
AXES = ("rep", "shard")
BF = jnp.bfloat16
F32 = jnp.float32
MINE = 4
W = 1024
WIDE = 1792
PART = 768
PAIR = 1536
ORDERS = ((0, 2, 1, 3), (2, 0, 1, 3), (1, 3, 2, 0), (3, 1, 2, 0))

VM = pl.BlockSpec(memory_space=pltpu.VMEM)
ANY = pl.BlockSpec(memory_space=pl.ANY)
SM = pl.BlockSpec(memory_space=pltpu.SMEM)


def place_of(index):
    rep, shard = divmod(index, 4)
    x, rest = divmod(rep, 8)
    z_hi, y = divmod(rest, 4)
    z_lo, core = divmod(shard, 2)
    return x, y, z_hi * 2 + z_lo, core


def index_of(x, y, z, core):
    return ((x * 2 + z // 2) * 4 + y) * 4 + (z % 2) * 2 + core


def move(value, flip_x=0, flip_y=0, flip_z=0, flip_core=0):
    pairs = []
    for index in range(128):
        x, y, z, core = place_of(index)
        pairs.append((index, index_of(x ^ flip_x, y ^ flip_y, z ^ flip_z, core ^ flip_core)))
    return lax.ppermute(value, AXES, pairs)


def hop(value, link):
    by = 3 if link & 1 else 1
    return move(value, flip_y=by) if link > 1 else move(value, flip_x=by)


def link_bit(place, link):
    return place[4 + link]


def after(value, *others):
    return lax.optimization_barrier((value,) + others)[0]


def pick(value, index, axis=0):
    return lax.dynamic_index_in_dim(value, index, axis, keepdims=False)


def shape(*dims, dtype=BF):
    return jax.ShapeDtypeStruct(dims, dtype)


def call(body, args, specs, outs, out_specs=None, scratch=(), flops=0, aliases=None, room=4):
    held = sum(math.prod(o.shape) * o.dtype.itemsize for o in outs)
    held += sum(math.prod(a.shape) * a.dtype.itemsize for a, s in zip(args, specs) if s is VM)
    held += sum(math.prod(s.shape) * s.dtype.itemsize for s in scratch if jnp.issubdtype(s.dtype, jnp.floating))
    room = held + (room << 20)
    return pl.pallas_call(
        body,
        out_shape=outs,
        in_specs=specs,
        out_specs=out_specs or [VM] * len(outs),
        scratch_shapes=scratch,
        input_output_aliases=aliases or {},
        compiler_params=pltpu.CompilerParams(vmem_limit_bytes=room),
        cost_estimate=pl.CostEstimate(flops=1, bytes_accessed=1, transcendentals=0),
    )(*args)


def dot(left, right):
    return jnp.dot(left, right, preferred_element_type=F32)


def dot_t(left, right):
    return lax.dot_general(left, right, (((1,), (1,)), ((), ())), preferred_element_type=F32)


def t_dot(left, right):
    return lax.dot_general(left, right, (((0,), (0,)), ((), ())), preferred_element_type=F32)


def copies(pairs, sems):
    started = []
    for at, (source, target) in enumerate(pairs):
        copy = pltpu.make_async_copy(source, target, sems.at[at])
        copy.start()
        started.append(copy)
    return started


def finish(started):
    for copy in started:
        copy.wait()


def lanes(start, size):
    return pl.ds(pl.multiple_of(start, 128), size)


def rows_at(start, size):
    return pl.ds(pl.multiple_of(start, 16), size)


def cut_triple(
    place, gains, shifts, merger_bias, shrinker_bias, triple_bias, triple,
    small, out1, out2, out3, slab, sems,
):
    shard = place[2]
    started = copies([(triple.at[0], slab)], sems)
    narrow = [v[...].astype(F32) for v in (gains, shifts, merger_bias, shrinker_bias)]
    narrow = jnp.concatenate(narrow + [jnp.zeros((8, 256), F32)], axis=0)
    tall = jnp.concatenate(
        [jnp.zeros((8, 768), F32), triple_bias[...].astype(F32), jnp.zeros((6, 768), F32)], axis=0
    )
    both = jnp.concatenate([narrow, jnp.zeros((16, 512), F32)], axis=1) + tall
    small[...] = both.astype(BF)
    for ref in (out1, out2, out3):
        ref[pl.ds(256, 16), :] = both.astype(BF)
    finish(started)
    for k, ref in ((2, out2), (3, out3), (1, out1)):
        for p in range(3):
            ref[pl.ds(0, 256), pl.ds(p * 256, 256)] = slab[:, lanes(p * W + (shard ^ k) * 256, 256)]


def cut_rest(place, triple, expander, e1, e2, e3, w1, wz, slab, first, second, sems):
    shard = place[2]
    pairs = [(expander.at[0], first), (expander.at[1], second), (triple.at[1], slab)]
    started = copies(pairs, sems)
    started[0].wait()
    for k, ref in ((2, e2), (3, e3), (1, e1)):
        ref[...] = first[:, lanes((shard ^ k) * W, W)]
    finish(started[1:])
    for k, ref in ((2, wz.at[pl.ds(0, 256)]), (3, wz.at[pl.ds(256, 256)]), (1, w1)):
        block = shard ^ k
        ref[:, pl.ds(0, W)] = second[:, lanes(block * W, W)]
        for p in range(3):
            ref[:, pl.ds(W + p * 256, 256)] = slab[:, lanes(p * W + block * 256, 256)]


def own_triple(shard, layer, triple, wide):
    return [
        (
            triple.at[layer, :, lanes(p * W + shard * 256, 256)],
            wide.at[rows_at(shard * 256, 256), pl.ds(W + p * 256, 256)],
        )
        for p in range(3)
    ]


def own_expander(shard, layer, expander, wide):
    return [
        (expander.at[layer, :, lanes(shard * W, W)], wide.at[rows_at(shard * 256, 256), pl.ds(0, W)])
    ]


def piece_rows(shard, k, wide):
    return wide.at[rows_at((shard ^ k) * 256, 256)]


def first_triple(shard, pieces, wide):
    return [
        (ref.at[pl.ds(0, 256)], piece_rows(shard, k, wide).at[:, pl.ds(W, 768)])
        for k, ref in zip((1, 2, 3), pieces)
    ]


def first_expander(shard, pieces, wide):
    return [
        (ref, piece_rows(shard, k, wide).at[:, pl.ds(0, W)]) for k, ref in zip((1, 2, 3), pieces)
    ]


def second_wide(shard, pieces, wide):
    one, two, three = pieces
    return [
        (one, piece_rows(shard, 1, wide)),
        (two.at[pl.ds(0, 256)], piece_rows(shard, 2, wide)),
        (three, piece_rows(shard, 3, wide)),
    ]


def spots(shard):
    row = lax.broadcasted_iota(jnp.int32, (512, 1), 0)
    col = lax.broadcasted_iota(jnp.int32, (1, 512), 1)

    def at(i):
        return (((i >> 7) ^ shard) << 7) | (i & 127)

    return at(row), at(col)


def rotate(values, turn, back=False):
    ahead = pltpu.roll(values, 256 - 16, 1) * turn[1]
    behind = pltpu.roll(values, 16, 1) * turn[2]
    if back:
        return values * turn[0] - ahead - behind
    return values * turn[0] + ahead + behind


def normalize(state):
    mean = jnp.mean(state, axis=-1, keepdims=True)
    centred = state - mean
    spread = jnp.mean(centred * centred, axis=-1, keepdims=True)
    factor = lax.rsqrt(spread + EPS_NORM)
    return centred * factor, factor


ROOT = math.sqrt(2.0 / math.pi)


def gelu_both(v):
    square = v * v
    t = jnp.tanh(ROOT * v * (1.0 + 0.044715 * square))
    half = 0.5 * (1.0 + t)
    slope = half + 0.5 * v * (1.0 - t * t) * (ROOT + (3.0 * 0.044715 * ROOT) * square)
    return v * half, slope


def heads_out(normed, wide, bias, turn, qkv):
    scale = HD ** (-0.5)
    for p in range(3):
        part = dot(normed[...], wide[:, pl.ds(W + p * 256, 256)]) + bias[:, pl.ds(p * 256, 256)]
        if p < 2:
            part = rotate(part, turn)
        if p == 0:
            part = part * scale
        qkv[:, pl.ds(p * 256, 256)] = part.astype(BF)


def probabilities(qkv, h, allowed):
    q = qkv[:, pl.ds(h * HD, HD)]
    k = qkv[:, pl.ds(256 + h * HD, HD)]
    scores = jnp.where(allowed, dot_t(q, k), -1000000000.0)
    powered = jnp.exp(scores - jnp.max(scores, axis=-1, keepdims=True))
    return powered * (1.0 / jnp.sum(powered, axis=-1, keepdims=True))


def attend(qkv, allowed, mixed):
    for h in range(MINE):
        low = probabilities(qkv, h, allowed).astype(BF)
        mixed[:, pl.ds(h * HD, HD)] = dot(low, qkv[:, pl.ds(512 + h * HD, HD)]).astype(BF)


def attend_back(qkv, allowed, mixed, slope_mixed, slopes, forward):
    for h in range(MINE):
        probs = probabilities(qkv, h, allowed)
        low = probs.astype(BF)
        q = qkv[:, pl.ds(h * HD, HD)]
        k = qkv[:, pl.ds(256 + h * HD, HD)]
        v = qkv[:, pl.ds(512 + h * HD, HD)]
        if forward:
            mixed[:, pl.ds(h * HD, HD)] = dot(low, v).astype(BF)
        out = slope_mixed[:, pl.ds(h * HD, HD)]
        slope_probs = dot_t(out, v)
        centre = jnp.sum(probs * slope_probs, axis=-1, keepdims=True)
        slope_scores = (probs * (slope_probs - centre)).astype(BF)
        slopes[:, pl.ds(h * HD, HD)] = dot(slope_scores, k)
        slopes[:, pl.ds(256 + h * HD, HD)] = t_dot(slope_scores, q)
        slopes[:, pl.ds(512 + h * HD, HD)] = t_dot(low, out)


def hand_out(left, right, send, keep):
    for n in range(4):
        cols = pl.ds(n * 256, 256)
        part = dot(left[...], right[:, cols])
        spread_out(part, cols, send, keep)


def spread_out(part, cols, send, keep):
    keep[pl.ds(0, 128), cols] = part[0:128]
    send[pl.ds(0, 128), cols] = part[128:256].astype(BF)
    keep[pl.ds(128, 128), cols] = part[256:384]
    send[pl.ds(128, 128), cols] = part[384:512].astype(BF)


def first_attention(
    place, x0, x1, x2, x3, small, bias, turn, triple, merger, t1, t2, t3,
    normed, qkv, mixed, send, keep, vec, wide, merge, smalls, sems,
):
    shard, length = place[2], place[3]
    pairs = [(small, smalls.at[shard])]
    pairs += [(t1.at[pl.ds(256, 16)], smalls.at[shard ^ 1])]
    pairs += [(t2.at[pl.ds(256, 16)], smalls.at[shard ^ 2])]
    pairs += [(t3.at[pl.ds(256, 16)], smalls.at[shard ^ 3])]
    pairs += own_triple(shard, 0, triple, wide) + [(merger.at[0], merge)]
    started = copies(pairs + first_triple(shard, (t1, t2, t3), wide), sems)
    for copy in started[:4]:
        copy.wait()
    vec[...] = jnp.zeros_like(vec)
    for j in range(4):
        vec[pl.ds(0, 8), pl.ds(j * 256, 256)] = smalls[j].astype(F32)[0:8, 0:256]
    for p in range(3):
        block = p * 4 + shard
        j = (block * 11) >> 5
        vec[pl.ds(8, 2), pl.ds(p * 256, 256)] = smalls[j, :, lanes((block - 3 * j) * 256, 256)].astype(
            F32
        )[8:10]
    vec[pl.ds(10, 2), :] = bias[...].astype(F32)
    gain, shift = vec[pl.ds(0, 1), :], vec[pl.ds(2, 1), :]
    for k, ref in enumerate((x0, x1, x2, x3)):
        hat, _ = normalize(ref[...].astype(F32))
        normed[pl.ds(k * 128, 128), :] = (hat * gain + shift).astype(BF)
    finish(started[4:])
    row, col = spots(shard)
    allowed = (col <= row) & (col < length)
    heads_out(normed, wide, vec[pl.ds(8, 1), pl.ds(0, 768)], turn, qkv)
    attend(qkv, allowed, mixed)
    hand_out(mixed, merge, send, keep)


def first_forward(
    place, normed, vec, expander, shrinker, e1, e2, e3,
    before, send, keep, wide, shrink, act, sems,
):
    shard = place[2]
    pairs = own_expander(shard, 0, expander, wide) + first_expander(shard, (e1, e2, e3), wide)
    started = copies(pairs + [(shrinker.at[0], shrink)], sems)
    finish(started)
    for n in range(4):
        cols = pl.ds(n * 256, 256)
        part = dot(normed[...], wide[:, cols]) + vec[pl.ds(10, 1), cols]
        before[:, cols] = part
        act[:, cols] = gelu_both(part)[0].astype(BF)
    hand_out(act, shrink, send, keep)


def slopes_out(ss, bias, wide, send, keep):
    bias[...] = jnp.broadcast_to(jnp.sum(ss[...].astype(F32), axis=0, keepdims=True), bias.shape)
    for n in range(4):
        part = dot_t(ss[...], wide[pl.ds(n * 256, 256), :])
        spread_out(part, pl.ds(n * 256, 256), send, keep)


def triple_slopes(slopes, turn, ss):
    scale = HD ** (-0.5)
    ss[:, pl.ds(W, 256)] = (rotate(slopes[:, pl.ds(0, 256)], turn, True) * scale).astype(BF)
    ss[:, pl.ds(W + 256, 256)] = rotate(slopes[:, pl.ds(256, 256)], turn, True).astype(BF)
    ss[:, pl.ds(W + 512, 256)] = slopes[:, pl.ds(512, 256)].astype(BF)


def last_layer(
    place, n0, n1, n2, n3, u0, u1, u2, u3, vec, turn, triple, merger, expander, shrinker, w1, w2, w3,
    normed, up, act, ss, mixed, bsend, bkeep, send, keep, bias,
    wide, merge, shrink, qkv, slopes, out, before, sems,
):
    shard, length = place[2], place[3]
    pairs = own_triple(shard, 1, triple, wide) + own_expander(shard, 1, expander, wide)
    pairs += second_wide(shard, (w1, w2, w3), wide) + [(merger.at[1], merge), (shrinker.at[1], shrink)]
    started = copies(pairs, sems)
    row, col = spots(shard)
    for k, (n, u) in enumerate(((n0, u0), (n1, u1), (n2, u2), (n3, u3))):
        rows = pl.ds(k * 128, 128)
        normed[rows, :] = n[...]
        up[rows, :] = jnp.where(row[k * 128 : k * 128 + 128] < length, u[...].astype(F32), 0.0).astype(BF)
    finish(started)
    for n in range(4):
        cols = pl.ds(n * 256, 256)
        part = dot(normed[...], wide[:, cols]) + vec[pl.ds(11, 1), cols]
        value, slope = gelu_both(part)
        act[:, cols] = value.astype(BF)
        ss[:, cols] = (dot_t(up[...], shrink[cols, :]) * slope).astype(BF)
    hand_out(act, shrink, bsend.at[pl.ds(256, 256)], bkeep.at[pl.ds(256, 256)])
    allowed = (col <= row) & (col < length)
    heads_out(normed, wide, vec[pl.ds(9, 1), pl.ds(0, 768)], turn, qkv)
    out[...] = dot_t(up[...], merge[...]).astype(BF)
    attend_back(qkv, allowed, mixed, out, slopes, True)
    hand_out(mixed, merge, bsend.at[pl.ds(0, 256)], bkeep.at[pl.ds(0, 256)])
    triple_slopes(slopes, turn, ss)
    slopes_out(ss, bias, wide, send, keep)


def first_back(
    place, u0, u1, u2, u3, before, qkv, turn, triple, merger, expander, shrinker,
    t1, t2, t3, e1, e2, e3,
    up, act, ss, send, keep, bias, wide, merge, shrink, slopes, out, sems,
):
    shard, length = place[2], place[3]
    pairs = own_triple(shard, 0, triple, wide) + own_expander(shard, 0, expander, wide)
    pairs += first_triple(shard, (t1, t2, t3), wide)
    pairs += first_expander(shard, (e1, e2, e3), wide)
    started = copies(pairs + [(merger.at[0], merge), (shrinker.at[0], shrink)], sems)
    for k, u in enumerate((u0, u1, u2, u3)):
        up[pl.ds(k * 128, 128), :] = u[...]
    finish(started)
    for n in range(4):
        cols = pl.ds(n * 256, 256)
        value, slope = gelu_both(before[:, cols])
        act[:, cols] = value.astype(BF)
        ss[:, cols] = (dot_t(up[...], shrink[cols, :]) * slope).astype(BF)
    row, col = spots(shard)
    allowed = (col <= row) & (col < length)
    out[...] = dot_t(up[...], merge[...]).astype(BF)
    attend_back(qkv, allowed, None, out, slopes, False)
    triple_slopes(slopes, turn, ss)
    slopes_out(ss, bias, wide, send, keep)


def halve(term, cols, o, bit, send, keep, at):
    for ref, half in ((keep, bit), (send, 1 - bit)):
        value = term[pl.ds(pl.multiple_of(half * 128, 128), 128), cols].astype(BF)
        for k in range(8):
            ref[pl.ds(k * 64 + o * 16, 16), at] = value[k * 16 : k * 16 + 16]


def terms_one(place, act, up, normed, ss, s0, k0, s2, k2, term):
    whole = pl.ds(0, PART)
    for o in range(4):
        cols = pl.ds(o * 256, 256)
        term[...] = t_dot(act[:, cols], up[:, pl.ds(0, PART)])
        halve(term, whole, o, link_bit(place, ORDERS[0][0]), s0, k0, whole)
        term[...] = t_dot(normed[:, cols], ss[:, pl.ds(0, PART)])
        halve(term, whole, o, link_bit(place, ORDERS[2][0]), s2, k2, whole)


def terms_two(place, act, up, normed, ss, mixed, s1, k1, s3, k3, term, last):
    one, three = link_bit(place, ORDERS[1][0]), link_bit(place, ORDERS[3][0])
    whole = pl.ds(0, PART)
    last[...] = t_dot(mixed[...], up[...])
    for o in range(4):
        cols = pl.ds(o * 256, 256)
        term[:, pl.ds(0, 256)] = t_dot(act[:, cols], up[:, pl.ds(PART, 256)])
        term[:, pl.ds(256, 256)] = last[:, cols]
        both = t_dot(normed[:, cols], ss[:, pl.ds(PART, W)])
        term[:, pl.ds(512, 256)] = both[:, 256:512]
        halve(term, whole, o, one, s1, k1, whole)
        term[:, pl.ds(0, 256)] = both[:, 0:256]
        term[:, pl.ds(256, 512)] = both[:, 512:W]
        halve(term, whole, o, three, s3, k3, whole)


def weight_one(place, act, up, normed, ss):
    return call(
        terms_one, [place, act, up, normed, ss], [SM] + [VM] * 4, [shape(512, PART)] * 4,
        scratch=[pltpu.VMEM((256, PART), F32)], flops=2 * 10**9,
    )


def weight_two(place, act, up, normed, ss, mixed):
    return call(
        terms_two, [place, act, up, normed, ss, mixed], [SM] + [VM] * 5, [shape(512, PART)] * 4,
        scratch=[pltpu.VMEM((256, PART), F32), pltpu.VMEM((256, W), F32)], flops=2 * 10**9,
    )


def join(place, state, *refs, layer):
    shard, length = place[2], place[3]
    spot = shard * 128 + lax.broadcasted_iota(jnp.int32, (128, 1), 0)
    valid = (spot < length).astype(F32)
    if layer == 0:
        ak, ag, az, fk, fg, fz, vec, new, out, squares = refs
        attended = ak[pl.ds(0, 128), :] + ag[pl.ds(0, 128), :].astype(F32) + az[...].astype(F32)
        branch = fk[pl.ds(0, 128), :] + fg[pl.ds(0, 128), :].astype(F32) + fz[...].astype(F32)
    else:
        kept, got, far, vec, out, squares = refs
        attended, branch = [
            kept[pl.ds(at * 256, 128), :]
            + got[pl.ds(at * 256, 128), :].astype(F32)
            + far[pl.ds(at * 128, 128), :].astype(F32)
            for at in (0, 1)
        ]
    attended = attended + vec[pl.ds(4 + layer, 1), :]
    branch = branch + vec[pl.ds(6 + layer, 1), :]
    old = state[...].astype(F32)
    for at, item in enumerate((old, attended, branch)):
        total = jnp.sum(jnp.sum(item * item, axis=1, keepdims=True) * valid)
        squares[pl.ds(at, 1), :] = jnp.full((1, 128), total, F32)
    state_new = old + attended + branch
    if layer == 0:
        new[...] = state_new
        hat, _ = normalize(state_new)
        out[...] = (hat * vec[pl.ds(1, 1), :] + vec[pl.ds(3, 1), :]).astype(BF)
    else:
        out[...] = (state_new * valid).astype(BF)


def norm_back(place, state, slope, up, sk, sg, sz, vec, new, low, rows, *, layer):
    shard, length = place[2], place[3]
    spot = shard * 128 + lax.broadcasted_iota(jnp.int32, (128, 1), 0)
    given = slope[...].astype(F32)
    upstream = up[...].astype(F32)
    if layer == LAYERS - 1:
        given = jnp.where(spot < length, given, 0.0)
        upstream = given
    sn = sk[pl.ds(0, 128), :] + sg[pl.ds(0, 128), :].astype(F32) + sz[...].astype(F32)
    hat, factor = normalize(state[...].astype(F32))
    rows[...] = jnp.zeros_like(rows)
    rows[pl.ds(0, 1), :] = jnp.sum(sn * hat, axis=0, keepdims=True)
    rows[pl.ds(1, 1), :] = jnp.sum(sn, axis=0, keepdims=True)
    rows[pl.ds(2, 1), :] = jnp.sum(upstream, axis=0, keepdims=True)
    d = sn * vec[pl.ds(layer, 1), :]
    mean = jnp.mean(d, axis=-1, keepdims=True)
    along = jnp.mean(d * hat, axis=-1, keepdims=True)
    result = given + factor * (d - mean - hat * along)
    new[...] = result
    low[...] = result.astype(BF)


def vectors_out(place, rows0, bias0, rows1, bias1, out, full):
    shard = place[2]
    full[...] = jnp.zeros_like(full)
    for at, (rows, bias) in enumerate(((rows0, bias0), (rows1, bias1))):
        base = at * 7
        full[pl.ds(base, 3), :] = rows[pl.ds(0, 3), :]
        for p in range(3):
            full[pl.ds(base + 3 + p, 1), lanes(shard * 256, 256)] = bias[
                pl.ds(0, 1), pl.ds(W + p * 256, 256)
            ]
        full[pl.ds(base + 6, 1), :] = bias[pl.ds(0, 1), pl.ds(0, W)]
    out[pl.ds(0, 16), :] = full[:, pl.ds(0, 512)]
    out[pl.ds(16, 16), :] = full[:, pl.ds(512, 512)]


def add_half(kept, got, bit, refs, at):
    size = kept.shape[0] // 2
    for ref, half in zip(refs, (1 - bit, bit)):
        rows = rows_at(half * size, size)
        total = kept[rows, :].astype(F32) + got[rows, :].astype(F32)
        ref[:, at] = total.astype(BF)


def fold_one(place, ka, ga, kb, gb, sa, ha, sb, hb, *, parts):
    for part, (k, g, s, h) in zip(parts, ((ka, ga, sa, ha), (kb, gb, sb, hb))):
        add_half(k, g, link_bit(place, ORDERS[part][1]), (s, h), slice(None))


def fold_two(place, k0, g0, k1, g1, k2, g2, k3, g3, sa, ha, sb, hb):
    for part, (k, g) in enumerate(((k0, g0), (k1, g1), (k2, g2), (k3, g3))):
        refs = (sb, hb) if part > 1 else (sa, ha)
        at = pl.ds((part & 1) * PART, PART)
        add_half(k, g, link_bit(place, ORDERS[part][2]), refs, at)


def fold_three(place, ka, ga, kb, gb, sa, ha, sb, hb):
    for part, (k, g, s, h) in zip((0, 2), ((ka, ga, sa, ha), (kb, gb, sb, hb))):
        add_half(k, g, link_bit(place, ORDERS[part][3]), (s, h), slice(None))


def first_folds(place, kept, got, parts):
    args = [kept[0], got[0], kept[1], got[1]]
    return call(
        functools.partial(fold_one, parts=parts), [place] + args, [SM] + [VM] * 4, [shape(256, PART)] * 4
    )


def z_send(place, *refs):
    ka, ga, kb, gb, *refs = refs
    shard = place[2]
    z_lo = shard >> 1
    if len(refs) == 6:
        vector, *refs = refs
    else:
        vector = None
    side, across, cross, plain, wide = refs
    a = ka[...].astype(F32) + ga[...].astype(F32)
    b = kb[...].astype(F32) + gb[...].astype(F32)
    wide[:, pl.ds(0, W)] = b[:, 0:W]
    wide[:, pl.ds(W, 256)] = a[:, 1280:PAIR]
    wide[:, pl.ds(1280, 512)] = b[:, W:PAIR]
    plain[...] = a[:, 0:1280]
    cross[...] = wide[rows_at(z_lo * 32, 32), :]
    side[:, pl.ds(0, WIDE)] = wide[rows_at((1 - z_lo) * 32, 32), :].astype(BF)
    across[:, pl.ds(0, WIDE)] = cross[...].astype(BF)
    across[:, pl.ds(WIDE, 1280)] = plain[pl.ds(0, 32), :].astype(BF)
    across[:, pl.ds(WIDE + 1280, 1280)] = plain[pl.ds(32, 32), :].astype(BF)
    if vector is not None:
        side[:, pl.ds(WIDE, 512)] = vector[...].astype(BF)
        across[:, pl.ds(WIDE + 2560, 512)] = vector[...].astype(BF)


def local_rows():
    row = lax.broadcasted_iota(jnp.int32, (32, 1), 0) & 15
    return (row == 6) | (row == 13)


def z_sum(place, *refs):
    cross, plain, za, zb, z2, *refs = refs
    vector = None
    if len(refs) == 6:
        vector, *refs = refs
        near, kept, whole, vec, both = refs
    else:
        near, kept, whole, both = refs
    core = place[2] & 1
    both[pl.ds(0, 32), :] = cross[...] + z2[:, pl.ds(0, WIDE)].astype(F32)
    both[pl.ds(32, 32), :] = za[:, pl.ds(0, WIDE)].astype(F32) + zb[:, pl.ds(0, WIDE)].astype(F32)
    for at in range(2):
        own = both[rows_at(at * 32 + core * 16, 16), :]
        other = both[rows_at(at * 32 + (1 - core) * 16, 16), :]
        kept[pl.ds(at * 16, 16), :] = own.astype(BF)
        near[pl.ds(at * 16, 16), pl.ds(0, WIDE)] = other.astype(BF)
    for at in range(2):
        rows = pl.ds(at * 32, 32)
        got = z2[:, pl.ds(WIDE + at * 1280, 1280)].astype(F32)
        whole[rows, :] = (plain[rows, :] + got).astype(BF)
    if vector is not None:
        sides = za[:, pl.ds(WIDE, 512)].astype(F32) + zb[:, pl.ds(WIDE, 512)].astype(F32)
        total = vector[...] + z2[:, pl.ds(WIDE + 2560, 512)].astype(F32)
        total = total + jnp.where(local_rows(), 0.0, sides)
        vec[...] = total
        near[:, pl.ds(WIDE, 512)] = total.astype(BF)


def payload_parts(place, kept, near, whole, a, b):
    shard = place[2]
    for k in range(4):
        rows = rows_at((shard ^ k) * 16, 16)
        ref, at = (near, k >> 1) if k & 1 else (kept, k >> 1)
        source = ref[pl.ds(at * 16, 16), pl.ds(0, WIDE)]
        b[rows, pl.ds(0, W)] = source[:, 0:W]
        a[rows, pl.ds(1280, 256)] = source[:, W:1280]
        b[rows, pl.ds(W, 512)] = source[:, 1280:WIDE]
    a[pl.ds(0, 64), pl.ds(0, 1280)] = whole[...]


def payload_both(place, kept, near, whole, out):
    payload_parts(place, kept, near, whole, out.at[pl.ds(0, 64)], out.at[pl.ds(64, 64)])


def payload(place, kept, near, whole, *refs):
    *vec, a, b = refs
    payload_parts(place, kept, near, whole, a, b)
    if not vec:
        return
    vec = vec[0]
    total = vec[...] + jnp.where(local_rows(), 0.0, near[:, pl.ds(WIDE, 512)].astype(F32))
    low = total.astype(BF)
    a[pl.ds(64, 16), :] = jnp.zeros((16, PAIR), BF)
    a[pl.ds(64, 16), pl.ds(0, 512)] = low[0:16]
    a[pl.ds(64, 16), pl.ds(512, 512)] = low[16:32]


def line_up(own, got, bit, size, outs, cols):
    for ref, at in zip(outs, cols):
        ref[rows_at(bit * size, size), :] = own[pl.ds(0, size), at]
        ref[rows_at((1 - bit) * size, size), :] = got[pl.ds(0, size), at]


def vector_rows(own, got, at, size):
    rows = pl.ds(at, size)
    return (own[rows, :].astype(F32) + got[rows, :].astype(F32)).astype(BF)


def gather_four(place, oa, ga, ob, gb, a, b):
    line_up(oa, ga, link_bit(place, ORDERS[0][3]), 64, [a], [slice(None)])
    line_up(ob, gb, link_bit(place, ORDERS[2][3]), 64, [b], [slice(None)])
    if a.shape[0] > 128:
        a[pl.ds(128, 16), :] = vector_rows(oa, ga, 64, 16)


def gather_three(place, oa, ga, ob, gb, p0, p1, p2, p3):
    cols = [pl.ds(0, PART), pl.ds(PART, PART)]
    line_up(oa, ga, link_bit(place, ORDERS[0][2]), 128, [p0, p1], cols)
    line_up(ob, gb, link_bit(place, ORDERS[2][2]), 128, [p2, p3], cols)
    if p0.shape[0] == 256:
        return
    low = vector_rows(oa, ga, 128, 16)
    p0[pl.ds(256, 32), :] = jnp.zeros((32, PART), BF)
    p0[pl.ds(256, 16), pl.ds(0, 512)] = low[:, 0:512]
    p0[pl.ds(272, 16), pl.ds(0, 512)] = low[:, 512:W]


def gather_two(place, o0, g0, o1, g1, o2, g2, o3, g3, p0, p1, p2, p3):
    outs = (p0, p1, p2, p3)
    for part, (o, g) in enumerate(((o0, g0), (o1, g1), (o2, g2), (o3, g3))):
        line_up(o, g, link_bit(place, ORDERS[part][1]), 256, [outs[part]], [slice(None)])
    p0[pl.ds(512, 32), :] = vector_rows(o0, g0, 256, 32)


def each(count, step):
    lax.fori_loop(0, count, lambda at, none: step(at) or none, 0)


def put(part, value, o, base, t, m, e, s):
    rows = rows_at(base, 16)
    if part == 0:
        s[rows_at(o * 256 + base, 16), pl.ds(0, PART)] = value
    elif part == 1:
        s[rows_at(o * 256 + base, 16), pl.ds(PART, 256)] = value[:, 0:256]
        m[rows, pl.ds(o * 256, 256)] = value[:, 256:512]
        t[rows, pl.ds(o * 256, 256)] = value[:, 512:PART]
    elif part == 2:
        e[rows, pl.ds(o * W, PART)] = value
    else:
        e[rows, pl.ds(o * W + PART, 256)] = value[:, 0:256]
        t[rows, pl.ds(W + o * 256, 256)] = value[:, 256:512]
        t[rows, pl.ds(2 * W + o * 256, 256)] = value[:, 512:PART]


def assemble_last(every, t_out, m_out, e_out, s_out, t, m, e, s, sems):
    def device(at):
        x, y = at >> 2, at & 3
        bits = ((x & 1) ^ (x >> 1), x >> 1, (y & 1) ^ (y >> 1), y >> 1)
        for part in range(4):
            unit = sum(bits[link] << (3 - n) for n, link in enumerate(ORDERS[part]))
            for o in range(4):
                rows = rows_at(at * 128 + (part >> 1) * 64 + o * 16, 16)
                value = every[rows, pl.ds((part & 1) * PART, PART)].astype(F32)
                put(part, value, o, unit * 16, t, m, e, s)

    each(16, device)
    pairs = [(t, t_out.at[1]), (m, m_out.at[1]), (e, e_out.at[1]), (s, s_out.at[1])]
    finish(copies(pairs, sems))


def put_half(place, p0, p1, p2, p3, *refs, mine):
    if not mine:
        old, *refs = refs
        t_out, m_out, e_out, s_out, *sums, s0, s1, m1, t1, e2, e3, t3, both, vec, sems = refs[4:]
    else:
        t_out, m_out, e_out, s_out, s0, s1, m1, t1, e2, e3, t3, sems = refs[4:]
    pairs = []
    for part, ref in enumerate((p0, p1, p2, p3)):
        half = link_bit(place, ORDERS[part][0])
        base = (half if mine else 1 - half) * 128
        rows = rows_at(base, 128)
        for o in range(4):
            for k in range(8):
                value = ref[pl.ds(k * 64 + o * 16, 16), :].astype(F32)
                at = pl.ds(k * 16, 16)
                if part == 0:
                    s0[o, at, :] = value
                elif part == 1:
                    s1[o, at, :] = value[:, 0:256]
                    m1[at, pl.ds(o * 256, 256)] = value[:, 256:512]
                    t1[at, pl.ds(o * 256, 256)] = value[:, 512:PART]
                elif part == 2:
                    e2[o, at, :] = value
                else:
                    e3[o, at, :] = value[:, 0:256]
                    t3[at, pl.ds(o * 256, 256)] = value[:, 256:512]
                    t3[at, pl.ds(W + o * 256, 256)] = value[:, 512:PART]
            if part < 2:
                target = s_out.at[0, rows_at(o * 256 + base, 128)]
                pairs.append((s0.at[o], target.at[:, pl.ds(0, PART)]) if part == 0 else (s1.at[o], target.at[:, pl.ds(PART, 256)]))
            else:
                target = e_out.at[0, rows]
                pairs.append((e2.at[o], target.at[:, pl.ds(o * W, PART)]) if part == 2 else (e3.at[o], target.at[:, pl.ds(o * W + PART, 256)]))
        if part == 1:
            pairs.append((m1, m_out.at[0, rows]))
            pairs.append((t1, t_out.at[0, rows, pl.ds(0, W)]))
        if part == 3:
            pairs.append((t3, t_out.at[0, rows, pl.ds(W, 2 * W)]))
    started = copies(pairs, sems)
    if not mine:
        fetch = copies([(old.at[pl.ds(512, 32)], both)], sems.at[pl.ds(len(pairs), 1)])
        finish(fetch)
        low = both[...].astype(F32) + p0[pl.ds(512, 32), :].astype(F32)
        vec[:, pl.ds(0, 512)] = low[0:16, 0:512]
        vec[:, pl.ds(512, 512)] = low[16:32, 0:512]
        for at in range(LAYERS):
            own_sums(vec, at, place[2], *sums)
    finish(started)


def own_sums(vec, layer, shard, g_sum, s_sum, b_sum, b_copy, t_sum, e_sum):
    base = layer * 7
    row = pl.ds(layer, 1)
    for at, ref in ((0, g_sum), (1, s_sum), (2, b_sum), (2, b_copy)):
        ref[row, :] = vec[pl.ds(base + at, 1), lanes(shard * 256, 256)]
    for r in range(3):
        block = shard * 3 + r
        t_sum[row, pl.ds(r * 256, 256)] = vec[
            pl.ds(base + 3 + (block >> 2), 1), lanes((block & 3) * 256, 256)
        ]
    e_sum[row, :] = vec[pl.ds(base + 6, 1), :]


def hops(values, parts, phase):
    return [hop(value, ORDERS[part][phase]) for value, part in zip(values, parts)]


def fold_middle(place, one, two):
    kept = [one[0], two[0], one[1], two[1]]
    got = [one[2], two[2], one[3], two[3]]
    args = [v for pair in zip(kept, got) for v in pair]
    sa, ka, sb, kb = call(fold_two, [place] + args, [SM] + [VM] * 8, [shape(128, PAIR)] * 4)
    ga, gb = hops([sa, sb], (0, 2), 2)
    return [ka, ga, kb, gb]


def fold_last(place, units):
    sa, ka, sb, kb = call(fold_three, [place] + units, [SM] + [VM] * 4, [shape(64, PAIR)] * 4)
    ga, gb = hops([sa, sb], (0, 2), 3)
    return [ka, ga, kb, gb]


def send_z(place, units, vector):
    more = 512 * len(vector)
    side, across, cross, plain = call(
        z_send, [place] + units + vector, [SM] + [VM] * (4 + len(vector)),
        [
            shape(32, WIDE + more), shape(32, WIDE + 2560 + more),
            shape(32, WIDE, dtype=F32), shape(64, 1280, dtype=F32),
        ],
        scratch=[pltpu.VMEM((64, WIDE), F32)],
    )
    z2 = move(across, flip_z=2)
    za = move(side, flip_z=1)
    zb = move(side, flip_z=3)
    return [cross, plain, za, zb, z2] + vector


def sum_z(place, terms):
    vectors = len(terms) - 5
    near, kept, whole, *vec = call(
        z_sum, [place] + terms, [SM] + [VM] * len(terms),
        [shape(32, WIDE + 512 * vectors), shape(32, WIDE), shape(64, 1280)]
        + [shape(32, 512, dtype=F32)] * vectors,
        scratch=[pltpu.VMEM((64, WIDE), F32)],
    )
    return [kept, move(near, flip_core=1), whole] + vec


OUTS = [
    shape(LAYERS, 256, 3072, dtype=F32),
    shape(LAYERS, 256, 1024, dtype=F32),
    shape(LAYERS, 256, 4096, dtype=F32),
    shape(LAYERS, 1024, 1024, dtype=F32),
]


def line_unit(place, pieces):
    rows = 80 if len(pieces) == 4 else 64
    a, b = call(
        payload, [place] + pieces, [SM] + [VM] * len(pieces), [shape(rows, PAIR), shape(64, PAIR)]
    )
    ga, gb = hops([a, b], (0, 2), 3)
    return [a, ga, b, gb]


def line_four(place, args):
    rows = args[0].shape[0] + 64
    a, b = call(gather_four, [place] + args, [SM] + [VM] * 4, [shape(rows, PAIR), shape(128, PAIR)])
    ga, gb = hops([a, b], (0, 2), 2)
    return [a, ga, b, gb]


def line_three(place, args):
    rows = 288 if args[0].shape[0] > 128 else 256
    own = call(
        gather_three, [place] + args, [SM] + [VM] * 4, [shape(rows, PART)] + [shape(256, PART)] * 3
    )
    got = hops(own, range(4), 1)
    return [v for pair in zip(own, got) for v in pair]


def line_two(place, args):
    own = call(
        gather_two, [place] + args, [SM] + [VM] * 8, [shape(544, PART)] + [shape(512, PART)] * 3
    )
    return list(own), hops(own, range(4), 0)


def collect_last(place, pieces):
    (both,) = call(payload_both, [place] + pieces, [SM] + [VM] * 3, [shape(128, PAIR)])
    planes = [[(x * 2 + z) * 4 + y for x in range(4) for y in range(4)] for z in range(2)]
    return lax.all_gather(both, "rep", axis_index_groups=planes, axis=0, tiled=True)


def put_last(every):
    return call(
        assemble_last, [every], [VM], OUTS, out_specs=[ANY] * 4,
        scratch=[pltpu.VMEM(out.shape[1:], F32) for out in OUTS] + [pltpu.SemaphoreType.DMA((4,))],
    )


def put_sums(place, parts, earlier, old):
    outs, specs = list(OUTS), [ANY] * 4
    scratch = [
        pltpu.VMEM((4, 128, PART), F32), pltpu.VMEM((4, 128, 256), F32), pltpu.VMEM((128, W), F32),
        pltpu.VMEM((128, W), F32), pltpu.VMEM((4, 128, PART), F32), pltpu.VMEM((4, 128, 256), F32),
        pltpu.VMEM((128, 2 * W), F32),
    ]
    if old:
        outs += [shape(LAYERS, n, dtype=F32) for n in (256, 256, 256, 256, 768, 1024)]
        specs += [VM] * 6
        scratch += [pltpu.VMEM((32, PART), BF), pltpu.VMEM((16, W), F32)]
    return call(
        functools.partial(put_half, mine=not old), [place] + parts + old + list(earlier),
        [SM] + [VM] * 4 + [ANY] * (4 + len(old)), outs, out_specs=specs,
        scratch=scratch + [pltpu.SemaphoreType.DMA((20,))],
        aliases={5 + len(old) + i: i for i in range(4)},
    )


def gather_tokens(own):
    far = move(own, flip_z=1)
    near = move(own, flip_core=1)
    return [own, near, far, move(far, flip_core=1)]


def gather_late(own):
    far = move(own, flip_z=1)
    return [own, move(after(own, far), flip_core=1), far, move(far, flip_core=1)]


def body(
    inputs,
    lengths,
    gains,
    shifts,
    triple,
    triple_bias,
    merger,
    merger_bias,
    expander,
    expander_bias,
    shrinker,
    shrinker_bias,
    cotangent,
):
    rep = lax.axis_index("rep")
    shard = lax.axis_index("shard")
    length = lengths[0]
    x, y = rep // 8, rep % 4
    place = [x, y, shard, length, (x & 1) ^ (x >> 1), x >> 1, (y & 1) ^ (y >> 1), y >> 1]
    place = jnp.stack(place).astype(jnp.int32)

    small, *pieces = call(
        cut_triple,
        [place, gains, shifts, merger_bias, shrinker_bias, triple_bias, triple],
        [SM] + [VM] * 5 + [ANY],
        [shape(16, 768)] + [shape(272, 768)] * 3,
        scratch=[pltpu.VMEM((256, 3072), BF), pltpu.SemaphoreType.DMA((1,))],
    )

    def recut(one, two, three):
        return [
            move(one, flip_core=1),
            move(two, flip_z=1),
            move(three, flip_z=3, flip_core=1),
        ]

    t_pieces = recut(*pieces)
    x_blocks = gather_tokens(after(inputs, small))
    cut = call(
        cut_rest, [after(place, pieces[0], x_blocks[1]), triple, expander], [SM, ANY, ANY],
        [shape(256, W)] * 3 + [shape(256, WIDE), shape(512, WIDE)],
        scratch=[
            pltpu.VMEM((256, 3072), BF), pltpu.VMEM((256, 4096), BF), pltpu.VMEM((256, 4096), BF),
            pltpu.SemaphoreType.DMA((3,)),
        ],
    )
    e_pieces = recut(*after(tuple(cut[:3]), x_blocks[2]))

    spot = after(jnp.arange(512, dtype=jnp.int32), x_blocks[1])
    spot = (((spot >> 7) ^ shard) << 7) | (spot & 127)
    index = jnp.arange(ROT // 2, dtype=F32)
    freq = jnp.exp(index * (-2.0 * math.log(10000.0) / ROT))
    lane = jnp.arange(256, dtype=jnp.int32) % HD
    phase = spot.astype(F32)[:, None] * jnp.tile(freq, 16)[None, :]
    cosine, sine = jnp.cos(phase), jnp.sin(phase)
    turn = jnp.stack(
        [
            jnp.where(lane < ROT, cosine, 1.0),
            jnp.where(lane < ROT // 2, -sine, 0.0),
            jnp.where((lane >= ROT // 2) & (lane < ROT), sine, 0.0),
        ]
    )

    full = shape(512, W)
    send, keep = shape(256, W), shape(256, W, dtype=F32)
    wide = pltpu.VMEM((W, WIDE), BF)
    merge, shrink = pltpu.VMEM((256, W), BF), pltpu.VMEM((W, W), BF)

    normed0, qkv0, mixed0, a_send, a_keep, vec = call(
        first_attention,
        [place] + x_blocks + [small, expander_bias, turn, triple, merger] + t_pieces,
        [SM] + [VM] * 4 + [ANY, VM, VM] + [ANY] * 5,
        [full, shape(512, 768), shape(512, 256), send, keep, shape(16, W, dtype=F32)],
        scratch=[wide, merge, pltpu.VMEM((4, 16, 768), BF), pltpu.SemaphoreType.DMA((11,))],
        room=14,
        flops=2 * 10**9,
    )
    a_got = move(a_send, flip_core=1)
    w_near, w_far = after(tuple(cut[3:]), e_pieces[1], e_pieces[2], a_send)
    w_far = move(w_far, flip_z=3)
    before0, f_send, f_keep = call(
        first_forward,
        [place, normed0, vec, expander, shrinker] + e_pieces,
        [SM, VM, VM] + [ANY] * 5,
        [shape(512, W, dtype=F32), send, keep],
        scratch=[wide, shrink, pltpu.VMEM((512, W), BF), pltpu.SemaphoreType.DMA((5,))],
        room=14,
        flops=2 * 10**9,
    )
    f_got = move(f_send, flip_core=1)
    up_blocks = gather_tokens(after(cotangent, e_pieces[1]))

    def other(kept, got):
        return move((kept[128:] + got[128:].astype(F32)).astype(BF), flip_z=1)

    a_far = other(after(a_keep, up_blocks[2]), a_got)
    sums = [a_keep, a_got, a_far, f_keep, f_got, other(f_keep, f_got)]
    block = [shape(128, W, dtype=F32), shape(128, W), shape(8, 128, dtype=F32)]
    state1, normed1, squares0 = call(
        functools.partial(join, layer=0), [after(place, up_blocks[3]), inputs] + sums + [vec], [SM] + [VM] * 8, block
    )
    n_blocks = gather_tokens(normed1)
    w_far = after(w_far, n_blocks[1])
    w_pieces = [move(w_near, flip_core=1), w_far, move(w_far[256:], flip_core=1)]

    normed1, up1, act1, ss1, mixed1, b_send, b_keep, send1, keep1, bias1 = call(
        last_layer,
        [place] + n_blocks + up_blocks + [vec, turn, triple, merger, expander, shrinker] + w_pieces,
        [SM] + [VM] * 10 + [ANY] * 7,
        [full, full, full, shape(512, WIDE), shape(512, 256), full, shape(512, W, dtype=F32)]
        + [send, keep, shape(8, WIDE, dtype=F32)],
        scratch=[
            wide, merge, shrink, pltpu.VMEM((512, 768), BF), pltpu.VMEM((512, 768), F32),
            pltpu.VMEM((512, 256), BF), pltpu.VMEM((512, W), F32), pltpu.SemaphoreType.DMA((9,)),
        ],
        room=14,
        flops=8 * 10**9,
    )
    got1 = move(send1, flip_core=1)
    s0, k0, s2, k2 = weight_one(place, act1, up1, normed1, ss1)
    low1 = (keep1[128:] + after(got1, s0)[128:].astype(F32)).astype(BF)
    far1 = move(low1, flip_z=1)
    s1, k1, s3, k3 = weight_two(after(place, low1), act1, up1, normed1, ss1, mixed1)
    g0, g2 = hops(after((s0, s2), low1), (0, 2), 0)
    slope1, low1, rows1 = call(
        functools.partial(norm_back, layer=1),
        [after(place, s1), state1, cotangent, cotangent, keep1, got1, far1, vec],
        [SM] + [VM] * 7,
        [shape(128, W, dtype=F32), shape(128, W), shape(8, W, dtype=F32)],
    )
    u_blocks = gather_late(low1)
    g1, g3 = hops(after((s1, s3), low1), (1, 3), 0)
    s0, k0, s2, k2 = first_folds(after(place, low1), (k0, k2), (g0, g2), (0, 2))
    one1 = [k0, k2] + hops([s0, s2], (0, 2), 1)

    up0, act0, ss0, send0, keep0, bias0 = call(
        first_back,
        [place] + u_blocks + [before0, qkv0, turn, triple, merger, expander, shrinker]
        + t_pieces + e_pieces,
        [SM] + [VM] * 7 + [ANY] * 10,
        [full, full, shape(512, WIDE), send, keep, shape(8, WIDE, dtype=F32)],
        scratch=[
            wide, merge, shrink, pltpu.VMEM((512, 768), F32), pltpu.VMEM((512, 256), BF),
            pltpu.SemaphoreType.DMA((12,)),
        ],
        room=14,
        flops=5 * 10**9,
    )
    got0 = move(send0, flip_core=1)
    s0, k0, s2, k2 = weight_one(place, act0, up0, normed0, ss0)
    f1, h1, f3, h3 = first_folds(after(place, s0), (k1, k3), (g1, g3), (1, 3))
    g0, g2 = hops((s0, s2), (0, 2), 0)
    s1, k1, s3, k3 = weight_two(after(place, f1), act0, up0, normed0, ss0, mixed0)
    two1 = [h1, h3] + hops([f1, f3], (1, 3), 1)
    g1, g3 = hops((s1, s3), (1, 3), 0)
    far0 = other(keep0, got0)
    s0, k0, s2, k2 = first_folds(place, (k0, k2), (g0, g2), (0, 2))
    one0 = [k0, k2] + hops([s0, s2], (0, 2), 1)
    units1 = fold_middle(after(place, s0), one1, two1)
    s1, k1, s3, k3 = first_folds(place, (k1, k3), (g1, g3), (1, 3))
    two0 = [k1, k3] + hops([s1, s3], (1, 3), 1)
    units1 = fold_last(after(place, s1), units1)
    units0 = fold_middle(place, one0, two0)
    terms1 = send_z(after(place, units0[0]), units1, [])
    units0 = fold_last(place, units0)
    pieces1 = sum_z(after(place, units0[0]), terms1)
    input_grad, _, rows0 = call(
        functools.partial(norm_back, layer=0),
        [place, inputs, slope1, low1, keep0, got0, far0, vec],
        [SM] + [VM] * 7,
        [shape(128, W, dtype=F32), shape(128, W), shape(8, W, dtype=F32)],
    )
    (vector,) = call(
        vectors_out, [place, rows0, bias0, rows1, bias1], [SM] + [VM] * 4,
        [shape(32, 512, dtype=F32)], scratch=[pltpu.VMEM((16, W), F32)],
    )
    every1 = collect_last(after(place, units0[0]), pieces1)
    terms0 = send_z(place, units0, [vector])
    pieces0 = sum_z(place, terms0)
    line0 = line_unit(place, pieces0)
    b_got = move(after(b_send, pieces1[0]), flip_core=1)
    b_low = (
        b_keep.reshape(2, 256, W)[:, 128:] + b_got.reshape(2, 256, W)[:, 128:].astype(F32)
    ).astype(BF)
    b_far = move(b_low.reshape(256, W), flip_z=1)
    hidden_out, squares1 = call(
        functools.partial(join, layer=1),
        [place, state1, b_keep, b_got, b_far, vec],
        [SM] + [VM] * 5,
        [shape(128, W), shape(8, 128, dtype=F32)],
    )

    line0 = line_four(after(place, hidden_out), line0)
    totals = jnp.concatenate([squares0[:3, :1], squares1[:3, :1]]).reshape(1, 6)
    totals = totals + move(totals, flip_core=1)
    totals = totals + move(totals, flip_z=1)
    rms_stats = jnp.sqrt(totals / (length.astype(F32) * W) + 1e-06)
    line0 = line_three(after(place, rms_stats), line0)
    own0, got0 = line_two(place, line0)
    sums1 = put_last(after(every1, own0[0]))
    sums0 = put_sums(place, own0, sums1, [])
    *sums0, g_sum, s_sum, b_sum, b_copy, t_sum, e_sum = put_sums(place, got0, sums0, [own0[0]])
    return (
        hidden_out,
        input_grad,
        g_sum,
        s_sum,
        sums0[0],
        t_sum,
        sums0[1],
        b_sum,
        sums0[2],
        e_sum,
        sums0[3],
        b_copy,
        rms_stats,
    )


def solution(mesh):
    return jax.shard_map(
        body,
        mesh=mesh,
        in_specs=(
            P(("rep", "shard"), None),
            P("rep"),
            P(None, "shard"),
            P(None, "shard"),
            P(None, "shard", None),
            P(None, "shard"),
            P(None, "shard", None),
            P(None, "shard"),
            P(None, "shard", None),
            P(None, "shard"),
            P(None, "shard", None),
            P(None, "shard"),
            P(("rep", "shard"), None),
        ),
        out_specs=(
            P(("rep", "shard"), None),
            P(("rep", "shard"), None),
            P(None, "shard"),
            P(None, "shard"),
            P(None, "shard", None),
            P(None, "shard"),
            P(None, "shard", None),
            P(None, "shard"),
            P(None, "shard", None),
            P(None, "shard"),
            P(None, "shard", None),
            P(None, "shard"),
            P("rep", None),
        ),
        check_vma=False,
    )
```

```python
import functools
import math

import jax
import jax.numpy as jnp
from jax import lax
from jax.experimental import pallas as pl
from jax.experimental.pallas import tpu as pltpu
from jax.sharding import PartitionSpec as P

HD = 64
ROT = 32
LAYERS = 2
EPS_NORM = 1e-05
AXES = ("rep", "shard")
BF = jnp.bfloat16
F32 = jnp.float32
MINE = 4
W = 1024
WIDE = 1792
PART = 768
PAIR = 1536
ORDERS = ((0, 2, 1, 3), (2, 0, 1, 3), (1, 3, 2, 0), (3, 1, 2, 0))

VM = pl.BlockSpec(memory_space=pltpu.VMEM)
ANY = pl.BlockSpec(memory_space=pl.ANY)
HBM = pl.BlockSpec(memory_space=pltpu.HBM)
SM = pl.BlockSpec(memory_space=pltpu.SMEM)


def place_of(index):
    rep, shard = divmod(index, 4)
    x, rest = divmod(rep, 8)
    z_hi, y = divmod(rest, 4)
    z_lo, core = divmod(shard, 2)
    return x, y, z_hi * 2 + z_lo, core


def index_of(x, y, z, core):
    return ((x * 2 + z // 2) * 4 + y) * 4 + (z % 2) * 2 + core


def move(value, flip_x=0, flip_y=0, flip_z=0, flip_core=0):
    pairs = []
    for index in range(128):
        x, y, z, core = place_of(index)
        pairs.append((index, index_of(x ^ flip_x, y ^ flip_y, z ^ flip_z, core ^ flip_core)))
    return lax.ppermute(value, AXES, pairs)


def hop(value, link):
    by = 3 if link & 1 else 1
    return move(value, flip_y=by) if link > 1 else move(value, flip_x=by)


def link_bit(place, link):
    return place[4 + link]


def after(value, *others):
    return lax.optimization_barrier((value,) + others)[0]


def pick(value, index, axis=0):
    return lax.dynamic_index_in_dim(value, index, axis, keepdims=False)


def shape(*dims, dtype=BF):
    return jax.ShapeDtypeStruct(dims, dtype)


def call(body, args, specs, outs, out_specs=None, scratch=(), flops=0, aliases=None, room=4):
    held = sum(math.prod(o.shape) * o.dtype.itemsize for o in outs)
    held += sum(math.prod(a.shape) * a.dtype.itemsize for a, s in zip(args, specs) if s is VM)
    held += sum(math.prod(s.shape) * s.dtype.itemsize for s in scratch if jnp.issubdtype(s.dtype, jnp.floating))
    room = held + (room << 20)
    return pl.pallas_call(
        body,
        out_shape=outs,
        in_specs=specs,
        out_specs=out_specs or [VM] * len(outs),
        scratch_shapes=scratch,
        input_output_aliases=aliases or {},
        compiler_params=pltpu.CompilerParams(vmem_limit_bytes=room),
        cost_estimate=pl.CostEstimate(flops=1, bytes_accessed=1, transcendentals=0),
    )(*args)


def dot(left, right):
    return jnp.dot(left, right, preferred_element_type=F32)


def dot_t(left, right):
    return lax.dot_general(left, right, (((1,), (1,)), ((), ())), preferred_element_type=F32)


def t_dot(left, right):
    return lax.dot_general(left, right, (((0,), (0,)), ((), ())), preferred_element_type=F32)


def copies(pairs, sems):
    started = []
    for at, (source, target) in enumerate(pairs):
        copy = pltpu.make_async_copy(source, target, sems.at[at])
        copy.start()
        started.append(copy)
    return started


def finish(started):
    for copy in started:
        copy.wait()


def lanes(start, size):
    return pl.ds(pl.multiple_of(start, 128), size)


def rows_at(start, size):
    return pl.ds(pl.multiple_of(start, 16), size)


def cut_triple(
    place, gains, shifts, merger_bias, shrinker_bias, triple_bias, triple,
    small, out1, out2, out3, slab, sems,
):
    shard = place[2]
    started = copies([(triple.at[0], slab)], sems)
    narrow = [v[...].astype(F32) for v in (gains, shifts, merger_bias, shrinker_bias)]
    narrow = jnp.concatenate(narrow + [jnp.zeros((8, 256), F32)], axis=0)
    tall = jnp.concatenate(
        [jnp.zeros((8, 768), F32), triple_bias[...].astype(F32), jnp.zeros((6, 768), F32)], axis=0
    )
    both = jnp.concatenate([narrow, jnp.zeros((16, 512), F32)], axis=1) + tall
    small[...] = both.astype(BF)
    for ref in (out1, out2, out3):
        ref[pl.ds(256, 16), :] = both.astype(BF)
    finish(started)
    for k, ref in ((2, out2), (3, out3), (1, out1)):
        for p in range(3):
            ref[pl.ds(0, 256), pl.ds(p * 256, 256)] = slab[:, lanes(p * W + (shard ^ k) * 256, 256)]


def cut_rest(
    place, cotangent, triple, expander, e1, e2, e3, w1, wz, slab, first, second, sems
):
    shard = place[2]
    pairs = [(expander.at[0], first), (expander.at[1], second), (triple.at[1], slab)]
    started = copies(pairs, sems)
    e2[pl.ds(256, 128), :] = cotangent[...]
    started[0].wait()
    for k, ref in ((2, e2), (3, e3), (1, e1)):
        ref[pl.ds(0, 256), :] = first[:, lanes((shard ^ k) * W, W)]
    finish(started[1:])
    for k, ref in ((2, wz.at[pl.ds(0, 256)]), (3, wz.at[pl.ds(256, 256)]), (1, w1)):
        block = shard ^ k
        ref[:, pl.ds(0, W)] = second[:, lanes(block * W, W)]
        for p in range(3):
            ref[:, pl.ds(W + p * 256, 256)] = slab[:, lanes(p * W + block * 256, 256)]


def own_triple(shard, layer, triple, wide):
    return [
        (
            triple.at[layer, :, lanes(p * W + shard * 256, 256)],
            wide.at[rows_at(shard * 256, 256), pl.ds(W + p * 256, 256)],
        )
        for p in range(3)
    ]


def own_expander(shard, layer, expander, wide):
    return [
        (expander.at[layer, :, lanes(shard * W, W)], wide.at[rows_at(shard * 256, 256), pl.ds(0, W)])
    ]


def piece_rows(shard, k, wide):
    return wide.at[rows_at((shard ^ k) * 256, 256)]


def first_triple(shard, pieces, wide):
    return [
        (ref.at[pl.ds(0, 256)], piece_rows(shard, k, wide).at[:, pl.ds(W, 768)])
        for k, ref in zip((1, 2, 3), pieces)
    ]


def first_expander(shard, pieces, wide):
    return [
        (ref.at[pl.ds(0, 256)], piece_rows(shard, k, wide).at[:, pl.ds(0, W)])
        for k, ref in zip((1, 2, 3), pieces)
    ]


def second_wide(shard, pieces, wide):
    one, two, three = pieces
    return [
        (one, piece_rows(shard, 1, wide)),
        (two.at[pl.ds(0, 256)], piece_rows(shard, 2, wide)),
        (three, piece_rows(shard, 3, wide)),
    ]


def spots(shard):
    row = lax.broadcasted_iota(jnp.int32, (512, 1), 0)
    col = lax.broadcasted_iota(jnp.int32, (1, 512), 1)

    def at(i):
        return (((i >> 7) ^ shard) << 7) | (i & 127)

    return at(row), at(col)


def rotate(values, turn, back=False):
    ahead = pltpu.roll(values, 256 - 16, 1) * turn[1]
    behind = pltpu.roll(values, 16, 1) * turn[2]
    if back:
        return values * turn[0] - ahead - behind
    return values * turn[0] + ahead + behind


def normalize(state):
    mean = jnp.mean(state, axis=-1, keepdims=True)
    centred = state - mean
    spread = jnp.mean(centred * centred, axis=-1, keepdims=True)
    factor = lax.rsqrt(spread + EPS_NORM)
    return centred * factor, factor


ROOT = math.sqrt(2.0 / math.pi)


def gelu_both(v):
    square = v * v
    t = jnp.tanh(ROOT * v * (1.0 + 0.044715 * square))
    half = 0.5 * (1.0 + t)
    slope = half + 0.5 * v * (1.0 - t * t) * (ROOT + (3.0 * 0.044715 * ROOT) * square)
    return v * half, slope


def heads_out(normed, wide, bias, turn, qkv):
    scale = HD ** (-0.5)
    for p in range(3):
        part = dot(normed[...], wide[:, pl.ds(W + p * 256, 256)]) + bias[:, pl.ds(p * 256, 256)]
        if p < 2:
            part = rotate(part, turn)
        if p == 0:
            part = part * scale
        qkv[:, pl.ds(p * 256, 256)] = part.astype(BF)


def probabilities(qkv, h, allowed):
    q = qkv[:, pl.ds(h * HD, HD)]
    k = qkv[:, pl.ds(256 + h * HD, HD)]
    scores = jnp.where(allowed, dot_t(q, k), -1000000000.0)
    powered = jnp.exp(scores - jnp.max(scores, axis=-1, keepdims=True))
    return powered * (1.0 / jnp.sum(powered, axis=-1, keepdims=True))


def attend(qkv, allowed, mixed):
    for h in range(MINE):
        low = probabilities(qkv, h, allowed).astype(BF)
        mixed[:, pl.ds(h * HD, HD)] = dot(low, qkv[:, pl.ds(512 + h * HD, HD)]).astype(BF)


def attend_back(qkv, allowed, mixed, slope_mixed, slopes, forward):
    for h in range(MINE):
        probs = probabilities(qkv, h, allowed)
        low = probs.astype(BF)
        q = qkv[:, pl.ds(h * HD, HD)]
        k = qkv[:, pl.ds(256 + h * HD, HD)]
        v = qkv[:, pl.ds(512 + h * HD, HD)]
        if forward:
            mixed[:, pl.ds(h * HD, HD)] = dot(low, v).astype(BF)
        out = slope_mixed[:, pl.ds(h * HD, HD)]
        slope_probs = dot_t(out, v)
        centre = jnp.sum(probs * slope_probs, axis=-1, keepdims=True)
        slope_scores = (probs * (slope_probs - centre)).astype(BF)
        slopes[:, pl.ds(h * HD, HD)] = dot(slope_scores, k)
        slopes[:, pl.ds(256 + h * HD, HD)] = t_dot(slope_scores, q)
        slopes[:, pl.ds(512 + h * HD, HD)] = t_dot(low, out)


def hand_out(left, right, send, keep):
    for n in range(4):
        cols = pl.ds(n * 256, 256)
        part = dot(left[...], right[:, cols])
        spread_out(part, cols, send, keep)


def spread_out(part, cols, send, keep):
    keep[pl.ds(0, 128), cols] = part[0:128]
    send[pl.ds(0, 128), cols] = part[128:256].astype(BF)
    keep[pl.ds(128, 128), cols] = part[256:384]
    send[pl.ds(128, 128), cols] = part[384:512].astype(BF)


def first_attention(
    place, x0, x1, x2, x3, small, bias, turn, triple, merger, t1, t2, t3,
    normed, qkv, mixed, send, keep, vec, wide, merge, smalls, sems,
):
    shard, length = place[2], place[3]
    pairs = [(small, smalls.at[shard])]
    pairs += [(t1.at[pl.ds(256, 16)], smalls.at[shard ^ 1])]
    pairs += [(t2.at[pl.ds(256, 16)], smalls.at[shard ^ 2])]
    pairs += [(t3.at[pl.ds(256, 16)], smalls.at[shard ^ 3])]
    pairs += own_triple(shard, 0, triple, wide) + [(merger.at[0], merge)]
    started = copies(pairs + first_triple(shard, (t1, t2, t3), wide), sems)
    for copy in started[:4]:
        copy.wait()
    vec[...] = jnp.zeros_like(vec)
    for j in range(4):
        vec[pl.ds(0, 8), pl.ds(j * 256, 256)] = smalls[j].astype(F32)[0:8, 0:256]
    for p in range(3):
        block = p * 4 + shard
        j = (block * 11) >> 5
        vec[pl.ds(8, 2), pl.ds(p * 256, 256)] = smalls[j, :, lanes((block - 3 * j) * 256, 256)].astype(
            F32
        )[8:10]
    vec[pl.ds(10, 2), :] = bias[...].astype(F32)
    gain, shift = vec[pl.ds(0, 1), :], vec[pl.ds(2, 1), :]
    for k, ref in enumerate((x0, x1, x2, x3)):
        hat, _ = normalize(ref[...].astype(F32))
        normed[pl.ds(k * 128, 128), :] = (hat * gain + shift).astype(BF)
    finish(started[4:])
    row, col = spots(shard)
    allowed = (col <= row) & (col < length)
    heads_out(normed, wide, vec[pl.ds(8, 1), pl.ds(0, 768)], turn, qkv)
    attend(qkv, allowed, mixed)
    hand_out(mixed, merge, send, keep)


def first_forward(
    place, normed, vec, expander, shrinker, e1, e2, e3,
    before, send, keep, wide, shrink, act, sems,
):
    shard = place[2]
    pairs = own_expander(shard, 0, expander, wide) + first_expander(shard, (e1, e2, e3), wide)
    started = copies(pairs + [(shrinker.at[0], shrink)], sems)
    finish(started)
    for n in range(4):
        cols = pl.ds(n * 256, 256)
        part = dot(normed[...], wide[:, cols]) + vec[pl.ds(10, 1), cols]
        before[:, cols] = part
        act[:, cols] = gelu_both(part)[0].astype(BF)
    hand_out(act, shrink, send, keep)


def slopes_out(ss, bias, wide, send, keep):
    bias[...] = jnp.broadcast_to(jnp.sum(ss[...].astype(F32), axis=0, keepdims=True), bias.shape)
    for n in range(4):
        part = dot_t(ss[...], wide[pl.ds(n * 256, 256), :])
        spread_out(part, pl.ds(n * 256, 256), send, keep)


def triple_slopes(slopes, turn, ss):
    scale = HD ** (-0.5)
    ss[:, pl.ds(W, 256)] = (rotate(slopes[:, pl.ds(0, 256)], turn, True) * scale).astype(BF)
    ss[:, pl.ds(W + 256, 256)] = rotate(slopes[:, pl.ds(256, 256)], turn, True).astype(BF)
    ss[:, pl.ds(W + 512, 256)] = slopes[:, pl.ds(512, 256)].astype(BF)


def last_layer(
    place, n0, n1, n2, n3, u0, u1, u2, u3, vec, turn, triple, merger, expander, shrinker, w1, w2, w3,
    normed, up, act, ss, mixed, bsend, bkeep, send, keep, bias,
    wide, merge, shrink, qkv, slopes, out, before, sems,
):
    shard, length = place[2], place[3]
    pairs = own_triple(shard, 1, triple, wide) + own_expander(shard, 1, expander, wide)
    pairs += second_wide(shard, (w1, w2, w3), wide) + [(merger.at[1], merge), (shrinker.at[1], shrink)]
    started = copies(pairs, sems)
    row, col = spots(shard)
    for k, (n, u) in enumerate(((n0, u0), (n1, u1), (n2, u2), (n3, u3))):
        rows = pl.ds(k * 128, 128)
        normed[rows, :] = n[...]
        up[rows, :] = jnp.where(row[k * 128 : k * 128 + 128] < length, u[...].astype(F32), 0.0).astype(BF)
    finish(started)
    for n in range(4):
        cols = pl.ds(n * 256, 256)
        part = dot(normed[...], wide[:, cols]) + vec[pl.ds(11, 1), cols]
        value, slope = gelu_both(part)
        act[:, cols] = value.astype(BF)
        ss[:, cols] = (dot_t(up[...], shrink[cols, :]) * slope).astype(BF)
    hand_out(act, shrink, bsend.at[pl.ds(256, 256)], bkeep.at[pl.ds(256, 256)])
    allowed = (col <= row) & (col < length)
    heads_out(normed, wide, vec[pl.ds(9, 1), pl.ds(0, 768)], turn, qkv)
    out[...] = dot_t(up[...], merge[...]).astype(BF)
    attend_back(qkv, allowed, mixed, out, slopes, True)
    hand_out(mixed, merge, bsend.at[pl.ds(0, 256)], bkeep.at[pl.ds(0, 256)])
    triple_slopes(slopes, turn, ss)
    slopes_out(ss, bias, wide, send, keep)


def first_back(
    place, u0, u1, u2, u3, before, qkv, turn, triple, merger, expander, shrinker,
    t1, t2, t3, e1, e2, e3,
    up, act, ss, send, keep, bias, wide, merge, shrink, slopes, out, sems,
):
    shard, length = place[2], place[3]
    pairs = own_triple(shard, 0, triple, wide) + own_expander(shard, 0, expander, wide)
    pairs += first_triple(shard, (t1, t2, t3), wide)
    pairs += first_expander(shard, (e1, e2, e3), wide)
    started = copies(pairs + [(merger.at[0], merge), (shrinker.at[0], shrink)], sems)
    for k, u in enumerate((u0, u1, u2, u3)):
        up[pl.ds(k * 128, 128), :] = u[...]
    finish(started)
    for n in range(4):
        cols = pl.ds(n * 256, 256)
        value, slope = gelu_both(before[:, cols])
        act[:, cols] = value.astype(BF)
        ss[:, cols] = (dot_t(up[...], shrink[cols, :]) * slope).astype(BF)
    row, col = spots(shard)
    allowed = (col <= row) & (col < length)
    out[...] = dot_t(up[...], merge[...]).astype(BF)
    attend_back(qkv, allowed, None, out, slopes, False)
    triple_slopes(slopes, turn, ss)
    slopes_out(ss, bias, wide, send, keep)


def halve(term, cols, o, bit, send, keep, at):
    for ref, half in ((keep, bit), (send, 1 - bit)):
        value = term[pl.ds(pl.multiple_of(half * 128, 128), 128), cols].astype(BF)
        for k in range(8):
            ref[pl.ds(k * 64 + o * 16, 16), at] = value[k * 16 : k * 16 + 16]


def terms_one(place, act, up, normed, ss, s0, k0, s2, k2, term):
    whole = pl.ds(0, PART)
    for o in range(4):
        cols = pl.ds(o * 256, 256)
        term[...] = t_dot(act[:, cols], up[:, pl.ds(0, PART)])
        halve(term, whole, o, link_bit(place, ORDERS[0][0]), s0, k0, whole)
        term[...] = t_dot(normed[:, cols], ss[:, pl.ds(0, PART)])
        halve(term, whole, o, link_bit(place, ORDERS[2][0]), s2, k2, whole)


def terms_two(place, act, up, normed, ss, mixed, s1, k1, s3, k3, term, last):
    one, three = link_bit(place, ORDERS[1][0]), link_bit(place, ORDERS[3][0])
    whole = pl.ds(0, PART)
    last[...] = t_dot(mixed[...], up[...])
    for o in range(4):
        cols = pl.ds(o * 256, 256)
        term[:, pl.ds(0, 256)] = t_dot(act[:, cols], up[:, pl.ds(PART, 256)])
        term[:, pl.ds(256, 256)] = last[:, cols]
        both = t_dot(normed[:, cols], ss[:, pl.ds(PART, W)])
        term[:, pl.ds(512, 256)] = both[:, 256:512]
        halve(term, whole, o, one, s1, k1, whole)
        term[:, pl.ds(0, 256)] = both[:, 0:256]
        term[:, pl.ds(256, 512)] = both[:, 512:W]
        halve(term, whole, o, three, s3, k3, whole)


def weight_one(place, act, up, normed, ss):
    return call(
        terms_one, [place, act, up, normed, ss], [SM] + [VM] * 4, [shape(512, PART)] * 4,
        scratch=[pltpu.VMEM((256, PART), F32)], flops=2 * 10**9,
    )


def weight_two(place, act, up, normed, ss, mixed):
    return call(
        terms_two, [place, act, up, normed, ss, mixed], [SM] + [VM] * 5, [shape(512, PART)] * 4,
        scratch=[pltpu.VMEM((256, PART), F32), pltpu.VMEM((256, W), F32)], flops=2 * 10**9,
    )


def join(place, state, *refs, layer):
    shard, length = place[2], place[3]
    spot = shard * 128 + lax.broadcasted_iota(jnp.int32, (128, 1), 0)
    valid = (spot < length).astype(F32)
    if layer == 0:
        ak, ag, az, fk, fg, fz, vec, new, out, squares = refs
        attended = ak[pl.ds(0, 128), :] + ag[pl.ds(0, 128), :].astype(F32) + az[...].astype(F32)
        branch = fk[pl.ds(0, 128), :] + fg[pl.ds(0, 128), :].astype(F32) + fz[...].astype(F32)
    else:
        kept, got, far, vec, out, squares = refs
        attended, branch = [
            kept[pl.ds(at * 256, 128), :]
            + got[pl.ds(at * 256, 128), :].astype(F32)
            + far[pl.ds(at * 128, 128), :].astype(F32)
            for at in (0, 1)
        ]
    attended = attended + vec[pl.ds(4 + layer, 1), :]
    branch = branch + vec[pl.ds(6 + layer, 1), :]
    old = state[...].astype(F32)
    for at, item in enumerate((old, attended, branch)):
        total = jnp.sum(jnp.sum(item * item, axis=1, keepdims=True) * valid)
        squares[pl.ds(at, 1), :] = jnp.full((1, 128), total, F32)
    state_new = old + attended + branch
    if layer == 0:
        new[...] = state_new
        hat, _ = normalize(state_new)
        out[...] = (hat * vec[pl.ds(1, 1), :] + vec[pl.ds(3, 1), :]).astype(BF)
    else:
        out[...] = (state_new * valid).astype(BF)


def norm_back(place, state, slope, up, sk, sg, sz, vec, new, low, rows, *, layer):
    shard, length = place[2], place[3]
    spot = shard * 128 + lax.broadcasted_iota(jnp.int32, (128, 1), 0)
    given = slope[...].astype(F32)
    upstream = up[...].astype(F32)
    if layer == LAYERS - 1:
        given = jnp.where(spot < length, given, 0.0)
        upstream = given
    sn = sk[pl.ds(0, 128), :] + sg[pl.ds(0, 128), :].astype(F32) + sz[...].astype(F32)
    hat, factor = normalize(state[...].astype(F32))
    rows[...] = jnp.zeros_like(rows)
    rows[pl.ds(0, 1), :] = jnp.sum(sn * hat, axis=0, keepdims=True)
    rows[pl.ds(1, 1), :] = jnp.sum(sn, axis=0, keepdims=True)
    rows[pl.ds(2, 1), :] = jnp.sum(upstream, axis=0, keepdims=True)
    d = sn * vec[pl.ds(layer, 1), :]
    mean = jnp.mean(d, axis=-1, keepdims=True)
    along = jnp.mean(d * hat, axis=-1, keepdims=True)
    result = given + factor * (d - mean - hat * along)
    new[...] = result
    low[...] = result.astype(BF)


def vectors_out(place, rows0, bias0, rows1, bias1, out, full):
    shard = place[2]
    full[...] = jnp.zeros_like(full)
    for at, (rows, bias) in enumerate(((rows0, bias0), (rows1, bias1))):
        base = at * 7
        full[pl.ds(base, 3), :] = rows[pl.ds(0, 3), :]
        for p in range(3):
            full[pl.ds(base + 3 + p, 1), lanes(shard * 256, 256)] = bias[
                pl.ds(0, 1), pl.ds(W + p * 256, 256)
            ]
        full[pl.ds(base + 6, 1), :] = bias[pl.ds(0, 1), pl.ds(0, W)]
    out[pl.ds(0, 16), :] = full[:, pl.ds(0, 512)]
    out[pl.ds(16, 16), :] = full[:, pl.ds(512, 512)]


def add_half(kept, got, bit, refs, at):
    size = kept.shape[0] // 2
    for ref, half in zip(refs, (1 - bit, bit)):
        rows = rows_at(half * size, size)
        total = kept[rows, :].astype(F32) + got[rows, :].astype(F32)
        ref[:, at] = total.astype(BF)


def fold_one(place, ka, ga, kb, gb, sa, ha, sb, hb, *, parts):
    for part, (k, g, s, h) in zip(parts, ((ka, ga, sa, ha), (kb, gb, sb, hb))):
        add_half(k, g, link_bit(place, ORDERS[part][1]), (s, h), slice(None))


def fold_two(place, k0, g0, k1, g1, k2, g2, k3, g3, sa, ha, sb, hb):
    for part, (k, g) in enumerate(((k0, g0), (k1, g1), (k2, g2), (k3, g3))):
        refs = (sb, hb) if part > 1 else (sa, ha)
        at = pl.ds((part & 1) * PART, PART)
        add_half(k, g, link_bit(place, ORDERS[part][2]), refs, at)


def fold_three(place, ka, ga, kb, gb, sa, ha, sb, hb):
    for part, (k, g, s, h) in zip((0, 2), ((ka, ga, sa, ha), (kb, gb, sb, hb))):
        add_half(k, g, link_bit(place, ORDERS[part][3]), (s, h), slice(None))


def first_folds(place, kept, got, parts):
    args = [kept[0], got[0], kept[1], got[1]]
    return call(
        functools.partial(fold_one, parts=parts), [place] + args, [SM] + [VM] * 4, [shape(256, PART)] * 4
    )


def z_send(place, *refs):
    ka, ga, kb, gb, *refs = refs
    shard = place[2]
    z_lo = shard >> 1
    if len(refs) == 6:
        vector, *refs = refs
    else:
        vector = None
    side, across, cross, plain, wide = refs
    a = ka[...].astype(F32) + ga[...].astype(F32)
    b = kb[...].astype(F32) + gb[...].astype(F32)
    wide[:, pl.ds(0, W)] = b[:, 0:W]
    wide[:, pl.ds(W, 256)] = a[:, 1280:PAIR]
    wide[:, pl.ds(1280, 512)] = b[:, W:PAIR]
    plain[...] = a[:, 0:1280]
    cross[...] = wide[rows_at(z_lo * 32, 32), :]
    side[:, pl.ds(0, WIDE)] = wide[rows_at((1 - z_lo) * 32, 32), :].astype(BF)
    across[:, pl.ds(0, WIDE)] = cross[...].astype(BF)
    across[:, pl.ds(WIDE, 1280)] = plain[pl.ds(0, 32), :].astype(BF)
    across[:, pl.ds(WIDE + 1280, 1280)] = plain[pl.ds(32, 32), :].astype(BF)
    if vector is not None:
        side[:, pl.ds(WIDE, 512)] = vector[...].astype(BF)
        across[:, pl.ds(WIDE + 2560, 512)] = vector[...].astype(BF)


def local_rows():
    row = lax.broadcasted_iota(jnp.int32, (32, 1), 0) & 15
    return (row == 6) | (row == 13)


def z_sum(place, *refs):
    cross, plain, za, zb, z2, *refs = refs
    vector = None
    if len(refs) == 6:
        vector, *refs = refs
        near, kept, whole, vec, both = refs
    else:
        near, kept, whole, both = refs
    core = place[2] & 1
    both[pl.ds(0, 32), :] = cross[...] + z2[:, pl.ds(0, WIDE)].astype(F32)
    both[pl.ds(32, 32), :] = za[:, pl.ds(0, WIDE)].astype(F32) + zb[:, pl.ds(0, WIDE)].astype(F32)
    for at in range(2):
        own = both[rows_at(at * 32 + core * 16, 16), :]
        other = both[rows_at(at * 32 + (1 - core) * 16, 16), :]
        kept[pl.ds(at * 16, 16), :] = own.astype(BF)
        near[pl.ds(at * 16, 16), pl.ds(0, WIDE)] = other.astype(BF)
    for at in range(2):
        rows = pl.ds(at * 32, 32)
        got = z2[:, pl.ds(WIDE + at * 1280, 1280)].astype(F32)
        whole[rows, :] = (plain[rows, :] + got).astype(BF)
    if vector is not None:
        sides = za[:, pl.ds(WIDE, 512)].astype(F32) + zb[:, pl.ds(WIDE, 512)].astype(F32)
        total = vector[...] + z2[:, pl.ds(WIDE + 2560, 512)].astype(F32)
        total = total + jnp.where(local_rows(), 0.0, sides)
        vec[...] = total
        near[:, pl.ds(WIDE, 512)] = total.astype(BF)


def payload_parts(place, kept, near, whole, a, b):
    shard = place[2]
    for k in range(4):
        rows = rows_at((shard ^ k) * 16, 16)
        ref, at = (near, k >> 1) if k & 1 else (kept, k >> 1)
        source = ref[pl.ds(at * 16, 16), pl.ds(0, WIDE)]
        b[rows, pl.ds(0, W)] = source[:, 0:W]
        a[rows, pl.ds(1280, 256)] = source[:, W:1280]
        b[rows, pl.ds(W, 512)] = source[:, 1280:WIDE]
    a[pl.ds(0, 64), pl.ds(0, 1280)] = whole[...]


def payload_both(place, kept, near, whole, out):
    payload_parts(place, kept, near, whole, out.at[pl.ds(0, 64)], out.at[pl.ds(64, 64)])


def payload(place, kept, near, whole, *refs):
    *vec, a, b = refs
    payload_parts(place, kept, near, whole, a, b)
    if not vec:
        return
    vec = vec[0]
    total = vec[...] + jnp.where(local_rows(), 0.0, near[:, pl.ds(WIDE, 512)].astype(F32))
    low = total.astype(BF)
    a[pl.ds(64, 16), :] = jnp.zeros((16, PAIR), BF)
    a[pl.ds(64, 16), pl.ds(0, 512)] = low[0:16]
    a[pl.ds(64, 16), pl.ds(512, 512)] = low[16:32]


def line_up(own, got, bit, size, outs, cols):
    for ref, at in zip(outs, cols):
        ref[rows_at(bit * size, size), :] = own[pl.ds(0, size), at]
        ref[rows_at((1 - bit) * size, size), :] = got[pl.ds(0, size), at]


def vector_rows(own, got, at, size):
    rows = pl.ds(at, size)
    return (own[rows, :].astype(F32) + got[rows, :].astype(F32)).astype(BF)


def gather_four(place, oa, ga, ob, gb, a, b):
    line_up(oa, ga, link_bit(place, ORDERS[0][3]), 64, [a], [slice(None)])
    line_up(ob, gb, link_bit(place, ORDERS[2][3]), 64, [b], [slice(None)])
    if a.shape[0] > 128:
        a[pl.ds(128, 16), :] = vector_rows(oa, ga, 64, 16)


def gather_three(place, oa, ga, ob, gb, p0, p1, p2, p3):
    cols = [pl.ds(0, PART), pl.ds(PART, PART)]
    line_up(oa, ga, link_bit(place, ORDERS[0][2]), 128, [p0, p1], cols)
    line_up(ob, gb, link_bit(place, ORDERS[2][2]), 128, [p2, p3], cols)
    if p0.shape[0] == 256:
        return
    low = vector_rows(oa, ga, 128, 16)
    p0[pl.ds(256, 32), :] = jnp.zeros((32, PART), BF)
    p0[pl.ds(256, 16), pl.ds(0, 512)] = low[:, 0:512]
    p0[pl.ds(272, 16), pl.ds(0, 512)] = low[:, 512:W]


def gather_two(place, o0, g0, o1, g1, o2, g2, o3, g3, p0, p1, p2, p3):
    outs = (p0, p1, p2, p3)
    for part, (o, g) in enumerate(((o0, g0), (o1, g1), (o2, g2), (o3, g3))):
        line_up(o, g, link_bit(place, ORDERS[part][1]), 256, [outs[part]], [slice(None)])
    p0[pl.ds(512, 32), :] = vector_rows(o0, g0, 256, 32)


def each(count, step):
    lax.fori_loop(0, count, lambda at, none: step(at) or none, 0)


def put(part, value, o, base, t, m, e, s):
    rows = rows_at(base, 16)
    if part == 0:
        s[rows_at(o * 256 + base, 16), pl.ds(0, PART)] = value
    elif part == 1:
        s[rows_at(o * 256 + base, 16), pl.ds(PART, 256)] = value[:, 0:256]
        m[rows, pl.ds(o * 256, 256)] = value[:, 256:512]
        t[rows, pl.ds(o * 256, 256)] = value[:, 512:PART]
    elif part == 2:
        e[rows, pl.ds(o * W, PART)] = value
    else:
        e[rows, pl.ds(o * W + PART, 256)] = value[:, 0:256]
        t[rows, pl.ds(W + o * 256, 256)] = value[:, 256:512]
        t[rows, pl.ds(2 * W + o * 256, 256)] = value[:, 512:PART]


def assemble_last(every, t_out, m_out, e_out, s_out, t, m, e, s, sems):
    def device(at):
        x, y = at >> 2, at & 3
        bits = ((x & 1) ^ (x >> 1), x >> 1, (y & 1) ^ (y >> 1), y >> 1)
        for part in range(4):
            unit = sum(bits[link] << (3 - n) for n, link in enumerate(ORDERS[part]))
            for o in range(4):
                rows = rows_at(at * 128 + (part >> 1) * 64 + o * 16, 16)
                value = every[rows, pl.ds((part & 1) * PART, PART)].astype(F32)
                put(part, value, o, unit * 16, t, m, e, s)

    each(16, device)
    pairs = [(t, t_out.at[1]), (m, m_out.at[1]), (e, e_out.at[1]), (s, s_out.at[1])]
    finish(copies(pairs, sems))


def put_half(place, p0, p1, p2, p3, *refs, mine):
    if not mine:
        old, *refs = refs
        t_out, m_out, e_out, s_out, *sums, s0, s1, m1, t1, e2, e3, t3, both, vec, sems = refs[4:]
    else:
        t_out, m_out, e_out, s_out, s0, s1, m1, t1, e2, e3, t3, sems = refs[4:]
    pairs = []
    for part, ref in enumerate((p0, p1, p2, p3)):
        half = link_bit(place, ORDERS[part][0])
        base = (half if mine else 1 - half) * 128
        rows = rows_at(base, 128)
        for o in range(4):
            for k in range(8):
                value = ref[pl.ds(k * 64 + o * 16, 16), :].astype(F32)
                at = pl.ds(k * 16, 16)
                if part == 0:
                    s0[o, at, :] = value
                elif part == 1:
                    s1[o, at, :] = value[:, 0:256]
                    m1[at, pl.ds(o * 256, 256)] = value[:, 256:512]
                    t1[at, pl.ds(o * 256, 256)] = value[:, 512:PART]
                elif part == 2:
                    e2[o, at, :] = value
                else:
                    e3[o, at, :] = value[:, 0:256]
                    t3[at, pl.ds(o * 256, 256)] = value[:, 256:512]
                    t3[at, pl.ds(W + o * 256, 256)] = value[:, 512:PART]
            if part < 2:
                target = s_out.at[0, rows_at(o * 256 + base, 128)]
                pairs.append((s0.at[o], target.at[:, pl.ds(0, PART)]) if part == 0 else (s1.at[o], target.at[:, pl.ds(PART, 256)]))
            else:
                target = e_out.at[0, rows]
                pairs.append((e2.at[o], target.at[:, pl.ds(o * W, PART)]) if part == 2 else (e3.at[o], target.at[:, pl.ds(o * W + PART, 256)]))
        if part == 1:
            pairs.append((m1, m_out.at[0, rows]))
            pairs.append((t1, t_out.at[0, rows, pl.ds(0, W)]))
        if part == 3:
            pairs.append((t3, t_out.at[0, rows, pl.ds(W, 2 * W)]))
    started = copies(pairs, sems)
    if not mine:
        fetch = copies([(old.at[pl.ds(512, 32)], both)], sems.at[pl.ds(len(pairs), 1)])
        finish(fetch)
        low = both[...].astype(F32) + p0[pl.ds(512, 32), :].astype(F32)
        vec[:, pl.ds(0, 512)] = low[0:16, 0:512]
        vec[:, pl.ds(512, 512)] = low[16:32, 0:512]
        for at in range(LAYERS):
            own_sums(vec, at, place[2], *sums)
    finish(started)


def own_sums(vec, layer, shard, g_sum, s_sum, b_sum, b_copy, t_sum, e_sum):
    base = layer * 7
    row = pl.ds(layer, 1)
    for at, ref in ((0, g_sum), (1, s_sum), (2, b_sum), (2, b_copy)):
        ref[row, :] = vec[pl.ds(base + at, 1), lanes(shard * 256, 256)]
    for r in range(3):
        block = shard * 3 + r
        t_sum[row, pl.ds(r * 256, 256)] = vec[
            pl.ds(base + 3 + (block >> 2), 1), lanes((block & 3) * 256, 256)
        ]
    e_sum[row, :] = vec[pl.ds(base + 6, 1), :]


def hops(values, parts, phase):
    return [hop(value, ORDERS[part][phase]) for value, part in zip(values, parts)]


def fold_middle(place, one, two):
    kept = [one[0], two[0], one[1], two[1]]
    got = [one[2], two[2], one[3], two[3]]
    args = [v for pair in zip(kept, got) for v in pair]
    sa, ka, sb, kb = call(fold_two, [place] + args, [SM] + [VM] * 8, [shape(128, PAIR)] * 4)
    ga, gb = hops([sa, sb], (0, 2), 2)
    return [ka, ga, kb, gb]


def fold_last(place, units):
    sa, ka, sb, kb = call(fold_three, [place] + units, [SM] + [VM] * 4, [shape(64, PAIR)] * 4)
    ga, gb = hops([sa, sb], (0, 2), 3)
    return [ka, ga, kb, gb]


def send_z(place, units, vector):
    more = 512 * len(vector)
    side, across, cross, plain = call(
        z_send, [place] + units + vector, [SM] + [VM] * (4 + len(vector)),
        [
            shape(32, WIDE + more), shape(32, WIDE + 2560 + more),
            shape(32, WIDE, dtype=F32), shape(64, 1280, dtype=F32),
        ],
        scratch=[pltpu.VMEM((64, WIDE), F32)],
    )
    z2 = move(across, flip_z=2)
    za = move(side, flip_z=1)
    zb = move(side, flip_z=3)
    return [cross, plain, za, zb, z2] + vector


def sum_z(place, terms):
    vectors = len(terms) - 5
    near, kept, whole, *vec = call(
        z_sum, [place] + terms, [SM] + [VM] * len(terms),
        [shape(32, WIDE + 512 * vectors), shape(32, WIDE), shape(64, 1280)]
        + [shape(32, 512, dtype=F32)] * vectors,
        scratch=[pltpu.VMEM((64, WIDE), F32)],
    )
    return [kept, move(near, flip_core=1), whole] + vec


OUTS = [
    shape(LAYERS, 256, 3072, dtype=F32),
    shape(LAYERS, 256, 1024, dtype=F32),
    shape(LAYERS, 256, 4096, dtype=F32),
    shape(LAYERS, 1024, 1024, dtype=F32),
]


def line_unit(place, pieces):
    rows = 80 if len(pieces) == 4 else 64
    a, b = call(
        payload, [place] + pieces, [SM] + [VM] * len(pieces), [shape(rows, PAIR), shape(64, PAIR)]
    )
    ga, gb = hops([a, b], (0, 2), 3)
    return [a, ga, b, gb]


def line_four(place, args):
    rows = args[0].shape[0] + 64
    a, b = call(gather_four, [place] + args, [SM] + [VM] * 4, [shape(rows, PAIR), shape(128, PAIR)])
    ga, gb = hops([a, b], (0, 2), 2)
    return [a, ga, b, gb]


def line_three(place, args):
    rows = 288 if args[0].shape[0] > 128 else 256
    own = call(
        gather_three, [place] + args, [SM] + [VM] * 4, [shape(rows, PART)] + [shape(256, PART)] * 3
    )
    got = hops(own, range(4), 1)
    return [v for pair in zip(own, got) for v in pair]


def line_two(place, args):
    own = call(
        gather_two, [place] + args, [SM] + [VM] * 8, [shape(544, PART)] + [shape(512, PART)] * 3
    )
    return list(own), hops(own, range(4), 0)


def collect_last(place, pieces):
    (both,) = call(payload_both, [place] + pieces, [SM] + [VM] * 3, [shape(128, PAIR)])
    planes = [[(x * 2 + z) * 4 + y for x in range(4) for y in range(4)] for z in range(2)]
    return lax.all_gather(both, "rep", axis_index_groups=planes, axis=0, tiled=True)


def put_last(every):
    return call(
        assemble_last, [every], [VM], OUTS, out_specs=[ANY] * 4,
        scratch=[pltpu.VMEM(out.shape[1:], F32) for out in OUTS] + [pltpu.SemaphoreType.DMA((4,))],
    )


def put_sums(place, parts, earlier, old):
    outs, specs = list(OUTS), [ANY] * 4
    scratch = [
        pltpu.VMEM((4, 128, PART), F32), pltpu.VMEM((4, 128, 256), F32), pltpu.VMEM((128, W), F32),
        pltpu.VMEM((128, W), F32), pltpu.VMEM((4, 128, PART), F32), pltpu.VMEM((4, 128, 256), F32),
        pltpu.VMEM((128, 2 * W), F32),
    ]
    if old:
        outs += [shape(LAYERS, n, dtype=F32) for n in (256, 256, 256, 256, 768, 1024)]
        specs += [VM] * 6
        scratch += [pltpu.VMEM((32, PART), BF), pltpu.VMEM((16, W), F32)]
    return call(
        functools.partial(put_half, mine=not old), [place] + parts + old + list(earlier),
        [SM] + [VM] * 4 + [ANY] * (4 + len(old)), outs, out_specs=specs,
        scratch=scratch + [pltpu.SemaphoreType.DMA((20,))],
        aliases={5 + len(old) + i: i for i in range(4)},
    )


def gather_tokens(own):
    far = move(own, flip_z=1)
    near = move(own, flip_core=1)
    return [own, near, far, move(far, flip_core=1)]


def gather_late(own):
    far = move(own, flip_z=1)
    return [own, move(after(own, far), flip_core=1), far, move(far, flip_core=1)]


def body(
    inputs,
    lengths,
    gains,
    shifts,
    triple,
    triple_bias,
    merger,
    merger_bias,
    expander,
    expander_bias,
    shrinker,
    shrinker_bias,
    cotangent,
):
    rep = lax.axis_index("rep")
    shard = lax.axis_index("shard")
    length = lengths[0]
    x, y = rep // 8, rep % 4
    place = [x, y, shard, length, (x & 1) ^ (x >> 1), x >> 1, (y & 1) ^ (y >> 1), y >> 1]
    place = jnp.stack(place).astype(jnp.int32)

    small, *pieces = call(
        cut_triple,
        [place, gains, shifts, merger_bias, shrinker_bias, triple_bias, triple],
        [SM] + [VM] * 5 + [HBM],
        [shape(16, 768)] + [shape(272, 768)] * 3,
        scratch=[pltpu.VMEM((256, 3072), BF), pltpu.SemaphoreType.DMA((1,))],
    )

    def recut(one, two, three):
        return [
            move(one, flip_core=1),
            move(two, flip_z=1),
            move(three, flip_z=3, flip_core=1),
        ]

    t_pieces = recut(*pieces)
    x_blocks = gather_tokens(after(inputs, small))
    cut = call(
        cut_rest, [after(place, pieces[0], x_blocks[1]), cotangent, triple, expander],
        [SM, VM, HBM, HBM],
        [shape(256, W), shape(384, W), shape(256, W)]
        + [shape(256, WIDE), shape(512, WIDE)],
        scratch=[
            pltpu.VMEM((256, 3072), BF), pltpu.VMEM((256, 4096), BF), pltpu.VMEM((256, 4096), BF),
            pltpu.SemaphoreType.DMA((3,)),
        ],
    )
    e_pieces = recut(*after(tuple(cut[:2]), x_blocks[2]), after(cut[2], t_pieces[2]))

    spot = after(jnp.arange(512, dtype=jnp.int32), x_blocks[1])
    spot = (((spot >> 7) ^ shard) << 7) | (spot & 127)
    index = jnp.arange(ROT // 2, dtype=F32)
    freq = jnp.exp(index * (-2.0 * math.log(10000.0) / ROT))
    lane = jnp.arange(256, dtype=jnp.int32) % HD
    phase = spot.astype(F32)[:, None] * jnp.tile(freq, 16)[None, :]
    cosine, sine = jnp.cos(phase), jnp.sin(phase)
    turn = jnp.stack(
        [
            jnp.where(lane < ROT, cosine, 1.0),
            jnp.where(lane < ROT // 2, -sine, 0.0),
            jnp.where((lane >= ROT // 2) & (lane < ROT), sine, 0.0),
        ]
    )

    full = shape(512, W)
    send, keep = shape(256, W), shape(256, W, dtype=F32)
    wide = pltpu.VMEM((W, WIDE), BF)
    merge, shrink = pltpu.VMEM((256, W), BF), pltpu.VMEM((W, W), BF)

    normed0, qkv0, mixed0, a_send, a_keep, vec = call(
        first_attention,
        [place] + x_blocks + [small, expander_bias, turn, triple, merger] + t_pieces,
        [SM] + [VM] * 4 + [ANY, VM, VM, HBM, HBM] + [ANY] * 3,
        [full, shape(512, 768), shape(512, 256), send, keep, shape(16, W, dtype=F32)],
        scratch=[wide, merge, pltpu.VMEM((4, 16, 768), BF), pltpu.SemaphoreType.DMA((11,))],
        room=14,
        flops=2 * 10**9,
    )
    a_got = move(after(a_send, e_pieces[1]), flip_core=1)
    w_near, w_far = after(tuple(cut[3:]), e_pieces[2])
    w_far = move(w_far, flip_z=3)
    before0, f_send, f_keep = call(
        first_forward,
        [place, normed0, vec, expander, shrinker] + e_pieces,
        [SM, VM, VM, HBM, HBM] + [ANY] * 3,
        [shape(512, W, dtype=F32), send, keep],
        scratch=[wide, shrink, pltpu.VMEM((512, W), BF), pltpu.SemaphoreType.DMA((5,))],
        room=14,
        flops=2 * 10**9,
    )
    f_got = move(f_send, flip_core=1)

    def other(kept, got):
        return move((kept[128:] + got[128:].astype(F32)).astype(BF), flip_z=1)

    a_far = other(a_keep, a_got)
    sums = [a_keep, a_got, a_far, f_keep, f_got, other(f_keep, f_got)]
    block = [shape(128, W, dtype=F32), shape(128, W), shape(8, 128, dtype=F32)]
    state1, normed1, squares0 = call(
        functools.partial(join, layer=0), [place, inputs] + sums + [vec], [SM] + [VM] * 8, block
    )
    n_blocks = gather_tokens(normed1)
    w_far = after(w_far, n_blocks[2])
    u_far = after(e_pieces[1][256:], f_got)
    up_blocks = [
        cotangent, move(after(cotangent, f_got), flip_core=1), u_far, move(u_far, flip_core=1)
    ]
    w_pieces = [move(w_near, flip_core=1), w_far, move(w_far[256:], flip_core=1)]

    normed1, up1, act1, ss1, mixed1, b_send, b_keep, send1, keep1, bias1 = call(
        last_layer,
        [place] + n_blocks + up_blocks + [vec, turn, triple, merger, expander, shrinker] + w_pieces,
        [SM] + [VM] * 10 + [HBM] * 4 + [ANY] * 3,
        [full, full, full, shape(512, WIDE), shape(512, 256), full, shape(512, W, dtype=F32)]
        + [send, keep, shape(8, WIDE, dtype=F32)],
        scratch=[
            wide, merge, shrink, pltpu.VMEM((512, 768), BF), pltpu.VMEM((512, 768), F32),
            pltpu.VMEM((512, 256), BF), pltpu.VMEM((512, W), F32), pltpu.SemaphoreType.DMA((9,)),
        ],
        room=14,
        flops=8 * 10**9,
    )
    got1 = move(send1, flip_core=1)
    s0, k0, s2, k2 = weight_one(place, act1, up1, normed1, ss1)
    low1 = (keep1[128:] + after(got1, s0)[128:].astype(F32)).astype(BF)
    far1 = move(low1, flip_z=1)
    s1, k1, s3, k3 = weight_two(after(place, low1), act1, up1, normed1, ss1, mixed1)
    g0, g2 = hops(after((s0, s2), low1), (0, 2), 0)
    slope1, low1, rows1 = call(
        functools.partial(norm_back, layer=1),
        [after(place, s1), state1, cotangent, cotangent, keep1, got1, far1, vec],
        [SM] + [VM] * 7,
        [shape(128, W, dtype=F32), shape(128, W), shape(8, W, dtype=F32)],
    )
    u_blocks = gather_late(low1)
    g1, g3 = hops(after((s1, s3), low1), (1, 3), 0)
    s0, k0, s2, k2 = first_folds(after(place, low1), (k0, k2), (g0, g2), (0, 2))
    one1 = [k0, k2] + hops([s0, s2], (0, 2), 1)

    up0, act0, ss0, send0, keep0, bias0 = call(
        first_back,
        [place] + u_blocks + [before0, qkv0, turn, triple, merger, expander, shrinker]
        + t_pieces + e_pieces,
        [SM] + [VM] * 7 + [HBM] * 4 + [ANY] * 6,
        [full, full, shape(512, WIDE), send, keep, shape(8, WIDE, dtype=F32)],
        scratch=[
            wide, merge, shrink, pltpu.VMEM((512, 768), F32), pltpu.VMEM((512, 256), BF),
            pltpu.SemaphoreType.DMA((12,)),
        ],
        room=14,
        flops=5 * 10**9,
    )
    got0 = move(send0, flip_core=1)
    s0, k0, s2, k2 = weight_one(place, act0, up0, normed0, ss0)
    f1, h1, f3, h3 = first_folds(after(place, s0), (k1, k3), (g1, g3), (1, 3))
    g0, g2 = hops((s0, s2), (0, 2), 0)
    s1, k1, s3, k3 = weight_two(after(place, f1), act0, up0, normed0, ss0, mixed0)
    two1 = [h1, h3] + hops([f1, f3], (1, 3), 1)
    g1, g3 = hops((s1, s3), (1, 3), 0)
    far0 = other(keep0, got0)
    s0, k0, s2, k2 = first_folds(place, (k0, k2), (g0, g2), (0, 2))
    one0 = [k0, k2] + hops([s0, s2], (0, 2), 1)
    units1 = fold_middle(after(place, s0), one1, two1)
    s1, k1, s3, k3 = first_folds(place, (k1, k3), (g1, g3), (1, 3))
    two0 = [k1, k3] + hops([s1, s3], (1, 3), 1)
    units1 = fold_last(after(place, s1), units1)
    input_grad, _, rows0 = call(
        functools.partial(norm_back, layer=0),
        [place, inputs, slope1, low1, keep0, got0, far0, vec],
        [SM] + [VM] * 7,
        [shape(128, W, dtype=F32), shape(128, W), shape(8, W, dtype=F32)],
    )
    (vector,) = call(
        vectors_out, [place, rows0, bias0, rows1, bias1], [SM] + [VM] * 4,
        [shape(32, 512, dtype=F32)], scratch=[pltpu.VMEM((16, W), F32)],
    )
    units0 = fold_middle(after(place, vector), one0, two0)
    terms1 = send_z(after(place, units0[0]), units1, [])
    units0 = fold_last(place, units0)
    pieces1 = sum_z(after(place, units0[0]), terms1)
    every1 = collect_last(after(place, units0[0]), pieces1)
    terms0 = send_z(place, units0, [vector])
    pieces0 = sum_z(place, terms0)
    line0 = line_unit(place, pieces0)
    b_got = move(after(b_send, pieces1[0]), flip_core=1)
    b_low = (
        b_keep.reshape(2, 256, W)[:, 128:] + b_got.reshape(2, 256, W)[:, 128:].astype(F32)
    ).astype(BF)
    b_far = move(b_low.reshape(256, W), flip_z=1)
    hidden_out, squares1 = call(
        functools.partial(join, layer=1),
        [place, state1, b_keep, b_got, b_far, vec],
        [SM] + [VM] * 5,
        [shape(128, W), shape(8, 128, dtype=F32)],
    )

    line0 = line_four(after(place, hidden_out), line0)
    totals = jnp.concatenate([squares0[:3, :1], squares1[:3, :1]]).reshape(1, 6)
    totals = totals + move(totals, flip_core=1)
    totals = totals + move(totals, flip_z=1)
    rms_stats = jnp.sqrt(totals / (length.astype(F32) * W) + 1e-06)
    line0 = line_three(after(place, rms_stats), line0)
    own0, got0 = line_two(place, line0)
    sums1 = put_last(after(every1, own0[0]))
    sums0 = put_sums(place, own0, sums1, [])
    *sums0, g_sum, s_sum, b_sum, b_copy, t_sum, e_sum = put_sums(place, got0, sums0, [own0[0]])
    return (
        hidden_out,
        input_grad,
        g_sum,
        s_sum,
        sums0[0],
        t_sum,
        sums0[1],
        b_sum,
        sums0[2],
        e_sum,
        sums0[3],
        b_copy,
        rms_stats,
    )


def solution(mesh):
    return jax.shard_map(
        body,
        mesh=mesh,
        in_specs=(
            P(("rep", "shard"), None),
            P("rep"),
            P(None, "shard"),
            P(None, "shard"),
            P(None, "shard", None),
            P(None, "shard"),
            P(None, "shard", None),
            P(None, "shard"),
            P(None, "shard", None),
            P(None, "shard"),
            P(None, "shard", None),
            P(None, "shard"),
            P(("rep", "shard"), None),
        ),
        out_specs=(
            P(("rep", "shard"), None),
            P(("rep", "shard"), None),
            P(None, "shard"),
            P(None, "shard"),
            P(None, "shard", None),
            P(None, "shard"),
            P(None, "shard", None),
            P(None, "shard"),
            P(None, "shard", None),
            P(None, "shard"),
            P(None, "shard", None),
            P(None, "shard"),
            P("rep", None),
        ),
        check_vma=False,
    )
```

```python
import functools
import math

import jax
import jax.numpy as jnp
from jax import lax
from jax.experimental import pallas as pl
from jax.experimental.pallas import tpu as pltpu
from jax.sharding import PartitionSpec as P

HD = 64
ROT = 32
LAYERS = 2
EPS_NORM = 1e-05
AXES = ("rep", "shard")
BF = jnp.bfloat16
F32 = jnp.float32
MINE = 4
W = 1024
WIDE = 1792
PART = 768
PAIR = 1536
ORDERS = ((0, 2, 1, 3), (2, 0, 1, 3), (1, 3, 2, 0), (3, 1, 2, 0))

VM = pl.BlockSpec(memory_space=pltpu.VMEM)
ANY = pl.BlockSpec(memory_space=pl.ANY)
HBM = pl.BlockSpec(memory_space=pltpu.HBM)
SM = pl.BlockSpec(memory_space=pltpu.SMEM)


def place_of(index):
    rep, shard = divmod(index, 4)
    x, rest = divmod(rep, 8)
    z_hi, y = divmod(rest, 4)
    z_lo, core = divmod(shard, 2)
    return x, y, z_hi * 2 + z_lo, core


def index_of(x, y, z, core):
    return ((x * 2 + z // 2) * 4 + y) * 4 + (z % 2) * 2 + core


def move(value, flip_x=0, flip_y=0, flip_z=0, flip_core=0):
    pairs = []
    for index in range(128):
        x, y, z, core = place_of(index)
        pairs.append((index, index_of(x ^ flip_x, y ^ flip_y, z ^ flip_z, core ^ flip_core)))
    return lax.ppermute(value, AXES, pairs)


def hop(value, link):
    by = 3 if link & 1 else 1
    return move(value, flip_y=by) if link > 1 else move(value, flip_x=by)


def link_bit(place, link):
    return place[4 + link]


def after(value, *others):
    return lax.optimization_barrier((value,) + others)[0]


def pick(value, index, axis=0):
    return lax.dynamic_index_in_dim(value, index, axis, keepdims=False)


def shape(*dims, dtype=BF):
    return jax.ShapeDtypeStruct(dims, dtype)


def call(body, args, specs, outs, out_specs=None, scratch=(), flops=0, aliases=None, room=3):
    held = sum(math.prod(o.shape) * o.dtype.itemsize for o in outs)
    held += sum(math.prod(a.shape) * a.dtype.itemsize for a, s in zip(args, specs) if s is VM)
    held += sum(math.prod(s.shape) * s.dtype.itemsize for s in scratch if jnp.issubdtype(s.dtype, jnp.floating))
    room = held + (room << 20)
    return pl.pallas_call(
        body,
        out_shape=outs,
        in_specs=specs,
        out_specs=out_specs or [VM] * len(outs),
        scratch_shapes=scratch,
        input_output_aliases=aliases or {},
        compiler_params=pltpu.CompilerParams(vmem_limit_bytes=room),
        cost_estimate=pl.CostEstimate(flops=1, bytes_accessed=1, transcendentals=0),
    )(*args)


def dot(left, right):
    return jnp.dot(left, right, preferred_element_type=F32)


def dot_t(left, right):
    return lax.dot_general(left, right, (((1,), (1,)), ((), ())), preferred_element_type=F32)


def t_dot(left, right):
    return lax.dot_general(left, right, (((0,), (0,)), ((), ())), preferred_element_type=F32)


def copies(pairs, sems):
    started = []
    for at, (source, target) in enumerate(pairs):
        copy = pltpu.make_async_copy(source, target, sems.at[at])
        copy.start()
        started.append(copy)
    return started


def finish(started):
    for copy in started:
        copy.wait()


def lanes(start, size):
    return pl.ds(pl.multiple_of(start, 128), size)


def rows_at(start, size):
    return pl.ds(pl.multiple_of(start, 16), size)


def cut_triple(
    place, gains, shifts, merger_bias, shrinker_bias, triple_bias, triple,
    small, out1, out2, out3, slab, sems,
):
    shard = place[2]
    started = copies([(triple.at[0], slab)], sems)
    narrow = [v[...].astype(F32) for v in (gains, shifts, merger_bias, shrinker_bias)]
    narrow = jnp.concatenate(narrow + [jnp.zeros((8, 256), F32)], axis=0)
    tall = jnp.concatenate(
        [jnp.zeros((8, 768), F32), triple_bias[...].astype(F32), jnp.zeros((6, 768), F32)], axis=0
    )
    both = jnp.concatenate([narrow, jnp.zeros((16, 512), F32)], axis=1) + tall
    small[...] = both.astype(BF)
    for ref in (out1, out2, out3):
        ref[pl.ds(256, 16), :] = both.astype(BF)
    finish(started)
    for k, ref in ((2, out2), (3, out3), (1, out1)):
        for p in range(3):
            ref[pl.ds(0, 256), pl.ds(p * 256, 256)] = slab[:, lanes(p * W + (shard ^ k) * 256, 256)]


def cut_rest(
    place, cotangent, triple, expander, e1, e2, e3, w1, wz, slab, first, second, sems
):
    shard = place[2]
    pairs = [(expander.at[0], first), (expander.at[1], second), (triple.at[1], slab)]
    started = copies(pairs, sems)
    e2[pl.ds(256, 128), :] = cotangent[...]
    started[0].wait()
    for k, ref in ((2, e2), (3, e3), (1, e1)):
        ref[pl.ds(0, 256), :] = first[:, lanes((shard ^ k) * W, W)]
    finish(started[1:])
    for k, ref in ((2, wz.at[pl.ds(0, 256)]), (3, wz.at[pl.ds(256, 256)]), (1, w1)):
        block = shard ^ k
        ref[:, pl.ds(0, W)] = second[:, lanes(block * W, W)]
        for p in range(3):
            ref[:, pl.ds(W + p * 256, 256)] = slab[:, lanes(p * W + block * 256, 256)]


def own_triple(shard, layer, triple, wide):
    return [
        (
            triple.at[layer, :, lanes(p * W + shard * 256, 256)],
            wide.at[rows_at(shard * 256, 256), pl.ds(W + p * 256, 256)],
        )
        for p in range(3)
    ]


def own_expander(shard, layer, expander, wide):
    return [
        (expander.at[layer, :, lanes(shard * W, W)], wide.at[rows_at(shard * 256, 256), pl.ds(0, W)])
    ]


def piece_rows(shard, k, wide):
    return wide.at[rows_at((shard ^ k) * 256, 256)]


def first_triple(shard, pieces, wide):
    return [
        (ref.at[pl.ds(0, 256)], piece_rows(shard, k, wide).at[:, pl.ds(W, 768)])
        for k, ref in zip((1, 2, 3), pieces)
    ]


def first_expander(shard, pieces, wide):
    return [
        (ref.at[pl.ds(0, 256)], piece_rows(shard, k, wide).at[:, pl.ds(0, W)])
        for k, ref in zip((1, 2, 3), pieces)
    ]


def second_wide(shard, pieces, wide):
    one, two, three = pieces
    return [
        (one, piece_rows(shard, 1, wide)),
        (two.at[pl.ds(0, 256)], piece_rows(shard, 2, wide)),
        (three, piece_rows(shard, 3, wide)),
    ]


def spots(shard):
    row = lax.broadcasted_iota(jnp.int32, (512, 1), 0)
    col = lax.broadcasted_iota(jnp.int32, (1, 512), 1)

    def at(i):
        return (((i >> 7) ^ shard) << 7) | (i & 127)

    return at(row), at(col)


def rotate(values, turn, back=False):
    ahead = pltpu.roll(values, 256 - 16, 1) * turn[1]
    behind = pltpu.roll(values, 16, 1) * turn[2]
    if back:
        return values * turn[0] - ahead - behind
    return values * turn[0] + ahead + behind


def normalize(state):
    mean = jnp.mean(state, axis=-1, keepdims=True)
    centred = state - mean
    spread = jnp.mean(centred * centred, axis=-1, keepdims=True)
    factor = lax.rsqrt(spread + EPS_NORM)
    return centred * factor, factor


ROOT = math.sqrt(2.0 / math.pi)


def gelu_both(v):
    square = v * v
    t = jnp.tanh(ROOT * v * (1.0 + 0.044715 * square))
    half = 0.5 * (1.0 + t)
    slope = half + 0.5 * v * (1.0 - t * t) * (ROOT + (3.0 * 0.044715 * ROOT) * square)
    return v * half, slope


def heads_out(normed, wide, bias, turn, qkv):
    scale = HD ** (-0.5)
    for p in range(3):
        part = dot(normed[...], wide[:, pl.ds(W + p * 256, 256)]) + bias[:, pl.ds(p * 256, 256)]
        if p < 2:
            part = rotate(part, turn)
        if p == 0:
            part = part * scale
        qkv[:, pl.ds(p * 256, 256)] = part.astype(BF)


def probabilities(qkv, h, allowed):
    q = qkv[:, pl.ds(h * HD, HD)]
    k = qkv[:, pl.ds(256 + h * HD, HD)]
    scores = jnp.where(allowed, dot_t(q, k), -1000000000.0)
    powered = jnp.exp(scores - jnp.max(scores, axis=-1, keepdims=True))
    return powered * (1.0 / jnp.sum(powered, axis=-1, keepdims=True))


def attend(qkv, allowed, mixed):
    for h in range(MINE):
        low = probabilities(qkv, h, allowed).astype(BF)
        mixed[:, pl.ds(h * HD, HD)] = dot(low, qkv[:, pl.ds(512 + h * HD, HD)]).astype(BF)


def attend_back(qkv, allowed, mixed, slope_mixed, slopes, forward):
    for h in range(MINE):
        probs = probabilities(qkv, h, allowed)
        low = probs.astype(BF)
        q = qkv[:, pl.ds(h * HD, HD)]
        k = qkv[:, pl.ds(256 + h * HD, HD)]
        v = qkv[:, pl.ds(512 + h * HD, HD)]
        if forward:
            mixed[:, pl.ds(h * HD, HD)] = dot(low, v).astype(BF)
        out = slope_mixed[:, pl.ds(h * HD, HD)]
        slope_probs = dot_t(out, v)
        centre = jnp.sum(probs * slope_probs, axis=-1, keepdims=True)
        slope_scores = (probs * (slope_probs - centre)).astype(BF)
        slopes[:, pl.ds(h * HD, HD)] = dot(slope_scores, k)
        slopes[:, pl.ds(256 + h * HD, HD)] = t_dot(slope_scores, q)
        slopes[:, pl.ds(512 + h * HD, HD)] = t_dot(low, out)


def hand_out(left, right, send, keep):
    for n in range(2):
        cols = pl.ds(n * 512, 512)
        part = dot(left[...], right[:, cols])
        spread_out(part, cols, send, keep)


def spread_out(part, cols, send, keep):
    keep[pl.ds(0, 128), cols] = part[0:128]
    send[pl.ds(0, 128), cols] = part[128:256].astype(BF)
    keep[pl.ds(128, 128), cols] = part[256:384]
    send[pl.ds(128, 128), cols] = part[384:512].astype(BF)


def first_attention(
    place, x0, x1, x2, x3, small, bias, turn, triple, merger, t1, t2, t3,
    normed, qkv, mixed, send, keep, vec, wide, merge, smalls, sems,
):
    shard, length = place[2], place[3]
    pairs = [(small, smalls.at[shard])]
    pairs += [(t1.at[pl.ds(256, 16)], smalls.at[shard ^ 1])]
    pairs += [(t2.at[pl.ds(256, 16)], smalls.at[shard ^ 2])]
    pairs += [(t3.at[pl.ds(256, 16)], smalls.at[shard ^ 3])]
    pairs += own_triple(shard, 0, triple, wide) + [(merger.at[0], merge)]
    started = copies(pairs + first_triple(shard, (t1, t2, t3), wide), sems)
    for copy in started[:4]:
        copy.wait()
    vec[...] = jnp.zeros_like(vec)
    for j in range(4):
        vec[pl.ds(0, 8), pl.ds(j * 256, 256)] = smalls[j].astype(F32)[0:8, 0:256]
    for p in range(3):
        block = p * 4 + shard
        j = (block * 11) >> 5
        vec[pl.ds(8, 2), pl.ds(p * 256, 256)] = smalls[j, :, lanes((block - 3 * j) * 256, 256)].astype(
            F32
        )[8:10]
    vec[pl.ds(10, 2), :] = bias[...].astype(F32)
    gain, shift = vec[pl.ds(0, 1), :], vec[pl.ds(2, 1), :]
    for k, ref in enumerate((x0, x1, x2, x3)):
        hat, _ = normalize(ref[...].astype(F32))
        normed[pl.ds(k * 128, 128), :] = (hat * gain + shift).astype(BF)
    finish(started[4:])
    row, col = spots(shard)
    allowed = (col <= row) & (col < length)
    heads_out(normed, wide, vec[pl.ds(8, 1), pl.ds(0, 768)], turn, qkv)
    attend(qkv, allowed, mixed)
    hand_out(mixed, merge, send, keep)


def first_forward(
    place, normed, vec, expander, shrinker, e1, e2, e3,
    before, send, keep, wide, shrink, act, sems,
):
    shard = place[2]
    pairs = own_expander(shard, 0, expander, wide) + first_expander(shard, (e1, e2, e3), wide)
    started = copies(pairs + [(shrinker.at[0], shrink)], sems)
    finish(started)
    for n in range(2):
        cols = pl.ds(n * 512, 512)
        part = dot(normed[...], wide[:, cols]) + vec[pl.ds(10, 1), cols]
        before[:, cols] = part
        act[:, cols] = gelu_both(part)[0].astype(BF)
    hand_out(act, shrink, send, keep)


def slopes_out(ss, bias, wide, send, keep):
    bias[...] = jnp.broadcast_to(jnp.sum(ss[...].astype(F32), axis=0, keepdims=True), bias.shape)
    for n in range(2):
        part = dot_t(ss[...], wide[pl.ds(n * 512, 512), :])
        spread_out(part, pl.ds(n * 512, 512), send, keep)


def triple_slopes(slopes, turn, ss):
    scale = HD ** (-0.5)
    ss[:, pl.ds(W, 256)] = (rotate(slopes[:, pl.ds(0, 256)], turn, True) * scale).astype(BF)
    ss[:, pl.ds(W + 256, 256)] = rotate(slopes[:, pl.ds(256, 256)], turn, True).astype(BF)
    ss[:, pl.ds(W + 512, 256)] = slopes[:, pl.ds(512, 256)].astype(BF)


def last_layer(
    place, n0, n1, n2, n3, u0, u1, u2, u3, vec, turn, triple, merger, expander, shrinker, w1, w2, w3,
    normed, up, act, ss, mixed, bsend, bkeep, send, keep, bias,
    wide, merge, shrink, qkv, slopes, out, sems,
):
    shard, length = place[2], place[3]
    pairs = own_triple(shard, 1, triple, wide) + own_expander(shard, 1, expander, wide)
    pairs += second_wide(shard, (w1, w2, w3), wide) + [(merger.at[1], merge), (shrinker.at[1], shrink)]
    started = copies(pairs, sems)
    row, col = spots(shard)
    for k, (n, u) in enumerate(((n0, u0), (n1, u1), (n2, u2), (n3, u3))):
        rows = pl.ds(k * 128, 128)
        normed[rows, :] = n[...]
        up[rows, :] = jnp.where(row[k * 128 : k * 128 + 128] < length, u[...].astype(F32), 0.0).astype(BF)
    finish(started)
    for n in range(2):
        cols = pl.ds(n * 512, 512)
        part = dot(normed[...], wide[:, cols]) + vec[pl.ds(11, 1), cols]
        value, slope = gelu_both(part)
        act[:, cols] = value.astype(BF)
        ss[:, cols] = (dot_t(up[...], shrink[cols, :]) * slope).astype(BF)
    hand_out(act, shrink, bsend.at[pl.ds(256, 256)], bkeep.at[pl.ds(256, 256)])
    allowed = (col <= row) & (col < length)
    heads_out(normed, wide, vec[pl.ds(9, 1), pl.ds(0, 768)], turn, qkv)
    out[...] = dot_t(up[...], merge[...]).astype(BF)
    attend_back(qkv, allowed, mixed, out, slopes, True)
    hand_out(mixed, merge, bsend.at[pl.ds(0, 256)], bkeep.at[pl.ds(0, 256)])
    triple_slopes(slopes, turn, ss)
    slopes_out(ss, bias, wide, send, keep)


def first_back(
    place, u0, u1, u2, u3, before, qkv, turn, triple, merger, expander, shrinker,
    t1, t2, t3, e1, e2, e3,
    up, act, ss, send, keep, bias, wide, merge, shrink, slopes, out, sems,
):
    shard, length = place[2], place[3]
    pairs = own_triple(shard, 0, triple, wide) + own_expander(shard, 0, expander, wide)
    pairs += first_triple(shard, (t1, t2, t3), wide)
    pairs += first_expander(shard, (e1, e2, e3), wide)
    started = copies(pairs + [(merger.at[0], merge), (shrinker.at[0], shrink)], sems)
    for k, u in enumerate((u0, u1, u2, u3)):
        up[pl.ds(k * 128, 128), :] = u[...]
    finish(started)
    for n in range(2):
        cols = pl.ds(n * 512, 512)
        value, slope = gelu_both(before[:, cols])
        act[:, cols] = value.astype(BF)
        ss[:, cols] = (dot_t(up[...], shrink[cols, :]) * slope).astype(BF)
    row, col = spots(shard)
    allowed = (col <= row) & (col < length)
    out[...] = dot_t(up[...], merge[...]).astype(BF)
    attend_back(qkv, allowed, None, out, slopes, False)
    triple_slopes(slopes, turn, ss)
    slopes_out(ss, bias, wide, send, keep)


def halve(term, cols, o, bit, send, keep, at):
    for ref, half in ((keep, bit), (send, 1 - bit)):
        value = term[pl.ds(pl.multiple_of(half * 128, 128), 128), cols].astype(BF)
        for k in range(8):
            ref[pl.ds(k * 64 + o * 16, 16), at] = value[k * 16 : k * 16 + 16]


def terms_one(place, act, up, normed, ss, s0, k0, s2, k2, term):
    whole = pl.ds(0, PART)
    for o in range(4):
        cols = pl.ds(o * 256, 256)
        term[...] = t_dot(act[:, cols], up[:, pl.ds(0, PART)])
        halve(term, whole, o, link_bit(place, ORDERS[0][0]), s0, k0, whole)
        term[...] = t_dot(normed[:, cols], ss[:, pl.ds(0, PART)])
        halve(term, whole, o, link_bit(place, ORDERS[2][0]), s2, k2, whole)


def terms_two(place, act, up, normed, ss, mixed, s1, k1, s3, k3, term, last):
    one, three = link_bit(place, ORDERS[1][0]), link_bit(place, ORDERS[3][0])
    whole = pl.ds(0, PART)
    last[...] = t_dot(mixed[...], up[...])
    for o in range(4):
        cols = pl.ds(o * 256, 256)
        term[:, pl.ds(0, 256)] = t_dot(act[:, cols], up[:, pl.ds(PART, 256)])
        term[:, pl.ds(256, 256)] = last[:, cols]
        both = t_dot(normed[:, cols], ss[:, pl.ds(PART, W)])
        term[:, pl.ds(512, 256)] = both[:, 256:512]
        halve(term, whole, o, one, s1, k1, whole)
        term[:, pl.ds(0, 256)] = both[:, 0:256]
        term[:, pl.ds(256, 512)] = both[:, 512:W]
        halve(term, whole, o, three, s3, k3, whole)


def weight_one(place, act, up, normed, ss):
    return call(
        terms_one, [place, act, up, normed, ss], [SM] + [VM] * 4, [shape(512, PART)] * 4,
        scratch=[pltpu.VMEM((256, PART), F32)], flops=2 * 10**9,
    )


def weight_two(place, act, up, normed, ss, mixed):
    return call(
        terms_two, [place, act, up, normed, ss, mixed], [SM] + [VM] * 5, [shape(512, PART)] * 4,
        scratch=[pltpu.VMEM((256, PART), F32), pltpu.VMEM((256, W), F32)], flops=2 * 10**9,
    )


def join(place, state, *refs, layer):
    shard, length = place[2], place[3]
    spot = shard * 128 + lax.broadcasted_iota(jnp.int32, (128, 1), 0)
    valid = (spot < length).astype(F32)
    if layer == 0:
        ak, ag, az, fk, fg, fz, vec, new, out, squares = refs
        attended = ak[pl.ds(0, 128), :] + ag[pl.ds(0, 128), :].astype(F32) + az[...].astype(F32)
        branch = fk[pl.ds(0, 128), :] + fg[pl.ds(0, 128), :].astype(F32) + fz[...].astype(F32)
    else:
        kept, got, far, vec, out, squares = refs
        attended, branch = [
            kept[pl.ds(at * 256, 128), :]
            + got[pl.ds(at * 256, 128), :].astype(F32)
            + far[pl.ds(at * 128, 128), :].astype(F32)
            for at in (0, 1)
        ]
    attended = attended + vec[pl.ds(4 + layer, 1), :]
    branch = branch + vec[pl.ds(6 + layer, 1), :]
    old = state[...].astype(F32)
    for at, item in enumerate((old, attended, branch)):
        total = jnp.sum(jnp.sum(item * item, axis=1, keepdims=True) * valid)
        squares[pl.ds(at, 1), :] = jnp.full((1, 128), total, F32)
    state_new = old + attended + branch
    if layer == 0:
        new[...] = state_new
        hat, _ = normalize(state_new)
        out[...] = (hat * vec[pl.ds(1, 1), :] + vec[pl.ds(3, 1), :]).astype(BF)
    else:
        out[...] = (state_new * valid).astype(BF)


def norm_back(place, state, slope, up, sk, sg, sz, vec, new, low, rows, *, layer):
    shard, length = place[2], place[3]
    spot = shard * 128 + lax.broadcasted_iota(jnp.int32, (128, 1), 0)
    given = slope[...].astype(F32)
    upstream = up[...].astype(F32)
    if layer == LAYERS - 1:
        given = jnp.where(spot < length, given, 0.0)
        upstream = given
    sn = sk[pl.ds(0, 128), :] + sg[pl.ds(0, 128), :].astype(F32) + sz[...].astype(F32)
    hat, factor = normalize(state[...].astype(F32))
    rows[...] = jnp.zeros_like(rows)
    rows[pl.ds(0, 1), :] = jnp.sum(sn * hat, axis=0, keepdims=True)
    rows[pl.ds(1, 1), :] = jnp.sum(sn, axis=0, keepdims=True)
    rows[pl.ds(2, 1), :] = jnp.sum(upstream, axis=0, keepdims=True)
    d = sn * vec[pl.ds(layer, 1), :]
    mean = jnp.mean(d, axis=-1, keepdims=True)
    along = jnp.mean(d * hat, axis=-1, keepdims=True)
    result = given + factor * (d - mean - hat * along)
    new[...] = result
    low[...] = result.astype(BF)


def vectors_out(place, rows0, bias0, rows1, bias1, out, full):
    shard = place[2]
    full[...] = jnp.zeros_like(full)
    for at, (rows, bias) in enumerate(((rows0, bias0), (rows1, bias1))):
        base = at * 7
        full[pl.ds(base, 3), :] = rows[pl.ds(0, 3), :]
        for p in range(3):
            full[pl.ds(base + 3 + p, 1), lanes(shard * 256, 256)] = bias[
                pl.ds(0, 1), pl.ds(W + p * 256, 256)
            ]
        full[pl.ds(base + 6, 1), :] = bias[pl.ds(0, 1), pl.ds(0, W)]
    out[pl.ds(0, 16), :] = full[:, pl.ds(0, 512)]
    out[pl.ds(16, 16), :] = full[:, pl.ds(512, 512)]


def add_half(kept, got, bit, refs, at):
    size = kept.shape[0] // 2
    for ref, half in zip(refs, (1 - bit, bit)):
        rows = rows_at(half * size, size)
        total = kept[rows, :].astype(F32) + got[rows, :].astype(F32)
        ref[:, at] = total.astype(BF)


def fold_one(place, ka, ga, kb, gb, sa, ha, sb, hb, *, parts):
    for part, (k, g, s, h) in zip(parts, ((ka, ga, sa, ha), (kb, gb, sb, hb))):
        add_half(k, g, link_bit(place, ORDERS[part][1]), (s, h), slice(None))


def fold_two(place, k0, g0, k1, g1, k2, g2, k3, g3, sa, ha, sb, hb):
    for part, (k, g) in enumerate(((k0, g0), (k1, g1), (k2, g2), (k3, g3))):
        refs = (sb, hb) if part > 1 else (sa, ha)
        at = pl.ds((part & 1) * PART, PART)
        add_half(k, g, link_bit(place, ORDERS[part][2]), refs, at)


def fold_three(place, ka, ga, kb, gb, sa, ha, sb, hb):
    for part, (k, g, s, h) in zip((0, 2), ((ka, ga, sa, ha), (kb, gb, sb, hb))):
        add_half(k, g, link_bit(place, ORDERS[part][3]), (s, h), slice(None))


def first_folds(place, kept, got, parts):
    args = [kept[0], got[0], kept[1], got[1]]
    return call(
        functools.partial(fold_one, parts=parts), [place] + args, [SM] + [VM] * 4, [shape(256, PART)] * 4
    )


def z_send(place, *refs):
    ka, ga, kb, gb, *refs = refs
    shard = place[2]
    z_lo = shard >> 1
    if len(refs) == 6:
        vector, *refs = refs
    else:
        vector = None
    side, across, cross, plain, wide = refs
    a = ka[...].astype(F32) + ga[...].astype(F32)
    b = kb[...].astype(F32) + gb[...].astype(F32)
    wide[:, pl.ds(0, W)] = b[:, 0:W]
    wide[:, pl.ds(W, 256)] = a[:, 1280:PAIR]
    wide[:, pl.ds(1280, 512)] = b[:, W:PAIR]
    plain[...] = a[:, 0:1280]
    cross[...] = wide[rows_at(z_lo * 32, 32), :]
    side[:, pl.ds(0, WIDE)] = wide[rows_at((1 - z_lo) * 32, 32), :].astype(BF)
    across[:, pl.ds(0, WIDE)] = cross[...].astype(BF)
    across[:, pl.ds(WIDE, 1280)] = plain[pl.ds(0, 32), :].astype(BF)
    across[:, pl.ds(WIDE + 1280, 1280)] = plain[pl.ds(32, 32), :].astype(BF)
    if vector is not None:
        side[:, pl.ds(WIDE, 512)] = vector[...].astype(BF)
        across[:, pl.ds(WIDE + 2560, 512)] = vector[...].astype(BF)


def local_rows():
    row = lax.broadcasted_iota(jnp.int32, (32, 1), 0) & 15
    return (row == 6) | (row == 13)


def z_sum(place, *refs):
    cross, plain, za, zb, z2, *refs = refs
    vector = None
    if len(refs) == 6:
        vector, *refs = refs
        near, kept, whole, vec, both = refs
    else:
        near, kept, whole, both = refs
    core = place[2] & 1
    both[pl.ds(0, 32), :] = cross[...] + z2[:, pl.ds(0, WIDE)].astype(F32)
    both[pl.ds(32, 32), :] = za[:, pl.ds(0, WIDE)].astype(F32) + zb[:, pl.ds(0, WIDE)].astype(F32)
    for at in range(2):
        own = both[rows_at(at * 32 + core * 16, 16), :]
        other = both[rows_at(at * 32 + (1 - core) * 16, 16), :]
        kept[pl.ds(at * 16, 16), :] = own.astype(BF)
        near[pl.ds(at * 16, 16), pl.ds(0, WIDE)] = other.astype(BF)
    for at in range(2):
        rows = pl.ds(at * 32, 32)
        got = z2[:, pl.ds(WIDE + at * 1280, 1280)].astype(F32)
        whole[rows, :] = (plain[rows, :] + got).astype(BF)
    if vector is not None:
        sides = za[:, pl.ds(WIDE, 512)].astype(F32) + zb[:, pl.ds(WIDE, 512)].astype(F32)
        total = vector[...] + z2[:, pl.ds(WIDE + 2560, 512)].astype(F32)
        total = total + jnp.where(local_rows(), 0.0, sides)
        vec[...] = total
        near[:, pl.ds(WIDE, 512)] = total.astype(BF)


def payload_parts(place, kept, near, whole, a, b):
    shard = place[2]
    for k in range(4):
        rows = rows_at((shard ^ k) * 16, 16)
        ref, at = (near, k >> 1) if k & 1 else (kept, k >> 1)
        source = ref[pl.ds(at * 16, 16), pl.ds(0, WIDE)]
        b[rows, pl.ds(0, W)] = source[:, 0:W]
        a[rows, pl.ds(1280, 256)] = source[:, W:1280]
        b[rows, pl.ds(W, 512)] = source[:, 1280:WIDE]
    a[pl.ds(0, 64), pl.ds(0, 1280)] = whole[...]


def payload_both(place, kept, near, whole, out):
    payload_parts(place, kept, near, whole, out.at[pl.ds(0, 64)], out.at[pl.ds(64, 64)])


def payload(place, kept, near, whole, *refs):
    *vec, a, b = refs
    payload_parts(place, kept, near, whole, a, b)
    if not vec:
        return
    vec = vec[0]
    total = vec[...] + jnp.where(local_rows(), 0.0, near[:, pl.ds(WIDE, 512)].astype(F32))
    low = total.astype(BF)
    a[pl.ds(64, 16), :] = jnp.zeros((16, PAIR), BF)
    a[pl.ds(64, 16), pl.ds(0, 512)] = low[0:16]
    a[pl.ds(64, 16), pl.ds(512, 512)] = low[16:32]


def line_up(own, got, bit, size, outs, cols):
    for ref, at in zip(outs, cols):
        ref[rows_at(bit * size, size), :] = own[pl.ds(0, size), at]
        ref[rows_at((1 - bit) * size, size), :] = got[pl.ds(0, size), at]


def vector_rows(own, got, at, size):
    rows = pl.ds(at, size)
    return (own[rows, :].astype(F32) + got[rows, :].astype(F32)).astype(BF)


def gather_four(place, oa, ga, ob, gb, a, b):
    line_up(oa, ga, link_bit(place, ORDERS[0][3]), 64, [a], [slice(None)])
    line_up(ob, gb, link_bit(place, ORDERS[2][3]), 64, [b], [slice(None)])
    if a.shape[0] > 128:
        a[pl.ds(128, 16), :] = vector_rows(oa, ga, 64, 16)


def gather_three(place, oa, ga, ob, gb, p0, p1, p2, p3):
    cols = [pl.ds(0, PART), pl.ds(PART, PART)]
    line_up(oa, ga, link_bit(place, ORDERS[0][2]), 128, [p0, p1], cols)
    line_up(ob, gb, link_bit(place, ORDERS[2][2]), 128, [p2, p3], cols)
    if p0.shape[0] == 256:
        return
    low = vector_rows(oa, ga, 128, 16)
    p0[pl.ds(256, 32), :] = jnp.zeros((32, PART), BF)
    p0[pl.ds(256, 16), pl.ds(0, 512)] = low[:, 0:512]
    p0[pl.ds(272, 16), pl.ds(0, 512)] = low[:, 512:W]


def gather_two(place, o0, g0, o1, g1, o2, g2, o3, g3, p0, p1, p2, p3):
    outs = (p0, p1, p2, p3)
    for part, (o, g) in enumerate(((o0, g0), (o1, g1), (o2, g2), (o3, g3))):
        line_up(o, g, link_bit(place, ORDERS[part][1]), 256, [outs[part]], [slice(None)])
    p0[pl.ds(512, 32), :] = vector_rows(o0, g0, 256, 32)


def each(count, step):
    lax.fori_loop(0, count, lambda at, none: step(at) or none, 0)


def put(part, value, o, base, t, m, e, s):
    rows = rows_at(base, 16)
    if part == 0:
        s[rows_at(o * 256 + base, 16), pl.ds(0, PART)] = value
    elif part == 1:
        s[rows_at(o * 256 + base, 16), pl.ds(PART, 256)] = value[:, 0:256]
        m[rows, pl.ds(o * 256, 256)] = value[:, 256:512]
        t[rows, pl.ds(o * 256, 256)] = value[:, 512:PART]
    elif part == 2:
        e[rows, pl.ds(o * W, PART)] = value
    else:
        e[rows, pl.ds(o * W + PART, 256)] = value[:, 0:256]
        t[rows, pl.ds(W + o * 256, 256)] = value[:, 256:512]
        t[rows, pl.ds(2 * W + o * 256, 256)] = value[:, 512:PART]


def assemble_last(every, t_out, m_out, e_out, s_out, t, m, e, s, sems):
    def device(at):
        x, y = at >> 2, at & 3
        bits = ((x & 1) ^ (x >> 1), x >> 1, (y & 1) ^ (y >> 1), y >> 1)
        for part in range(4):
            unit = sum(bits[link] << (3 - n) for n, link in enumerate(ORDERS[part]))
            for o in range(4):
                rows = rows_at(at * 128 + (part >> 1) * 64 + o * 16, 16)
                value = every[rows, pl.ds((part & 1) * PART, PART)].astype(F32)
                put(part, value, o, unit * 16, t, m, e, s)

    each(16, device)
    pairs = [(t, t_out.at[1]), (m, m_out.at[1]), (e, e_out.at[1]), (s, s_out.at[1])]
    finish(copies(pairs, sems))


def put_half(place, p0, p1, p2, p3, *refs, mine):
    if not mine:
        old, *refs = refs
        t_out, m_out, e_out, s_out, *sums, s0, s1, m1, t1, e2, e3, t3, both, vec, sems = refs[4:]
    else:
        t_out, m_out, e_out, s_out, s0, s1, m1, t1, e2, e3, t3, sems = refs[4:]
    pairs = []
    for part, ref in enumerate((p0, p1, p2, p3)):
        half = link_bit(place, ORDERS[part][0])
        base = (half if mine else 1 - half) * 128
        rows = rows_at(base, 128)
        for o in range(4):
            for k in range(8):
                value = ref[pl.ds(k * 64 + o * 16, 16), :].astype(F32)
                at = pl.ds(k * 16, 16)
                if part == 0:
                    s0[o, at, :] = value
                elif part == 1:
                    s1[o, at, :] = value[:, 0:256]
                    m1[at, pl.ds(o * 256, 256)] = value[:, 256:512]
                    t1[at, pl.ds(o * 256, 256)] = value[:, 512:PART]
                elif part == 2:
                    e2[o, at, :] = value
                else:
                    e3[o, at, :] = value[:, 0:256]
                    t3[at, pl.ds(o * 256, 256)] = value[:, 256:512]
                    t3[at, pl.ds(W + o * 256, 256)] = value[:, 512:PART]
            if part < 2:
                target = s_out.at[0, rows_at(o * 256 + base, 128)]
                pairs.append((s0.at[o], target.at[:, pl.ds(0, PART)]) if part == 0 else (s1.at[o], target.at[:, pl.ds(PART, 256)]))
            else:
                target = e_out.at[0, rows]
                pairs.append((e2.at[o], target.at[:, pl.ds(o * W, PART)]) if part == 2 else (e3.at[o], target.at[:, pl.ds(o * W + PART, 256)]))
        if part == 1:
            pairs.append((m1, m_out.at[0, rows]))
            pairs.append((t1, t_out.at[0, rows, pl.ds(0, W)]))
        if part == 3:
            pairs.append((t3, t_out.at[0, rows, pl.ds(W, 2 * W)]))
    started = copies(pairs, sems)
    if not mine:
        fetch = copies([(old.at[pl.ds(512, 32)], both)], sems.at[pl.ds(len(pairs), 1)])
        finish(fetch)
        low = both[...].astype(F32) + p0[pl.ds(512, 32), :].astype(F32)
        vec[:, pl.ds(0, 512)] = low[0:16, 0:512]
        vec[:, pl.ds(512, 512)] = low[16:32, 0:512]
        for at in range(LAYERS):
            own_sums(vec, at, place[2], *sums)
    finish(started)


def own_sums(vec, layer, shard, g_sum, s_sum, b_sum, b_copy, t_sum, e_sum):
    base = layer * 7
    row = pl.ds(layer, 1)
    for at, ref in ((0, g_sum), (1, s_sum), (2, b_sum), (2, b_copy)):
        ref[row, :] = vec[pl.ds(base + at, 1), lanes(shard * 256, 256)]
    for r in range(3):
        block = shard * 3 + r
        t_sum[row, pl.ds(r * 256, 256)] = vec[
            pl.ds(base + 3 + (block >> 2), 1), lanes((block & 3) * 256, 256)
        ]
    e_sum[row, :] = vec[pl.ds(base + 6, 1), :]


def hops(values, parts, phase):
    return [hop(value, ORDERS[part][phase]) for value, part in zip(values, parts)]


def fold_middle(place, one, two):
    kept = [one[0], two[0], one[1], two[1]]
    got = [one[2], two[2], one[3], two[3]]
    args = [v for pair in zip(kept, got) for v in pair]
    sa, ka, sb, kb = call(fold_two, [place] + args, [SM] + [VM] * 8, [shape(128, PAIR)] * 4)
    ga, gb = hops([sa, sb], (0, 2), 2)
    return [ka, ga, kb, gb]


def fold_last(place, units):
    sa, ka, sb, kb = call(fold_three, [place] + units, [SM] + [VM] * 4, [shape(64, PAIR)] * 4)
    ga, gb = hops([sa, sb], (0, 2), 3)
    return [ka, ga, kb, gb]


def send_z(place, units, vector):
    more = 512 * len(vector)
    side, across, cross, plain = call(
        z_send, [place] + units + vector, [SM] + [VM] * (4 + len(vector)),
        [
            shape(32, WIDE + more), shape(32, WIDE + 2560 + more),
            shape(32, WIDE, dtype=F32), shape(64, 1280, dtype=F32),
        ],
        scratch=[pltpu.VMEM((64, WIDE), F32)],
    )
    z2 = move(across, flip_z=2)
    za = move(side, flip_z=1)
    zb = move(side, flip_z=3)
    return [cross, plain, za, zb, z2] + vector


def sum_z(place, terms):
    vectors = len(terms) - 5
    near, kept, whole, *vec = call(
        z_sum, [place] + terms, [SM] + [VM] * len(terms),
        [shape(32, WIDE + 512 * vectors), shape(32, WIDE), shape(64, 1280)]
        + [shape(32, 512, dtype=F32)] * vectors,
        scratch=[pltpu.VMEM((64, WIDE), F32)],
    )
    return [kept, move(near, flip_core=1), whole] + vec


OUTS = [
    shape(LAYERS, 256, 3072, dtype=F32),
    shape(LAYERS, 256, 1024, dtype=F32),
    shape(LAYERS, 256, 4096, dtype=F32),
    shape(LAYERS, 1024, 1024, dtype=F32),
]


def line_unit(place, pieces):
    rows = 80 if len(pieces) == 4 else 64
    a, b = call(
        payload, [place] + pieces, [SM] + [VM] * len(pieces), [shape(rows, PAIR), shape(64, PAIR)]
    )
    ga, gb = hops([a, b], (0, 2), 3)
    return [a, ga, b, gb]


def line_four(place, args):
    rows = args[0].shape[0] + 64
    a, b = call(gather_four, [place] + args, [SM] + [VM] * 4, [shape(rows, PAIR), shape(128, PAIR)])
    ga, gb = hops([a, b], (0, 2), 2)
    return [a, ga, b, gb]


def line_three(place, args):
    rows = 288 if args[0].shape[0] > 128 else 256
    own = call(
        gather_three, [place] + args, [SM] + [VM] * 4, [shape(rows, PART)] + [shape(256, PART)] * 3
    )
    got = hops(own, range(4), 1)
    return [v for pair in zip(own, got) for v in pair]


def line_two(place, args):
    own = call(
        gather_two, [place] + args, [SM] + [VM] * 8, [shape(544, PART)] + [shape(512, PART)] * 3
    )
    return list(own), hops(own, range(4), 0)


def collect_last(place, pieces):
    (both,) = call(payload_both, [place] + pieces, [SM] + [VM] * 3, [shape(128, PAIR)])
    planes = [[(x * 2 + z) * 4 + y for x in range(4) for y in range(4)] for z in range(2)]
    return lax.all_gather(both, "rep", axis_index_groups=planes, axis=0, tiled=True)


def put_last(every):
    return call(
        assemble_last, [every], [VM], OUTS, out_specs=[ANY] * 4,
        scratch=[pltpu.VMEM(out.shape[1:], F32) for out in OUTS] + [pltpu.SemaphoreType.DMA((4,))],
    )


def put_sums(place, parts, earlier, old):
    outs, specs = list(OUTS), [ANY] * 4
    scratch = [
        pltpu.VMEM((4, 128, PART), F32), pltpu.VMEM((4, 128, 256), F32), pltpu.VMEM((128, W), F32),
        pltpu.VMEM((128, W), F32), pltpu.VMEM((4, 128, PART), F32), pltpu.VMEM((4, 128, 256), F32),
        pltpu.VMEM((128, 2 * W), F32),
    ]
    if old:
        outs += [shape(LAYERS, n, dtype=F32) for n in (256, 256, 256, 256, 768, 1024)]
        specs += [VM] * 6
        scratch += [pltpu.VMEM((32, PART), BF), pltpu.VMEM((16, W), F32)]
    return call(
        functools.partial(put_half, mine=not old), [place] + parts + old + list(earlier),
        [SM] + [VM] * 4 + [ANY] * (4 + len(old)), outs, out_specs=specs,
        scratch=scratch + [pltpu.SemaphoreType.DMA((20,))],
        aliases={5 + len(old) + i: i for i in range(4)},
    )


def gather_tokens(own):
    far = move(own, flip_z=1)
    near = move(own, flip_core=1)
    return [own, near, far, move(far, flip_core=1)]


def gather_late(own):
    far = move(own, flip_z=1)
    return [own, move(after(own, far), flip_core=1), far, move(far, flip_core=1)]


def body(
    inputs,
    lengths,
    gains,
    shifts,
    triple,
    triple_bias,
    merger,
    merger_bias,
    expander,
    expander_bias,
    shrinker,
    shrinker_bias,
    cotangent,
):
    rep = lax.axis_index("rep")
    shard = lax.axis_index("shard")
    length = lengths[0]
    x, y = rep // 8, rep % 4
    place = [x, y, shard, length, (x & 1) ^ (x >> 1), x >> 1, (y & 1) ^ (y >> 1), y >> 1]
    place = jnp.stack(place).astype(jnp.int32)

    small, *pieces = call(
        cut_triple,
        [place, gains, shifts, merger_bias, shrinker_bias, triple_bias, triple],
        [SM] + [VM] * 5 + [HBM],
        [shape(16, 768)] + [shape(272, 768)] * 3,
        scratch=[pltpu.VMEM((256, 3072), BF), pltpu.SemaphoreType.DMA((1,))],
    )

    def recut(one, two, three):
        return [
            move(one, flip_core=1),
            move(two, flip_z=1),
            move(three, flip_z=3, flip_core=1),
        ]

    t_pieces = recut(*pieces)
    x_blocks = gather_tokens(after(inputs, small))
    cut = call(
        cut_rest, [after(place, pieces[0], x_blocks[1]), cotangent, triple, expander],
        [SM, VM, HBM, HBM],
        [shape(256, W), shape(384, W), shape(256, W)]
        + [shape(256, WIDE), shape(512, WIDE)],
        scratch=[
            pltpu.VMEM((256, 3072), BF), pltpu.VMEM((256, 4096), BF), pltpu.VMEM((256, 4096), BF),
            pltpu.SemaphoreType.DMA((3,)),
        ],
    )
    e_pieces = recut(*after(tuple(cut[:2]), x_blocks[2]), after(cut[2], t_pieces[2]))

    spot = after(jnp.arange(512, dtype=jnp.int32), x_blocks[1])
    spot = (((spot >> 7) ^ shard) << 7) | (spot & 127)
    index = jnp.arange(ROT // 2, dtype=F32)
    freq = jnp.exp(index * (-2.0 * math.log(10000.0) / ROT))
    lane = jnp.arange(256, dtype=jnp.int32) % HD
    phase = spot.astype(F32)[:, None] * jnp.tile(freq, 16)[None, :]
    cosine, sine = jnp.cos(phase), jnp.sin(phase)
    turn = jnp.stack(
        [
            jnp.where(lane < ROT, cosine, 1.0),
            jnp.where(lane < ROT // 2, -sine, 0.0),
            jnp.where((lane >= ROT // 2) & (lane < ROT), sine, 0.0),
        ]
    )

    full = shape(512, W)
    send, keep = shape(256, W), shape(256, W, dtype=F32)
    wide = pltpu.VMEM((W, WIDE), BF)
    merge, shrink = pltpu.VMEM((256, W), BF), pltpu.VMEM((W, W), BF)

    normed0, qkv0, mixed0, a_send, a_keep, vec = call(
        first_attention,
        [place] + x_blocks + [small, expander_bias, turn, triple, merger] + t_pieces,
        [SM] + [VM] * 4 + [ANY, VM, VM, HBM, HBM] + [ANY] * 3,
        [full, shape(512, 768), shape(512, 256), send, keep, shape(16, W, dtype=F32)],
        scratch=[wide, merge, pltpu.VMEM((4, 16, 768), BF), pltpu.SemaphoreType.DMA((11,))],
        room=9,
        flops=2 * 10**9,
    )
    a_got = move(after(a_send, e_pieces[1]), flip_core=1)
    w_near, w_far = after(tuple(cut[3:]), e_pieces[2], turn)
    w_far = move(w_far, flip_z=3)
    before0, f_send, f_keep = call(
        first_forward,
        [place, normed0, vec, expander, shrinker] + e_pieces,
        [SM, VM, VM, HBM, HBM] + [ANY] * 3,
        [shape(512, W, dtype=F32), send, keep],
        scratch=[wide, shrink, pltpu.VMEM((512, W), BF), pltpu.SemaphoreType.DMA((5,))],
        room=9,
        flops=2 * 10**9,
    )
    f_got = move(f_send, flip_core=1)

    def other(kept, got):
        return move((kept[128:] + got[128:].astype(F32)).astype(BF), flip_z=1)

    a_far = other(a_keep, a_got)
    sums = [a_keep, a_got, a_far, f_keep, f_got, other(f_keep, f_got)]
    block = [shape(128, W, dtype=F32), shape(128, W), shape(8, 128, dtype=F32)]
    state1, normed1, squares0 = call(
        functools.partial(join, layer=0), [place, inputs] + sums + [vec], [SM] + [VM] * 8, block
    )
    n_blocks = gather_tokens(normed1)
    w_far = after(w_far, n_blocks[2])
    u_far = after(e_pieces[1][256:], f_got)
    up_blocks = [
        cotangent, move(after(cotangent, f_got), flip_core=1), u_far, move(u_far, flip_core=1)
    ]
    w_pieces = [move(w_near, flip_core=1), w_far, move(w_far[256:], flip_core=1)]

    normed1, up1, act1, ss1, mixed1, b_send, b_keep, send1, keep1, bias1 = call(
        last_layer,
        [place] + n_blocks + up_blocks + [vec, turn, triple, merger, expander, shrinker] + w_pieces,
        [SM] + [VM] * 10 + [HBM] * 4 + [ANY] * 3,
        [full, full, full, shape(512, WIDE), shape(512, 256), full, shape(512, W, dtype=F32)]
        + [send, keep, shape(8, WIDE, dtype=F32)],
        scratch=[
            wide, merge, shrink, pltpu.VMEM((512, 768), BF), pltpu.VMEM((512, 768), F32),
            pltpu.VMEM((512, 256), BF), pltpu.SemaphoreType.DMA((9,)),
        ],
        room=9,
        flops=8 * 10**9,
    )
    got1 = move(send1, flip_core=1)
    s0, k0, s2, k2 = weight_one(place, act1, up1, normed1, ss1)
    low1 = (keep1[128:] + after(got1, s0)[128:].astype(F32)).astype(BF)
    far1 = move(low1, flip_z=1)
    s1, k1, s3, k3 = weight_two(after(place, low1), act1, up1, normed1, ss1, mixed1)
    g0, g2 = hops(after((s0, s2), low1), (0, 2), 0)
    slope1, low1, rows1 = call(
        functools.partial(norm_back, layer=1),
        [after(place, s1), state1, cotangent, cotangent, keep1, got1, far1, vec],
        [SM] + [VM] * 7,
        [shape(128, W, dtype=F32), shape(128, W), shape(8, W, dtype=F32)],
    )
    u_blocks = gather_late(low1)
    g1, g3 = hops(after((s1, s3), low1), (1, 3), 0)
    s0, k0, s2, k2 = first_folds(after(place, low1), (k0, k2), (g0, g2), (0, 2))
    one1 = [k0, k2] + hops([s0, s2], (0, 2), 1)

    up0, act0, ss0, send0, keep0, bias0 = call(
        first_back,
        [place] + u_blocks + [before0, qkv0, turn, triple, merger, expander, shrinker]
        + t_pieces + e_pieces,
        [SM] + [VM] * 7 + [HBM] * 4 + [ANY] * 6,
        [full, full, shape(512, WIDE), send, keep, shape(8, WIDE, dtype=F32)],
        scratch=[
            wide, merge, shrink, pltpu.VMEM((512, 768), F32), pltpu.VMEM((512, 256), BF),
            pltpu.SemaphoreType.DMA((12,)),
        ],
        room=9,
        flops=5 * 10**9,
    )
    got0 = move(send0, flip_core=1)
    s0, k0, s2, k2 = weight_one(place, act0, up0, normed0, ss0)
    f1, h1, f3, h3 = first_folds(after(place, s0), (k1, k3), (g1, g3), (1, 3))
    g0, g2 = hops((s0, s2), (0, 2), 0)
    s1, k1, s3, k3 = weight_two(after(place, f1), act0, up0, normed0, ss0, mixed0)
    two1 = [h1, h3] + hops([f1, f3], (1, 3), 1)
    g1, g3 = hops((s1, s3), (1, 3), 0)
    far0 = other(keep0, got0)
    s0, k0, s2, k2 = first_folds(place, (k0, k2), (g0, g2), (0, 2))
    one0 = [k0, k2] + hops([s0, s2], (0, 2), 1)
    units1 = fold_middle(after(place, s0), one1, two1)
    s1, k1, s3, k3 = first_folds(place, (k1, k3), (g1, g3), (1, 3))
    two0 = [k1, k3] + hops([s1, s3], (1, 3), 1)
    units1 = fold_last(after(place, s1), units1)
    input_grad, _, rows0 = call(
        functools.partial(norm_back, layer=0),
        [place, inputs, slope1, low1, keep0, got0, far0, vec],
        [SM] + [VM] * 7,
        [shape(128, W, dtype=F32), shape(128, W), shape(8, W, dtype=F32)],
    )
    (vector,) = call(
        vectors_out, [place, rows0, bias0, rows1, bias1], [SM] + [VM] * 4,
        [shape(32, 512, dtype=F32)], scratch=[pltpu.VMEM((16, W), F32)],
    )
    units0 = fold_middle(after(place, vector), one0, two0)
    terms1 = send_z(after(place, units0[0]), units1, [])
    units0 = fold_last(place, units0)
    pieces1 = sum_z(after(place, units0[0]), terms1)
    every1 = collect_last(after(place, units0[0]), pieces1)
    terms0 = send_z(place, units0, [vector])
    pieces0 = sum_z(place, terms0)
    line0 = line_unit(place, pieces0)
    b_got = move(after(b_send, pieces1[0]), flip_core=1)
    b_low = (
        b_keep.reshape(2, 256, W)[:, 128:] + b_got.reshape(2, 256, W)[:, 128:].astype(F32)
    ).astype(BF)
    b_far = move(b_low.reshape(256, W), flip_z=1)
    hidden_out, squares1 = call(
        functools.partial(join, layer=1),
        [place, state1, b_keep, b_got, b_far, vec],
        [SM] + [VM] * 5,
        [shape(128, W), shape(8, 128, dtype=F32)],
    )

    line0 = line_four(after(place, hidden_out), line0)
    totals = jnp.concatenate([squares0[:3, :1], squares1[:3, :1]]).reshape(1, 6)
    totals = totals + move(totals, flip_core=1)
    totals = totals + move(totals, flip_z=1)
    rms_stats = jnp.sqrt(totals / (length.astype(F32) * W) + 1e-06)
    line0 = line_three(after(place, rms_stats), line0)
    own0, got0 = line_two(place, line0)
    sums1 = put_last(after(every1, own0[0]))
    sums0 = put_sums(place, own0, sums1, [])
    *sums0, g_sum, s_sum, b_sum, b_copy, t_sum, e_sum = put_sums(place, got0, sums0, [own0[0]])
    return (
        hidden_out,
        input_grad,
        g_sum,
        s_sum,
        sums0[0],
        t_sum,
        sums0[1],
        b_sum,
        sums0[2],
        e_sum,
        sums0[3],
        b_copy,
        rms_stats,
    )


def solution(mesh):
    return jax.shard_map(
        body,
        mesh=mesh,
        in_specs=(
            P(("rep", "shard"), None),
            P("rep"),
            P(None, "shard"),
            P(None, "shard"),
            P(None, "shard", None),
            P(None, "shard"),
            P(None, "shard", None),
            P(None, "shard"),
            P(None, "shard", None),
            P(None, "shard"),
            P(None, "shard", None),
            P(None, "shard"),
            P(("rep", "shard"), None),
        ),
        out_specs=(
            P(("rep", "shard"), None),
            P(("rep", "shard"), None),
            P(None, "shard"),
            P(None, "shard"),
            P(None, "shard", None),
            P(None, "shard"),
            P(None, "shard", None),
            P(None, "shard"),
            P(None, "shard", None),
            P(None, "shard"),
            P(None, "shard", None),
            P(None, "shard"),
            P("rep", None),
        ),
        check_vma=False,
    )
```

```python
import functools
import math

import jax
import jax.numpy as jnp
from jax import lax
from jax.experimental import pallas as pl
from jax.experimental.pallas import tpu as pltpu
from jax.sharding import PartitionSpec as P

HD = 64
ROT = 32
LAYERS = 2
EPS_NORM = 1e-05
AXES = ("rep", "shard")
BF = jnp.bfloat16
F32 = jnp.float32
MINE = 4
W = 1024
WIDE = 1792
PART = 768
PAIR = 1536
ORDERS = ((0, 2, 1, 3), (2, 0, 1, 3), (1, 3, 2, 0), (3, 1, 2, 0))

VM = pl.BlockSpec(memory_space=pltpu.VMEM)
ANY = pl.BlockSpec(memory_space=pl.ANY)
HBM = pl.BlockSpec(memory_space=pltpu.HBM)
SM = pl.BlockSpec(memory_space=pltpu.SMEM)


def place_of(index):
    rep, shard = divmod(index, 4)
    x, rest = divmod(rep, 8)
    z_hi, y = divmod(rest, 4)
    z_lo, core = divmod(shard, 2)
    return x, y, z_hi * 2 + z_lo, core


def index_of(x, y, z, core):
    return ((x * 2 + z // 2) * 4 + y) * 4 + (z % 2) * 2 + core


def move(value, flip_x=0, flip_y=0, flip_z=0, flip_core=0):
    pairs = []
    for index in range(128):
        x, y, z, core = place_of(index)
        pairs.append((index, index_of(x ^ flip_x, y ^ flip_y, z ^ flip_z, core ^ flip_core)))
    return lax.ppermute(value, AXES, pairs)


def hop(value, link):
    by = 3 if link & 1 else 1
    return move(value, flip_y=by) if link > 1 else move(value, flip_x=by)


def link_bit(place, link):
    return place[4 + link]


def after(value, *others):
    return lax.optimization_barrier((value,) + others)[0]


def pick(value, index, axis=0):
    return lax.dynamic_index_in_dim(value, index, axis, keepdims=False)


def shape(*dims, dtype=BF):
    return jax.ShapeDtypeStruct(dims, dtype)


def call(body, args, specs, outs, out_specs=None, scratch=(), flops=0, aliases=None, room=3):
    held = sum(math.prod(o.shape) * o.dtype.itemsize for o in outs)
    held += sum(math.prod(a.shape) * a.dtype.itemsize for a, s in zip(args, specs) if s is VM)
    held += sum(math.prod(s.shape) * s.dtype.itemsize for s in scratch if jnp.issubdtype(s.dtype, jnp.floating))
    room = held + (room << 20)
    return pl.pallas_call(
        body,
        out_shape=outs,
        in_specs=specs,
        out_specs=out_specs or [VM] * len(outs),
        scratch_shapes=scratch,
        input_output_aliases=aliases or {},
        compiler_params=pltpu.CompilerParams(vmem_limit_bytes=room),
        cost_estimate=pl.CostEstimate(flops=1, bytes_accessed=1, transcendentals=0),
    )(*args)


def dot(left, right):
    return jnp.dot(left, right, preferred_element_type=F32)


def dot_t(left, right):
    return lax.dot_general(left, right, (((1,), (1,)), ((), ())), preferred_element_type=F32)


def t_dot(left, right):
    return lax.dot_general(left, right, (((0,), (0,)), ((), ())), preferred_element_type=F32)


def copies(pairs, sems):
    started = []
    for at, (source, target) in enumerate(pairs):
        copy = pltpu.make_async_copy(source, target, sems.at[at])
        copy.start()
        started.append(copy)
    return started


def finish(started):
    for copy in started:
        copy.wait()


def lanes(start, size):
    return pl.ds(pl.multiple_of(start, 128), size)


def rows_at(start, size):
    return pl.ds(pl.multiple_of(start, 16), size)


def cut_triple(
    place, gains, shifts, merger_bias, shrinker_bias, triple_bias, triple,
    small, out1, out2, out3, slab, sems,
):
    shard = place[2]
    started = copies([(triple.at[0], slab)], sems)
    narrow = [v[...].astype(F32) for v in (gains, shifts, merger_bias, shrinker_bias)]
    narrow = jnp.concatenate(narrow + [jnp.zeros((8, 256), F32)], axis=0)
    tall = jnp.concatenate(
        [jnp.zeros((8, 768), F32), triple_bias[...].astype(F32), jnp.zeros((6, 768), F32)], axis=0
    )
    both = jnp.concatenate([narrow, jnp.zeros((16, 512), F32)], axis=1) + tall
    small[...] = both.astype(BF)
    for ref in (out1, out2, out3):
        ref[pl.ds(256, 16), :] = both.astype(BF)
    finish(started)
    for k, ref in ((2, out2), (3, out3), (1, out1)):
        for p in range(3):
            ref[pl.ds(0, 256), pl.ds(p * 256, 256)] = slab[:, lanes(p * W + (shard ^ k) * 256, 256)]


def cut_rest(
    place, cotangent, triple, expander, e1, e2, e3, w1, wz, slab, first, second, sems
):
    shard = place[2]
    pairs = [(expander.at[0], first), (expander.at[1], second), (triple.at[1], slab)]
    started = copies(pairs, sems)
    e2[pl.ds(256, 128), :] = cotangent[...]
    started[0].wait()
    for k, ref in ((2, e2), (3, e3), (1, e1)):
        ref[pl.ds(0, 256), :] = first[:, lanes((shard ^ k) * W, W)]
    finish(started[1:])
    for k, ref in ((2, wz.at[pl.ds(0, 256)]), (3, wz.at[pl.ds(256, 256)]), (1, w1)):
        block = shard ^ k
        ref[:, pl.ds(0, W)] = second[:, lanes(block * W, W)]
        for p in range(3):
            ref[:, pl.ds(W + p * 256, 256)] = slab[:, lanes(p * W + block * 256, 256)]


def own_triple(shard, layer, triple, wide):
    return [
        (
            triple.at[layer, :, lanes(p * W + shard * 256, 256)],
            wide.at[rows_at(shard * 256, 256), pl.ds(W + p * 256, 256)],
        )
        for p in range(3)
    ]


def own_expander(shard, layer, expander, wide):
    return [
        (expander.at[layer, :, lanes(shard * W, W)], wide.at[rows_at(shard * 256, 256), pl.ds(0, W)])
    ]


def piece_rows(shard, k, wide):
    return wide.at[rows_at((shard ^ k) * 256, 256)]


def first_triple(shard, pieces, wide):
    return [
        (ref.at[pl.ds(0, 256)], piece_rows(shard, k, wide).at[:, pl.ds(W, 768)])
        for k, ref in zip((1, 2, 3), pieces)
    ]


def first_expander(shard, pieces, wide):
    return [
        (ref.at[pl.ds(0, 256)], piece_rows(shard, k, wide).at[:, pl.ds(0, W)])
        for k, ref in zip((1, 2, 3), pieces)
    ]


def second_wide(shard, pieces, wide):
    one, two, three = pieces
    return [
        (one, piece_rows(shard, 1, wide)),
        (two.at[pl.ds(0, 256)], piece_rows(shard, 2, wide)),
        (three, piece_rows(shard, 3, wide)),
    ]


def spots(shard):
    row = lax.broadcasted_iota(jnp.int32, (512, 1), 0)
    col = lax.broadcasted_iota(jnp.int32, (1, 512), 1)

    def at(i):
        return (((i >> 7) ^ shard) << 7) | (i & 127)

    return at(row), at(col)


def rotate(values, turn, back=False):
    ahead = pltpu.roll(values, 256 - 16, 1) * turn[1]
    behind = pltpu.roll(values, 16, 1) * turn[2]
    if back:
        return values * turn[0] - ahead - behind
    return values * turn[0] + ahead + behind


def normalize(state):
    mean = jnp.mean(state, axis=-1, keepdims=True)
    centred = state - mean
    spread = jnp.mean(centred * centred, axis=-1, keepdims=True)
    factor = lax.rsqrt(spread + EPS_NORM)
    return centred * factor, factor


ROOT = math.sqrt(2.0 / math.pi)


def gelu_both(v):
    square = v * v
    t = jnp.tanh(ROOT * v * (1.0 + 0.044715 * square))
    half = 0.5 * (1.0 + t)
    slope = half + 0.5 * v * (1.0 - t * t) * (ROOT + (3.0 * 0.044715 * ROOT) * square)
    return v * half, slope


def heads_out(normed, wide, bias, turn, qkv):
    scale = HD ** (-0.5)
    for p in range(3):
        part = dot(normed[...], wide[:, pl.ds(W + p * 256, 256)]) + bias[:, pl.ds(p * 256, 256)]
        if p < 2:
            part = rotate(part, turn)
        if p == 0:
            part = part * scale
        qkv[:, pl.ds(p * 256, 256)] = part.astype(BF)


def probabilities(qkv, h, allowed):
    q = qkv[:, pl.ds(h * HD, HD)]
    k = qkv[:, pl.ds(256 + h * HD, HD)]
    scores = jnp.where(allowed, dot_t(q, k), -1000000000.0)
    powered = jnp.exp(scores - jnp.max(scores, axis=-1, keepdims=True))
    return powered * (1.0 / jnp.sum(powered, axis=-1, keepdims=True))


def attend(qkv, allowed, mixed):
    for h in range(MINE):
        low = probabilities(qkv, h, allowed).astype(BF)
        mixed[:, pl.ds(h * HD, HD)] = dot(low, qkv[:, pl.ds(512 + h * HD, HD)]).astype(BF)


def attend_back(qkv, allowed, mixed, slope_mixed, slopes, forward):
    for h in range(MINE):
        probs = probabilities(qkv, h, allowed)
        low = probs.astype(BF)
        q = qkv[:, pl.ds(h * HD, HD)]
        k = qkv[:, pl.ds(256 + h * HD, HD)]
        v = qkv[:, pl.ds(512 + h * HD, HD)]
        if forward:
            mixed[:, pl.ds(h * HD, HD)] = dot(low, v).astype(BF)
        out = slope_mixed[:, pl.ds(h * HD, HD)]
        slope_probs = dot_t(out, v)
        centre = jnp.sum(probs * slope_probs, axis=-1, keepdims=True)
        slope_scores = (probs * (slope_probs - centre)).astype(BF)
        slopes[:, pl.ds(h * HD, HD)] = dot(slope_scores, k)
        slopes[:, pl.ds(256 + h * HD, HD)] = t_dot(slope_scores, q)
        slopes[:, pl.ds(512 + h * HD, HD)] = t_dot(low, out)


def hand_out(left, right, send, keep):
    for n in range(2):
        cols = pl.ds(n * 512, 512)
        part = dot(left[...], right[:, cols])
        spread_out(part, cols, send, keep)


def spread_out(part, cols, send, keep):
    keep[pl.ds(0, 128), cols] = part[0:128]
    send[pl.ds(0, 128), cols] = part[128:256].astype(BF)
    keep[pl.ds(128, 128), cols] = part[256:384]
    send[pl.ds(128, 128), cols] = part[384:512].astype(BF)


def first_attention(
    place, x0, x1, x2, x3, small, bias, turn, triple, merger, t1, t2, t3,
    normed, qkv, mixed, send, keep, vec, wide, merge, smalls, sems,
):
    shard, length = place[2], place[3]
    pairs = [(small, smalls.at[shard])]
    pairs += [(t1.at[pl.ds(256, 16)], smalls.at[shard ^ 1])]
    pairs += [(t2.at[pl.ds(256, 16)], smalls.at[shard ^ 2])]
    pairs += [(t3.at[pl.ds(256, 16)], smalls.at[shard ^ 3])]
    pairs += own_triple(shard, 0, triple, wide) + [(merger.at[0], merge)]
    started = copies(pairs + first_triple(shard, (t1, t2, t3), wide), sems)
    for copy in started[:4]:
        copy.wait()
    vec[...] = jnp.zeros_like(vec)
    for j in range(4):
        vec[pl.ds(0, 8), pl.ds(j * 256, 256)] = smalls[j].astype(F32)[0:8, 0:256]
    for p in range(3):
        block = p * 4 + shard
        j = (block * 11) >> 5
        vec[pl.ds(8, 2), pl.ds(p * 256, 256)] = smalls[j, :, lanes((block - 3 * j) * 256, 256)].astype(
            F32
        )[8:10]
    vec[pl.ds(10, 2), :] = bias[...].astype(F32)
    gain, shift = vec[pl.ds(0, 1), :], vec[pl.ds(2, 1), :]
    for k, ref in enumerate((x0, x1, x2, x3)):
        hat, _ = normalize(ref[...].astype(F32))
        normed[pl.ds(k * 128, 128), :] = (hat * gain + shift).astype(BF)
    finish(started[4:])
    row, col = spots(shard)
    allowed = (col <= row) & (col < length)
    heads_out(normed, wide, vec[pl.ds(8, 1), pl.ds(0, 768)], turn, qkv)
    attend(qkv, allowed, mixed)
    hand_out(mixed, merge, send, keep)


def first_forward(
    place, normed, vec, expander, shrinker, e1, e2, e3,
    before, send, keep, wide, shrink, act, sems,
):
    shard = place[2]
    pairs = own_expander(shard, 0, expander, wide) + first_expander(shard, (e1, e2, e3), wide)
    started = copies(pairs + [(shrinker.at[0], shrink)], sems)
    finish(started)
    for n in range(2):
        cols = pl.ds(n * 512, 512)
        part = dot(normed[...], wide[:, cols]) + vec[pl.ds(10, 1), cols]
        before[:, cols] = part
        act[:, cols] = gelu_both(part)[0].astype(BF)
    hand_out(act, shrink, send, keep)


def slopes_out(ss, bias, wide, send, keep):
    bias[...] = jnp.broadcast_to(jnp.sum(ss[...].astype(F32), axis=0, keepdims=True), bias.shape)
    for n in range(2):
        part = dot_t(ss[...], wide[pl.ds(n * 512, 512), :])
        spread_out(part, pl.ds(n * 512, 512), send, keep)


def triple_slopes(slopes, turn, ss):
    scale = HD ** (-0.5)
    ss[:, pl.ds(W, 256)] = (rotate(slopes[:, pl.ds(0, 256)], turn, True) * scale).astype(BF)
    ss[:, pl.ds(W + 256, 256)] = rotate(slopes[:, pl.ds(256, 256)], turn, True).astype(BF)
    ss[:, pl.ds(W + 512, 256)] = slopes[:, pl.ds(512, 256)].astype(BF)


def last_layer(
    place, n0, n1, n2, n3, u0, u1, u2, u3, vec, turn, triple, merger, expander, shrinker, w1, w2, w3,
    normed, up, act, ss, mixed, send, keep, bias,
    wide, merge, shrink, qkv, slopes, out, sems,
):
    shard, length = place[2], place[3]
    pairs = own_triple(shard, 1, triple, wide) + own_expander(shard, 1, expander, wide)
    pairs += second_wide(shard, (w1, w2, w3), wide) + [(merger.at[1], merge), (shrinker.at[1], shrink)]
    started = copies(pairs, sems)
    row, col = spots(shard)
    for k, (n, u) in enumerate(((n0, u0), (n1, u1), (n2, u2), (n3, u3))):
        rows = pl.ds(k * 128, 128)
        normed[rows, :] = n[...]
        up[rows, :] = jnp.where(row[k * 128 : k * 128 + 128] < length, u[...].astype(F32), 0.0).astype(BF)
    finish(started)
    for n in range(2):
        cols = pl.ds(n * 512, 512)
        part = dot(normed[...], wide[:, cols]) + vec[pl.ds(11, 1), cols]
        value, slope = gelu_both(part)
        act[:, cols] = value.astype(BF)
        ss[:, cols] = (dot_t(up[...], shrink[cols, :]) * slope).astype(BF)
    allowed = (col <= row) & (col < length)
    heads_out(normed, wide, vec[pl.ds(9, 1), pl.ds(0, 768)], turn, qkv)
    out[...] = dot_t(up[...], merge[...]).astype(BF)
    attend_back(qkv, allowed, mixed, out, slopes, True)
    triple_slopes(slopes, turn, ss)
    slopes_out(ss, bias, wide, send, keep)


def last_branches(act, mixed, merger, shrinker, send, keep, merge, shrink, sems):
    finish(copies([(merger.at[1], merge), (shrinker.at[1], shrink)], sems))
    hand_out(mixed, merge, send.at[pl.ds(0, 256)], keep.at[pl.ds(0, 256)])
    hand_out(act, shrink, send.at[pl.ds(256, 256)], keep.at[pl.ds(256, 256)])


def first_back(
    place, u0, u1, u2, u3, before, qkv, turn, triple, merger, expander, shrinker,
    t1, t2, t3, e1, e2, e3,
    up, act, ss, send, keep, bias, wide, merge, shrink, slopes, out, sems,
):
    shard, length = place[2], place[3]
    pairs = own_triple(shard, 0, triple, wide) + own_expander(shard, 0, expander, wide)
    pairs += first_triple(shard, (t1, t2, t3), wide)
    pairs += first_expander(shard, (e1, e2, e3), wide)
    started = copies(pairs + [(merger.at[0], merge), (shrinker.at[0], shrink)], sems)
    for k, u in enumerate((u0, u1, u2, u3)):
        up[pl.ds(k * 128, 128), :] = u[...]
    finish(started)
    for n in range(2):
        cols = pl.ds(n * 512, 512)
        value, slope = gelu_both(before[:, cols])
        act[:, cols] = value.astype(BF)
        ss[:, cols] = (dot_t(up[...], shrink[cols, :]) * slope).astype(BF)
    row, col = spots(shard)
    allowed = (col <= row) & (col < length)
    out[...] = dot_t(up[...], merge[...]).astype(BF)
    attend_back(qkv, allowed, None, out, slopes, False)
    triple_slopes(slopes, turn, ss)
    slopes_out(ss, bias, wide, send, keep)


def halve(term, cols, o, bit, send, keep, at):
    for ref, half in ((keep, bit), (send, 1 - bit)):
        value = term[pl.ds(pl.multiple_of(half * 128, 128), 128), cols].astype(BF)
        for k in range(8):
            ref[pl.ds(k * 64 + o * 16, 16), at] = value[k * 16 : k * 16 + 16]


def terms_one(place, act, up, normed, ss, s0, k0, s2, k2, term):
    whole = pl.ds(0, PART)
    for o in range(4):
        cols = pl.ds(o * 256, 256)
        term[...] = t_dot(act[:, cols], up[:, pl.ds(0, PART)])
        halve(term, whole, o, link_bit(place, ORDERS[0][0]), s0, k0, whole)
        term[...] = t_dot(normed[:, cols], ss[:, pl.ds(0, PART)])
        halve(term, whole, o, link_bit(place, ORDERS[2][0]), s2, k2, whole)


def terms_two(place, act, up, normed, ss, mixed, s1, k1, s3, k3, term, last):
    one, three = link_bit(place, ORDERS[1][0]), link_bit(place, ORDERS[3][0])
    whole = pl.ds(0, PART)
    last[...] = t_dot(mixed[...], up[...])
    for o in range(4):
        cols = pl.ds(o * 256, 256)
        term[:, pl.ds(0, 256)] = t_dot(act[:, cols], up[:, pl.ds(PART, 256)])
        term[:, pl.ds(256, 256)] = last[:, cols]
        both = t_dot(normed[:, cols], ss[:, pl.ds(PART, W)])
        term[:, pl.ds(512, 256)] = both[:, 256:512]
        halve(term, whole, o, one, s1, k1, whole)
        term[:, pl.ds(0, 256)] = both[:, 0:256]
        term[:, pl.ds(256, 512)] = both[:, 512:W]
        halve(term, whole, o, three, s3, k3, whole)


def weight_one(place, act, up, normed, ss):
    return call(
        terms_one, [place, act, up, normed, ss], [SM] + [VM] * 4, [shape(512, PART)] * 4,
        scratch=[pltpu.VMEM((256, PART), F32)], flops=2 * 10**9,
    )


def weight_two(place, act, up, normed, ss, mixed):
    return call(
        terms_two, [place, act, up, normed, ss, mixed], [SM] + [VM] * 5, [shape(512, PART)] * 4,
        scratch=[pltpu.VMEM((256, PART), F32), pltpu.VMEM((256, W), F32)], flops=2 * 10**9,
    )


def join(place, state, *refs, layer):
    shard, length = place[2], place[3]
    spot = shard * 128 + lax.broadcasted_iota(jnp.int32, (128, 1), 0)
    valid = (spot < length).astype(F32)
    if layer == 0:
        ak, ag, az, fk, fg, fz, vec, new, out, squares = refs
        attended = ak[pl.ds(0, 128), :] + ag[pl.ds(0, 128), :].astype(F32) + az[...].astype(F32)
        branch = fk[pl.ds(0, 128), :] + fg[pl.ds(0, 128), :].astype(F32) + fz[...].astype(F32)
    else:
        kept, got, far, vec, out, squares = refs
        attended, branch = [
            kept[pl.ds(at * 256, 128), :]
            + got[pl.ds(at * 256, 128), :].astype(F32)
            + far[pl.ds(at * 128, 128), :].astype(F32)
            for at in (0, 1)
        ]
    attended = attended + vec[pl.ds(4 + layer, 1), :]
    branch = branch + vec[pl.ds(6 + layer, 1), :]
    old = state[...].astype(F32)
    for at, item in enumerate((old, attended, branch)):
        total = jnp.sum(jnp.sum(item * item, axis=1, keepdims=True) * valid)
        squares[pl.ds(at, 1), :] = jnp.full((1, 128), total, F32)
    state_new = old + attended + branch
    if layer == 0:
        new[...] = state_new
        hat, _ = normalize(state_new)
        out[...] = (hat * vec[pl.ds(1, 1), :] + vec[pl.ds(3, 1), :]).astype(BF)
    else:
        out[...] = (state_new * valid).astype(BF)


def norm_back(place, state, slope, up, sk, sg, sz, vec, new, low, rows, *, layer):
    shard, length = place[2], place[3]
    spot = shard * 128 + lax.broadcasted_iota(jnp.int32, (128, 1), 0)
    given = slope[...].astype(F32)
    upstream = up[...].astype(F32)
    if layer == LAYERS - 1:
        given = jnp.where(spot < length, given, 0.0)
        upstream = given
    sn = sk[pl.ds(0, 128), :] + sg[pl.ds(0, 128), :].astype(F32) + sz[...].astype(F32)
    hat, factor = normalize(state[...].astype(F32))
    rows[...] = jnp.zeros_like(rows)
    rows[pl.ds(0, 1), :] = jnp.sum(sn * hat, axis=0, keepdims=True)
    rows[pl.ds(1, 1), :] = jnp.sum(sn, axis=0, keepdims=True)
    rows[pl.ds(2, 1), :] = jnp.sum(upstream, axis=0, keepdims=True)
    d = sn * vec[pl.ds(layer, 1), :]
    mean = jnp.mean(d, axis=-1, keepdims=True)
    along = jnp.mean(d * hat, axis=-1, keepdims=True)
    result = given + factor * (d - mean - hat * along)
    new[...] = result
    low[...] = result.astype(BF)


def vectors_out(place, rows0, bias0, rows1, bias1, out, full):
    shard = place[2]
    full[...] = jnp.zeros_like(full)
    for at, (rows, bias) in enumerate(((rows0, bias0), (rows1, bias1))):
        base = at * 7
        full[pl.ds(base, 3), :] = rows[pl.ds(0, 3), :]
        for p in range(3):
            full[pl.ds(base + 3 + p, 1), lanes(shard * 256, 256)] = bias[
                pl.ds(0, 1), pl.ds(W + p * 256, 256)
            ]
        full[pl.ds(base + 6, 1), :] = bias[pl.ds(0, 1), pl.ds(0, W)]
    out[pl.ds(0, 16), :] = full[:, pl.ds(0, 512)]
    out[pl.ds(16, 16), :] = full[:, pl.ds(512, 512)]


def add_half(kept, got, bit, refs, at):
    size = kept.shape[0] // 2
    for ref, half in zip(refs, (1 - bit, bit)):
        rows = rows_at(half * size, size)
        total = kept[rows, :].astype(F32) + got[rows, :].astype(F32)
        ref[:, at] = total.astype(BF)


def fold_one(place, ka, ga, kb, gb, sa, ha, sb, hb, *, parts):
    for part, (k, g, s, h) in zip(parts, ((ka, ga, sa, ha), (kb, gb, sb, hb))):
        add_half(k, g, link_bit(place, ORDERS[part][1]), (s, h), slice(None))


def fold_two(place, k0, g0, k1, g1, k2, g2, k3, g3, sa, ha, sb, hb):
    for part, (k, g) in enumerate(((k0, g0), (k1, g1), (k2, g2), (k3, g3))):
        refs = (sb, hb) if part > 1 else (sa, ha)
        at = pl.ds((part & 1) * PART, PART)
        add_half(k, g, link_bit(place, ORDERS[part][2]), refs, at)


def fold_three(place, ka, ga, kb, gb, sa, ha, sb, hb):
    for part, (k, g, s, h) in zip((0, 2), ((ka, ga, sa, ha), (kb, gb, sb, hb))):
        add_half(k, g, link_bit(place, ORDERS[part][3]), (s, h), slice(None))


def first_folds(place, kept, got, parts):
    args = [kept[0], got[0], kept[1], got[1]]
    return call(
        functools.partial(fold_one, parts=parts), [place] + args, [SM] + [VM] * 4, [shape(256, PART)] * 4
    )


def z_send(place, *refs):
    ka, ga, kb, gb, *refs = refs
    shard = place[2]
    z_lo = shard >> 1
    if len(refs) == 6:
        vector, *refs = refs
    else:
        vector = None
    side, across, cross, plain, wide = refs
    a = ka[...].astype(F32) + ga[...].astype(F32)
    b = kb[...].astype(F32) + gb[...].astype(F32)
    wide[:, pl.ds(0, W)] = b[:, 0:W]
    wide[:, pl.ds(W, 256)] = a[:, 1280:PAIR]
    wide[:, pl.ds(1280, 512)] = b[:, W:PAIR]
    plain[...] = a[:, 0:1280]
    cross[...] = wide[rows_at(z_lo * 32, 32), :]
    side[:, pl.ds(0, WIDE)] = wide[rows_at((1 - z_lo) * 32, 32), :].astype(BF)
    across[:, pl.ds(0, WIDE)] = cross[...].astype(BF)
    across[:, pl.ds(WIDE, 1280)] = plain[pl.ds(0, 32), :].astype(BF)
    across[:, pl.ds(WIDE + 1280, 1280)] = plain[pl.ds(32, 32), :].astype(BF)
    if vector is not None:
        side[:, pl.ds(WIDE, 512)] = vector[...].astype(BF)
        across[:, pl.ds(WIDE + 2560, 512)] = vector[...].astype(BF)


def local_rows():
    row = lax.broadcasted_iota(jnp.int32, (32, 1), 0) & 15
    return (row == 6) | (row == 13)


def z_sum(place, *refs):
    cross, plain, za, zb, z2, *refs = refs
    vector = None
    if len(refs) == 6:
        vector, *refs = refs
        near, kept, whole, vec, both = refs
    else:
        near, kept, whole, both = refs
    core = place[2] & 1
    both[pl.ds(0, 32), :] = cross[...] + z2[:, pl.ds(0, WIDE)].astype(F32)
    both[pl.ds(32, 32), :] = za[:, pl.ds(0, WIDE)].astype(F32) + zb[:, pl.ds(0, WIDE)].astype(F32)
    for at in range(2):
        own = both[rows_at(at * 32 + core * 16, 16), :]
        other = both[rows_at(at * 32 + (1 - core) * 16, 16), :]
        kept[pl.ds(at * 16, 16), :] = own.astype(BF)
        near[pl.ds(at * 16, 16), pl.ds(0, WIDE)] = other.astype(BF)
    for at in range(2):
        rows = pl.ds(at * 32, 32)
        got = z2[:, pl.ds(WIDE + at * 1280, 1280)].astype(F32)
        whole[rows, :] = (plain[rows, :] + got).astype(BF)
    if vector is not None:
        sides = za[:, pl.ds(WIDE, 512)].astype(F32) + zb[:, pl.ds(WIDE, 512)].astype(F32)
        total = vector[...] + z2[:, pl.ds(WIDE + 2560, 512)].astype(F32)
        total = total + jnp.where(local_rows(), 0.0, sides)
        vec[...] = total
        near[:, pl.ds(WIDE, 512)] = total.astype(BF)


def payload_parts(place, kept, near, whole, a, b):
    shard = place[2]
    for k in range(4):
        rows = rows_at((shard ^ k) * 16, 16)
        ref, at = (near, k >> 1) if k & 1 else (kept, k >> 1)
        source = ref[pl.ds(at * 16, 16), pl.ds(0, WIDE)]
        b[rows, pl.ds(0, W)] = source[:, 0:W]
        a[rows, pl.ds(1280, 256)] = source[:, W:1280]
        b[rows, pl.ds(W, 512)] = source[:, 1280:WIDE]
    a[pl.ds(0, 64), pl.ds(0, 1280)] = whole[...]


def payload_both(place, kept, near, whole, out):
    payload_parts(place, kept, near, whole, out.at[pl.ds(0, 64)], out.at[pl.ds(64, 64)])


def payload(place, kept, near, whole, *refs):
    *vec, a, b = refs
    payload_parts(place, kept, near, whole, a, b)
    if not vec:
        return
    vec = vec[0]
    total = vec[...] + jnp.where(local_rows(), 0.0, near[:, pl.ds(WIDE, 512)].astype(F32))
    low = total.astype(BF)
    a[pl.ds(64, 16), :] = jnp.zeros((16, PAIR), BF)
    a[pl.ds(64, 16), pl.ds(0, 512)] = low[0:16]
    a[pl.ds(64, 16), pl.ds(512, 512)] = low[16:32]


def line_up(own, got, bit, size, outs, cols):
    for ref, at in zip(outs, cols):
        ref[rows_at(bit * size, size), :] = own[pl.ds(0, size), at]
        ref[rows_at((1 - bit) * size, size), :] = got[pl.ds(0, size), at]


def vector_rows(own, got, at, size):
    rows = pl.ds(at, size)
    return (own[rows, :].astype(F32) + got[rows, :].astype(F32)).astype(BF)


def gather_four(place, oa, ga, ob, gb, a, b):
    line_up(oa, ga, link_bit(place, ORDERS[0][3]), 64, [a], [slice(None)])
    line_up(ob, gb, link_bit(place, ORDERS[2][3]), 64, [b], [slice(None)])
    if a.shape[0] > 128:
        a[pl.ds(128, 16), :] = vector_rows(oa, ga, 64, 16)


def gather_three(place, oa, ga, ob, gb, p0, p1, p2, p3):
    cols = [pl.ds(0, PART), pl.ds(PART, PART)]
    line_up(oa, ga, link_bit(place, ORDERS[0][2]), 128, [p0, p1], cols)
    line_up(ob, gb, link_bit(place, ORDERS[2][2]), 128, [p2, p3], cols)
    if p0.shape[0] == 256:
        return
    low = vector_rows(oa, ga, 128, 16)
    p0[pl.ds(256, 32), :] = jnp.zeros((32, PART), BF)
    p0[pl.ds(256, 16), pl.ds(0, 512)] = low[:, 0:512]
    p0[pl.ds(272, 16), pl.ds(0, 512)] = low[:, 512:W]


def gather_two(place, o0, g0, o1, g1, o2, g2, o3, g3, p0, p1, p2, p3):
    outs = (p0, p1, p2, p3)
    for part, (o, g) in enumerate(((o0, g0), (o1, g1), (o2, g2), (o3, g3))):
        line_up(o, g, link_bit(place, ORDERS[part][1]), 256, [outs[part]], [slice(None)])
    p0[pl.ds(512, 32), :] = vector_rows(o0, g0, 256, 32)


def each(count, step):
    lax.fori_loop(0, count, lambda at, none: step(at) or none, 0)


def put(part, value, o, base, t, m, e, s):
    rows = rows_at(base, 16)
    if part == 0:
        s[rows_at(o * 256 + base, 16), pl.ds(0, PART)] = value
    elif part == 1:
        s[rows_at(o * 256 + base, 16), pl.ds(PART, 256)] = value[:, 0:256]
        m[rows, pl.ds(o * 256, 256)] = value[:, 256:512]
        t[rows, pl.ds(o * 256, 256)] = value[:, 512:PART]
    elif part == 2:
        e[rows, pl.ds(o * W, PART)] = value
    else:
        e[rows, pl.ds(o * W + PART, 256)] = value[:, 0:256]
        t[rows, pl.ds(W + o * 256, 256)] = value[:, 256:512]
        t[rows, pl.ds(2 * W + o * 256, 256)] = value[:, 512:PART]


def assemble_last(every, t_out, m_out, e_out, s_out, t, m, e, s, sems):
    def device(at):
        x, y = at >> 2, at & 3
        bits = ((x & 1) ^ (x >> 1), x >> 1, (y & 1) ^ (y >> 1), y >> 1)
        for part in range(4):
            unit = sum(bits[link] << (3 - n) for n, link in enumerate(ORDERS[part]))
            for o in range(4):
                rows = rows_at(at * 128 + (part >> 1) * 64 + o * 16, 16)
                value = every[rows, pl.ds((part & 1) * PART, PART)].astype(F32)
                put(part, value, o, unit * 16, t, m, e, s)

    each(16, device)
    pairs = [(t, t_out.at[1]), (m, m_out.at[1]), (e, e_out.at[1]), (s, s_out.at[1])]
    finish(copies(pairs, sems))


def put_half(place, p0, p1, p2, p3, *refs, mine):
    if not mine:
        old, *refs = refs
        t_out, m_out, e_out, s_out, *sums, s0, s1, m1, t1, e2, e3, t3, both, vec, sems = refs[4:]
    else:
        t_out, m_out, e_out, s_out, s0, s1, m1, t1, e2, e3, t3, sems = refs[4:]
    pairs = []
    for part, ref in enumerate((p0, p1, p2, p3)):
        half = link_bit(place, ORDERS[part][0])
        base = (half if mine else 1 - half) * 128
        rows = rows_at(base, 128)
        for o in range(4):
            for k in range(8):
                value = ref[pl.ds(k * 64 + o * 16, 16), :].astype(F32)
                at = pl.ds(k * 16, 16)
                if part == 0:
                    s0[o, at, :] = value
                elif part == 1:
                    s1[o, at, :] = value[:, 0:256]
                    m1[at, pl.ds(o * 256, 256)] = value[:, 256:512]
                    t1[at, pl.ds(o * 256, 256)] = value[:, 512:PART]
                elif part == 2:
                    e2[o, at, :] = value
                else:
                    e3[o, at, :] = value[:, 0:256]
                    t3[at, pl.ds(o * 256, 256)] = value[:, 256:512]
                    t3[at, pl.ds(W + o * 256, 256)] = value[:, 512:PART]
            if part < 2:
                target = s_out.at[0, rows_at(o * 256 + base, 128)]
                pairs.append((s0.at[o], target.at[:, pl.ds(0, PART)]) if part == 0 else (s1.at[o], target.at[:, pl.ds(PART, 256)]))
            else:
                target = e_out.at[0, rows]
                pairs.append((e2.at[o], target.at[:, pl.ds(o * W, PART)]) if part == 2 else (e3.at[o], target.at[:, pl.ds(o * W + PART, 256)]))
        if part == 1:
            pairs.append((m1, m_out.at[0, rows]))
            pairs.append((t1, t_out.at[0, rows, pl.ds(0, W)]))
        if part == 3:
            pairs.append((t3, t_out.at[0, rows, pl.ds(W, 2 * W)]))
    started = copies(pairs, sems)
    if not mine:
        fetch = copies([(old.at[pl.ds(512, 32)], both)], sems.at[pl.ds(len(pairs), 1)])
        finish(fetch)
        low = both[...].astype(F32) + p0[pl.ds(512, 32), :].astype(F32)
        vec[:, pl.ds(0, 512)] = low[0:16, 0:512]
        vec[:, pl.ds(512, 512)] = low[16:32, 0:512]
        for at in range(LAYERS):
            own_sums(vec, at, place[2], *sums)
    finish(started)


def own_sums(vec, layer, shard, g_sum, s_sum, b_sum, b_copy, t_sum, e_sum):
    base = layer * 7
    row = pl.ds(layer, 1)
    for at, ref in ((0, g_sum), (1, s_sum), (2, b_sum), (2, b_copy)):
        ref[row, :] = vec[pl.ds(base + at, 1), lanes(shard * 256, 256)]
    for r in range(3):
        block = shard * 3 + r
        t_sum[row, pl.ds(r * 256, 256)] = vec[
            pl.ds(base + 3 + (block >> 2), 1), lanes((block & 3) * 256, 256)
        ]
    e_sum[row, :] = vec[pl.ds(base + 6, 1), :]


def hops(values, parts, phase):
    return [hop(value, ORDERS[part][phase]) for value, part in zip(values, parts)]


def fold_middle(place, one, two):
    kept = [one[0], two[0], one[1], two[1]]
    got = [one[2], two[2], one[3], two[3]]
    args = [v for pair in zip(kept, got) for v in pair]
    sa, ka, sb, kb = call(fold_two, [place] + args, [SM] + [VM] * 8, [shape(128, PAIR)] * 4)
    ga, gb = hops([sa, sb], (0, 2), 2)
    return [ka, ga, kb, gb]


def fold_last(place, units):
    sa, ka, sb, kb = call(fold_three, [place] + units, [SM] + [VM] * 4, [shape(64, PAIR)] * 4)
    ga, gb = hops([sa, sb], (0, 2), 3)
    return [ka, ga, kb, gb]


def send_z(place, units, vector):
    more = 512 * len(vector)
    side, across, cross, plain = call(
        z_send, [place] + units + vector, [SM] + [VM] * (4 + len(vector)),
        [
            shape(32, WIDE + more), shape(32, WIDE + 2560 + more),
            shape(32, WIDE, dtype=F32), shape(64, 1280, dtype=F32),
        ],
        scratch=[pltpu.VMEM((64, WIDE), F32)],
    )
    z2 = move(across, flip_z=2)
    za = move(side, flip_z=1)
    zb = move(side, flip_z=3)
    return [cross, plain, za, zb, z2] + vector


def sum_z(place, terms):
    vectors = len(terms) - 5
    near, kept, whole, *vec = call(
        z_sum, [place] + terms, [SM] + [VM] * len(terms),
        [shape(32, WIDE + 512 * vectors), shape(32, WIDE), shape(64, 1280)]
        + [shape(32, 512, dtype=F32)] * vectors,
        scratch=[pltpu.VMEM((64, WIDE), F32)],
    )
    return [kept, move(near, flip_core=1), whole] + vec


OUTS = [
    shape(LAYERS, 256, 3072, dtype=F32),
    shape(LAYERS, 256, 1024, dtype=F32),
    shape(LAYERS, 256, 4096, dtype=F32),
    shape(LAYERS, 1024, 1024, dtype=F32),
]


def line_unit(place, pieces):
    rows = 80 if len(pieces) == 4 else 64
    a, b = call(
        payload, [place] + pieces, [SM] + [VM] * len(pieces), [shape(rows, PAIR), shape(64, PAIR)]
    )
    ga, gb = hops([a, b], (0, 2), 3)
    return [a, ga, b, gb]


def line_four(place, args):
    rows = args[0].shape[0] + 64
    a, b = call(gather_four, [place] + args, [SM] + [VM] * 4, [shape(rows, PAIR), shape(128, PAIR)])
    ga, gb = hops([a, b], (0, 2), 2)
    return [a, ga, b, gb]


def line_three(place, args):
    rows = 288 if args[0].shape[0] > 128 else 256
    own = call(
        gather_three, [place] + args, [SM] + [VM] * 4, [shape(rows, PART)] + [shape(256, PART)] * 3
    )
    got = hops(own, range(4), 1)
    return [v for pair in zip(own, got) for v in pair]


def line_two(place, args):
    own = call(
        gather_two, [place] + args, [SM] + [VM] * 8, [shape(544, PART)] + [shape(512, PART)] * 3
    )
    return list(own), hops(own, range(4), 0)


def collect_last(place, pieces):
    (both,) = call(payload_both, [place] + pieces, [SM] + [VM] * 3, [shape(128, PAIR)])
    planes = [[(x * 2 + z) * 4 + y for x in range(4) for y in range(4)] for z in range(2)]
    return lax.all_gather(both, "rep", axis_index_groups=planes, axis=0, tiled=True)


def put_last(every):
    return call(
        assemble_last, [every], [VM], OUTS, out_specs=[ANY] * 4,
        scratch=[pltpu.VMEM(out.shape[1:], F32) for out in OUTS] + [pltpu.SemaphoreType.DMA((4,))],
    )


def put_sums(place, parts, earlier, old):
    outs, specs = list(OUTS), [ANY] * 4
    scratch = [
        pltpu.VMEM((4, 128, PART), F32), pltpu.VMEM((4, 128, 256), F32), pltpu.VMEM((128, W), F32),
        pltpu.VMEM((128, W), F32), pltpu.VMEM((4, 128, PART), F32), pltpu.VMEM((4, 128, 256), F32),
        pltpu.VMEM((128, 2 * W), F32),
    ]
    if old:
        outs += [shape(LAYERS, n, dtype=F32) for n in (256, 256, 256, 256, 768, 1024)]
        specs += [VM] * 6
        scratch += [pltpu.VMEM((32, PART), BF), pltpu.VMEM((16, W), F32)]
    return call(
        functools.partial(put_half, mine=not old), [place] + parts + old + list(earlier),
        [SM] + [VM] * 4 + [ANY] * (4 + len(old)), outs, out_specs=specs,
        scratch=scratch + [pltpu.SemaphoreType.DMA((20,))],
        aliases={5 + len(old) + i: i for i in range(4)},
    )


def gather_tokens(own):
    far = move(own, flip_z=1)
    near = move(own, flip_core=1)
    return [own, near, far, move(far, flip_core=1)]


def gather_late(own):
    far = move(own, flip_z=1)
    return [own, move(after(own, far), flip_core=1), far, move(far, flip_core=1)]


def body(
    inputs,
    lengths,
    gains,
    shifts,
    triple,
    triple_bias,
    merger,
    merger_bias,
    expander,
    expander_bias,
    shrinker,
    shrinker_bias,
    cotangent,
):
    rep = lax.axis_index("rep")
    shard = lax.axis_index("shard")
    length = lengths[0]
    x, y = rep // 8, rep % 4
    place = [x, y, shard, length, (x & 1) ^ (x >> 1), x >> 1, (y & 1) ^ (y >> 1), y >> 1]
    place = jnp.stack(place).astype(jnp.int32)

    small, *pieces = call(
        cut_triple,
        [place, gains, shifts, merger_bias, shrinker_bias, triple_bias, triple],
        [SM] + [VM] * 5 + [HBM],
        [shape(16, 768)] + [shape(272, 768)] * 3,
        scratch=[pltpu.VMEM((256, 3072), BF), pltpu.SemaphoreType.DMA((1,))],
    )

    def recut(one, two, three):
        return [
            move(one, flip_core=1),
            move(two, flip_z=1),
            move(three, flip_z=3, flip_core=1),
        ]

    t_pieces = recut(*pieces)
    x_blocks = gather_tokens(after(inputs, small))
    cut = call(
        cut_rest, [after(place, pieces[0], x_blocks[1]), cotangent, triple, expander],
        [SM, VM, HBM, HBM],
        [shape(256, W), shape(384, W), shape(256, W)]
        + [shape(256, WIDE), shape(512, WIDE)],
        scratch=[
            pltpu.VMEM((256, 3072), BF), pltpu.VMEM((256, 4096), BF), pltpu.VMEM((256, 4096), BF),
            pltpu.SemaphoreType.DMA((3,)),
        ],
    )
    e_pieces = recut(*after(tuple(cut[:2]), x_blocks[2]), after(cut[2], t_pieces[2]))

    spot = after(jnp.arange(512, dtype=jnp.int32), x_blocks[1])
    spot = (((spot >> 7) ^ shard) << 7) | (spot & 127)
    index = jnp.arange(ROT // 2, dtype=F32)
    freq = jnp.exp(index * (-2.0 * math.log(10000.0) / ROT))
    lane = jnp.arange(256, dtype=jnp.int32) % HD
    phase = spot.astype(F32)[:, None] * jnp.tile(freq, 16)[None, :]
    cosine, sine = jnp.cos(phase), jnp.sin(phase)
    turn = jnp.stack(
        [
            jnp.where(lane < ROT, cosine, 1.0),
            jnp.where(lane < ROT // 2, -sine, 0.0),
            jnp.where((lane >= ROT // 2) & (lane < ROT), sine, 0.0),
        ]
    )

    full = shape(512, W)
    send, keep = shape(256, W), shape(256, W, dtype=F32)
    wide = pltpu.VMEM((W, WIDE), BF)
    merge, shrink = pltpu.VMEM((256, W), BF), pltpu.VMEM((W, W), BF)

    normed0, qkv0, mixed0, a_send, a_keep, vec = call(
        first_attention,
        [place] + x_blocks + [small, expander_bias, turn, triple, merger] + t_pieces,
        [SM] + [VM] * 4 + [ANY, VM, VM, HBM, HBM] + [ANY] * 3,
        [full, shape(512, 768), shape(512, 256), send, keep, shape(16, W, dtype=F32)],
        scratch=[wide, merge, pltpu.VMEM((4, 16, 768), BF), pltpu.SemaphoreType.DMA((11,))],
        room=9,
        flops=2 * 10**9,
    )
    a_got = move(after(a_send, e_pieces[1]), flip_core=1)
    w_near, w_far = after(tuple(cut[3:]), e_pieces[2], turn)
    w_far = move(w_far, flip_z=3)
    before0, f_send, f_keep = call(
        first_forward,
        [place, normed0, vec, expander, shrinker] + e_pieces,
        [SM, VM, VM, HBM, HBM] + [ANY] * 3,
        [shape(512, W, dtype=F32), send, keep],
        scratch=[wide, shrink, pltpu.VMEM((512, W), BF), pltpu.SemaphoreType.DMA((5,))],
        room=9,
        flops=2 * 10**9,
    )
    f_got = move(f_send, flip_core=1)

    def other(kept, got):
        return move((kept[128:] + got[128:].astype(F32)).astype(BF), flip_z=1)

    a_far = other(a_keep, a_got)
    sums = [a_keep, a_got, a_far, f_keep, f_got, other(f_keep, f_got)]
    block = [shape(128, W, dtype=F32), shape(128, W), shape(8, 128, dtype=F32)]
    state1, normed1, squares0 = call(
        functools.partial(join, layer=0), [place, inputs] + sums + [vec], [SM] + [VM] * 8, block
    )
    n_blocks = gather_tokens(normed1)
    w_far = after(w_far, n_blocks[2])
    u_far = after(e_pieces[1][256:], f_got)
    up_blocks = [
        cotangent, move(after(cotangent, f_got), flip_core=1), u_far, move(u_far, flip_core=1)
    ]
    w_pieces = [move(w_near, flip_core=1), w_far, move(w_far[256:], flip_core=1)]

    normed1, up1, act1, ss1, mixed1, send1, keep1, bias1 = call(
        last_layer,
        [place] + n_blocks + up_blocks + [vec, turn, triple, merger, expander, shrinker] + w_pieces,
        [SM] + [VM] * 10 + [HBM] * 4 + [ANY] * 3,
        [full, full, full, shape(512, WIDE), shape(512, 256)]
        + [send, keep, shape(8, WIDE, dtype=F32)],
        scratch=[
            wide, merge, shrink, pltpu.VMEM((512, 768), BF), pltpu.VMEM((512, 768), F32),
            pltpu.VMEM((512, 256), BF), pltpu.SemaphoreType.DMA((9,)),
        ],
        room=9,
        flops=8 * 10**9,
    )
    got1 = move(send1, flip_core=1)
    s0, k0, s2, k2 = weight_one(place, act1, up1, normed1, ss1)
    low1 = (keep1[128:] + after(got1, s0)[128:].astype(F32)).astype(BF)
    far1 = move(low1, flip_z=1)
    s1, k1, s3, k3 = weight_two(after(place, low1), act1, up1, normed1, ss1, mixed1)
    g0, g2 = hops(after((s0, s2), low1), (0, 2), 0)
    b_send, b_keep = call(
        last_branches, [after(act1, s1), mixed1, merger, shrinker], [VM] * 2 + [HBM] * 2,
        [full, shape(512, W, dtype=F32)],
        scratch=[merge, shrink, pltpu.SemaphoreType.DMA((2,))], room=9,
    )
    slope1, low1, rows1 = call(
        functools.partial(norm_back, layer=1),
        [after(place, b_keep), state1, cotangent, cotangent, keep1, got1, far1, vec],
        [SM] + [VM] * 7,
        [shape(128, W, dtype=F32), shape(128, W), shape(8, W, dtype=F32)],
    )
    u_blocks = gather_late(low1)
    g1, g3 = hops(after((s1, s3), low1), (1, 3), 0)
    s0, k0, s2, k2 = first_folds(after(place, low1), (k0, k2), (g0, g2), (0, 2))
    one1 = [k0, k2] + hops([s0, s2], (0, 2), 1)

    up0, act0, ss0, send0, keep0, bias0 = call(
        first_back,
        [place] + u_blocks + [before0, qkv0, turn, triple, merger, expander, shrinker]
        + t_pieces + e_pieces,
        [SM] + [VM] * 7 + [HBM] * 4 + [ANY] * 6,
        [full, full, shape(512, WIDE), send, keep, shape(8, WIDE, dtype=F32)],
        scratch=[
            wide, merge, shrink, pltpu.VMEM((512, 768), F32), pltpu.VMEM((512, 256), BF),
            pltpu.SemaphoreType.DMA((12,)),
        ],
        room=9,
        flops=5 * 10**9,
    )
    got0 = move(send0, flip_core=1)
    s0, k0, s2, k2 = weight_one(place, act0, up0, normed0, ss0)
    f1, h1, f3, h3 = first_folds(after(place, s0), (k1, k3), (g1, g3), (1, 3))
    g0, g2 = hops((s0, s2), (0, 2), 0)
    s1, k1, s3, k3 = weight_two(after(place, f1), act0, up0, normed0, ss0, mixed0)
    two1 = [h1, h3] + hops([f1, f3], (1, 3), 1)
    g1, g3 = hops((s1, s3), (1, 3), 0)
    far0 = other(keep0, got0)
    s0, k0, s2, k2 = first_folds(place, (k0, k2), (g0, g2), (0, 2))
    one0 = [k0, k2] + hops([s0, s2], (0, 2), 1)
    units1 = fold_middle(after(place, s0), one1, two1)
    s1, k1, s3, k3 = first_folds(place, (k1, k3), (g1, g3), (1, 3))
    two0 = [k1, k3] + hops([s1, s3], (1, 3), 1)
    units1 = fold_last(after(place, s1), units1)
    input_grad, _, rows0 = call(
        functools.partial(norm_back, layer=0),
        [place, inputs, slope1, low1, keep0, got0, far0, vec],
        [SM] + [VM] * 7,
        [shape(128, W, dtype=F32), shape(128, W), shape(8, W, dtype=F32)],
    )
    (vector,) = call(
        vectors_out, [place, rows0, bias0, rows1, bias1], [SM] + [VM] * 4,
        [shape(32, 512, dtype=F32)], scratch=[pltpu.VMEM((16, W), F32)],
    )
    units0 = fold_middle(after(place, vector), one0, two0)
    terms1 = send_z(after(place, units0[0]), units1, [])
    units0 = fold_last(place, units0)
    pieces1 = sum_z(after(place, units0[0]), terms1)
    every1 = collect_last(after(place, units0[0]), pieces1)
    terms0 = send_z(place, units0, [vector])
    pieces0 = sum_z(place, terms0)
    line0 = line_unit(place, pieces0)
    b_got = move(after(b_send, pieces1[0]), flip_core=1)
    b_low = (
        b_keep.reshape(2, 256, W)[:, 128:] + b_got.reshape(2, 256, W)[:, 128:].astype(F32)
    ).astype(BF)
    b_far = move(b_low.reshape(256, W), flip_z=1)
    hidden_out, squares1 = call(
        functools.partial(join, layer=1),
        [place, state1, b_keep, b_got, b_far, vec],
        [SM] + [VM] * 5,
        [shape(128, W), shape(8, 128, dtype=F32)],
    )

    line0 = line_four(after(place, hidden_out), line0)
    totals = jnp.concatenate([squares0[:3, :1], squares1[:3, :1]]).reshape(1, 6)
    totals = totals + move(totals, flip_core=1)
    totals = totals + move(totals, flip_z=1)
    rms_stats = jnp.sqrt(totals / (length.astype(F32) * W) + 1e-06)
    line0 = line_three(after(place, rms_stats), line0)
    own0, got0 = line_two(place, line0)
    sums1 = put_last(after(every1, own0[0]))
    sums0 = put_sums(place, own0, sums1, [])
    *sums0, g_sum, s_sum, b_sum, b_copy, t_sum, e_sum = put_sums(place, got0, sums0, [own0[0]])
    return (
        hidden_out,
        input_grad,
        g_sum,
        s_sum,
        sums0[0],
        t_sum,
        sums0[1],
        b_sum,
        sums0[2],
        e_sum,
        sums0[3],
        b_copy,
        rms_stats,
    )


def solution(mesh):
    return jax.shard_map(
        body,
        mesh=mesh,
        in_specs=(
            P(("rep", "shard"), None),
            P("rep"),
            P(None, "shard"),
            P(None, "shard"),
            P(None, "shard", None),
            P(None, "shard"),
            P(None, "shard", None),
            P(None, "shard"),
            P(None, "shard", None),
            P(None, "shard"),
            P(None, "shard", None),
            P(None, "shard"),
            P(("rep", "shard"), None),
        ),
        out_specs=(
            P(("rep", "shard"), None),
            P(("rep", "shard"), None),
            P(None, "shard"),
            P(None, "shard"),
            P(None, "shard", None),
            P(None, "shard"),
            P(None, "shard", None),
            P(None, "shard"),
            P(None, "shard", None),
            P(None, "shard"),
            P(None, "shard", None),
            P(None, "shard"),
            P("rep", None),
        ),
        check_vma=False,
    )
```
